32 devices in a mesh: dp: 8 (over z, x), tensor: 4 (over y, core).
Axes of the slice: x: 2, y: 2, z: 4, core: 2. Of those that a mesh axis runs over, the one named last changes fastest.
Arguments:
- latent: bfloat16 [2048, 1152], P('dp'), may hold values from -6 to 6
- noise: bfloat16 [2048, 1152], P('dp'), may hold values from -6 to 6
- text: bfloat16 [16, 256, 1152], P('dp'), may hold values from -6 to 6
- tsteps: int32 [16], P('dp'), may hold values from 0 to 999
- clip_count: int32 [8], P('dp'), may hold values from 1 to 2, as said below
- text_len: int32 [16], P('dp'), may hold values from 32 to 256, as said below
- cotangent: bfloat16 [2048, 1152], P('dp'), may hold values from -6 to 6
- attn_w: float32 [8, 1152, 1152], P(None, 'dp', 'tensor')
- attn_m: float32 [8, 1152, 1152], P(None, 'dp', 'tensor'), may hold values from -0.00036621094 to 0.00036621094
- attn_v: float32 [8, 1152, 1152], P(None, 'dp', 'tensor'), may hold values from 4.344405e-11 to 1.737762e-10
- mlp_w: float32 [2, 1152, 4608], P(None, 'dp', 'tensor'), may hold values from -0.1875 to 0.1875
- mlp_m: float32 [2, 1152, 4608], P(None, 'dp', 'tensor'), may hold values from -0.00036621094 to 0.00036621094
- mlp_v: float32 [2, 1152, 4608], P(None, 'dp', 'tensor'), may hold values from 1.0861013e-11 to 4.344405e-11
- up_bias: float32 [4608], P('tensor'), may hold values from -0.5 to 0.5
- up_m: float32 [4608], P('tensor'), may hold values from -9.1552734e-05 to 9.1552734e-05
- up_v: float32 [4608], P('tensor'), may hold values from 1.737762e-12 to 6.951048e-12
- side_vec: float32 [9, 1152], replicated, may hold values from -0.5 to 1.5
- side_m: float32 [9, 1152], replicated, may hold values from -0.0014648438 to 0.0014648438
- side_v: float32 [9, 1152], replicated, may hold values from 1.737762e-10 to 6.951048e-10
- time_w: float32 [6, 256, 1152], P(None, 'dp'), may hold values from -0.375 to 0.375
- time_m: float32 [6, 256, 1152], P(None, 'dp'), may hold values from -0.00036621094 to 0.00036621094
- time_v: float32 [6, 256, 1152], P(None, 'dp'), may hold values from 4.344405e-11 to 1.737762e-10
Outputs:
- block_out: bfloat16 [2048, 1152], P('dp')
- latent_grad: float32 [2048, 1152], P('dp')
- grad_norm: float32 [], replicated
- attn_new: float32 [8, 1152, 1152], P(None, 'dp', 'tensor')
- attn_m_new: float32 [8, 1152, 1152], P(None, 'dp', 'tensor')
- attn_v_new: float32 [8, 1152, 1152], P(None, 'dp', 'tensor')
- mlp_new: float32 [2, 1152, 4608], P(None, 'dp', 'tensor')
- mlp_m_new: float32 [2, 1152, 4608], P(None, 'dp', 'tensor')
- mlp_v_new: float32 [2, 1152, 4608], P(None, 'dp', 'tensor')
- up_new: float32 [4608], P('tensor')
- up_m_new: float32 [4608], P('tensor')
- up_v_new: float32 [4608], P('tensor')
- side_new: float32 [9, 1152], replicated
- side_m_new: float32 [9, 1152], replicated
- side_v_new: float32 [9, 1152], replicated
- time_new: float32 [6, 256, 1152], P(None, 'dp')
- time_m_new: float32 [6, 256, 1152], P(None, 'dp')
- time_v_new: float32 [6, 256, 1152], P(None, 'dp')
The draws below stay inside these ranges and needn't reach their ends.
Inputs may be any that keep to these rules, and one draw needn't show every extreme that they name: `clip_count`: some index of dp has all 2 clips live in every draw. `text_len`: some clip uses all 256 caption slots in every draw.
All inputs are finite; a program needn't handle non-finite values.
Results may differ from the reference program's by a relative error of at most 0.025.
The reference program's roundings to bfloat16 on the way count: a program that leaves them out, or rounds other values in their place, can miss the bound.
Values may be sent and summed in bfloat16 or wider, within the bound.
A program may use at most 192 MiB of HBM per device.

```python
import math
import jax
import jax.numpy as jnp
from jax import lax

D = 1152
HEADS = 16
FF = 4608
TFREQ = 256
FRAMES = 16
TEXT = 256
PATCHES = 8
CLIPS_DEV = 2
OPT_STEP = 10
CLIPS = 16
ROWS = 2048
PARAMS = 23018112
N_DP = 8


def draw_clip_count(key, part):
    key = jax.random.fold_in(key, 11)
    first, second = jax.random.split(key)
    counts = jax.random.randint(first, (N_DP,), 1, CLIPS_DEV + 1)
    chosen = jax.random.randint(second, (), 0, N_DP)
    return jnp.where(jnp.arange(N_DP) == chosen, CLIPS_DEV, counts).astype(jnp.int32)


def draw_text_len(key, part):
    key = jax.random.fold_in(key, 23)
    first, second = jax.random.split(key)
    lengths = jax.random.randint(first, (CLIPS_DEV * N_DP,), max(1, TEXT // 8), TEXT + 1)
    chosen = jax.random.randint(second, (), 0, CLIPS_DEV * N_DP)
    return jnp.where(jnp.arange(CLIPS_DEV * N_DP) == chosen, TEXT, lengths).astype(jnp.int32)


def draw_attn_w(key, part):
    key = jax.random.fold_in(key, 37)
    base = jax.random.normal(key, (8, D, D), jnp.float32)
    factors = jnp.array([1.0, 1.0, 1.0, 2.0, 1.0, 1.0, 1.0, 4.0], jnp.float32)
    return base * factors[:, None, None] * D ** (-0.5)


def with_ends(values, key, low, largest):
    longest = values.shape.index(max(values.shape))
    spots = []
    for shift in (0, 1):
        where = [jax.random.randint(jax.random.fold_in(key, axis), (), 0, length) for axis, length in enumerate(values.shape)]
        where[longest] = (where[longest] + shift) % values.shape[longest]
        spots.append(tuple(where))
    return values.at[spots[0]].set(low).at[spots[1]].set(largest)


def shard_levels(own_key, extent, cuts, least, top_value):
    factor_of, own = 1.0, jax.random.fold_in(own_key, 6)
    for axis_at, blocks in cuts:
        steps = jnp.exp(jax.random.uniform(jax.random.fold_in(own, axis_at), (blocks,), jnp.float32, least / len(cuts), top_value / len(cuts)))
        factor_of = factor_of * jnp.repeat(steps, extent[axis_at] // blocks).reshape([-1 if axis == axis_at else 1 for axis in range(len(extent))])
    return factor_of


def normal_values(own_key, shape, scale, most, pieces=(), held_as=jnp.bfloat16):
    entries = scale * jax.random.normal(own_key, shape, jnp.float32)
    if pieces:
        entries = entries * shard_levels(own_key, shape, pieces, -0.22, 0.18)
    return jnp.clip(entries, -most, most).astype(held_as)


def setup_inputs(seed: int = 0) -> dict:
    splits = jax.random.split(jax.random.key(seed), 23)
    return {
        "latent": normal_values(splits[0], (ROWS, D), 1.0, 6.0, ((0, 8),)),
        "noise": normal_values(splits[1], (ROWS, D), 1.0, 6.0, ((0, 8),)),
        "text": normal_values(splits[2], (CLIPS, TEXT, D), 1.0, 6.0, ((0, 8),)),
        "tsteps": with_ends(jax.random.randint(splits[3], (CLIPS,), 0, 1000), jax.random.fold_in(splits[3], 1), 0, 999).astype(jnp.int32),
        "clip_count": draw_clip_count(jax.random.fold_in(splits[22], 71), 0),
        "text_len": draw_text_len(jax.random.fold_in(splits[22], 71), 0),
        "cotangent": normal_values(splits[6], (ROWS, D), 1.0, 6.0, ((0, 8),)),
        "attn_w": draw_attn_w(jax.random.fold_in(splits[22], 71), 0),
        "attn_m": normal_values(splits[8], (8, D, D), (0.111 * PARAMS ** -0.5), 0.00036621094, ((1, 8), (2, 4)), jnp.float32),
        "attn_v": jnp.clip(jnp.exp(math.log(1.737762017617328e-10) - 1.3862944 * jax.random.uniform(splits[9], (8, D, D), jnp.float32) ** shard_levels(splits[9], (8, D, D), ((1, 8), (2, 4)), -0.2, 0.2)), 4.34440504404332e-11, 1.737762017617328e-10),
        "mlp_w": normal_values(splits[10], (2, D, FF), D ** -0.5, 0.1875, ((1, 8), (2, 4)), jnp.float32),
        "mlp_m": normal_values(splits[11], (2, D, FF), (0.111 * PARAMS ** -0.5), 0.00036621094, ((1, 8), (2, 4)), jnp.float32),
        "mlp_v": jnp.clip(jnp.exp(math.log(4.34440504404332e-11) - 1.3862944 * jax.random.uniform(splits[12], (2, D, FF), jnp.float32) ** shard_levels(splits[12], (2, D, FF), ((1, 8), (2, 4)), -0.2, 0.2)), 1.08610126101083e-11, 4.34440504404332e-11),
        "up_bias": jnp.clip(jax.random.uniform(splits[13], (FF,), jnp.float32, -0.5, 0.5) * shard_levels(splits[13], (FF,), ((0, 4),), -0.4, 0.0), -0.5, 0.5),
        "up_m": normal_values(splits[14], (FF,), (0.03 * PARAMS ** -0.5), 9.1552734375e-05, ((0, 4),), jnp.float32),
        "up_v": jnp.clip(jnp.exp(math.log(6.951047810260791e-12) - 1.3862944 * jax.random.uniform(splits[15], (FF,), jnp.float32) ** shard_levels(splits[15], (FF,), ((0, 4),), -0.2, 0.2)), 1.7377619525651977e-12, 6.951047810260791e-12),
        "side_vec": jnp.clip(jax.random.uniform(splits[16], (9, D), jnp.float32, -0.5, 1.5), -0.5, 1.5),
        "side_m": normal_values(splits[17], (9, D), (0.444 * PARAMS ** -0.5), 0.0014648438, (), jnp.float32),
        "side_v": jnp.clip(jnp.exp(jax.random.uniform(splits[18], (9, D), jnp.float32, math.log(1.737762017617328e-10), math.log(6.951048070469312e-10))), 1.737762017617328e-10, 6.951048070469312e-10),
        "time_w": normal_values(splits[19], (6, TFREQ, D), TFREQ ** -0.5, 0.375, ((1, 8),), jnp.float32),
        "time_m": normal_values(splits[20], (6, TFREQ, D), (0.111 * PARAMS ** -0.5), 0.00036621094, ((1, 8),), jnp.float32),
        "time_v": jnp.clip(jnp.exp(math.log(1.737762017617328e-10) - 1.3862944 * jax.random.uniform(splits[21], (6, TFREQ, D), jnp.float32) ** shard_levels(splits[21], (6, TFREQ, D), ((1, 8),), -0.2, 0.2)), 4.34440504404332e-11, 1.737762017617328e-10),
    }


HIGHEST = lax.Precision.HIGHEST
BETA_ONE = 0.9
BETA_TWO = 0.999
EPSILON = 1e-08
DECAY_RATE = 0.01
CLIP_NORM = 1.0
RATE_MATRIX = 0.02
RATE_TIME = 0.05
RATE_VECTOR = 0.3

@jax.custom_vjp
def low(v):
    return lax.optimization_barrier(v.astype(jnp.bfloat16)).astype(jnp.float32)

@jax.custom_vjp
def low_back(v):
    return v

def low_keep(v):
    return (low(v), None)

def low_pass(kept, grad):
    return (grad,)

def back_keep(v):
    return (v, None)

def back_low(kept, grad):
    return (low(grad),)
low.defvjp(low_keep, low_pass)
low_back.defvjp(back_keep, back_low)

def alpha_bar():
    steps = jnp.arange(1000).astype(jnp.float32)
    betas = 0.0001 + (0.02 - 0.0001) * steps / 999.0
    return jnp.exp(jnp.cumsum(jnp.log(1.0 - betas)))

def pick_rows(table, indices):
    spots = jnp.arange(table.shape[0]).astype(jnp.int32)
    return lax.optimization_barrier(jnp.sum(jnp.where(spots[None, :] == indices[:, None], table[None, :], 0.0), axis=1))

def time_features(indices):
    half = TFREQ // 2
    freqs = jnp.exp(-math.log(10000.0) * jnp.arange(half).astype(jnp.float32) / half)
    angles = indices.astype(jnp.float32)[:, None] * freqs[None, :]
    return jnp.concatenate([jnp.cos(angles), jnp.sin(angles)], axis=1)

def layer_norm(values):
    centered = values - lax.optimization_barrier(jnp.mean(values, axis=-1, keepdims=True))
    return centered * lax.rsqrt(lax.optimization_barrier(jnp.mean(centered * centered, axis=-1, keepdims=True)) + 1e-06)

def gelu_tanh(upper):
    return 0.5 * upper * (1.0 + jnp.tanh(0.7978845608028654 * (upper + 0.044715 * upper * upper * upper)))

def softmax_rows(scores):
    peak = lax.optimization_barrier(jnp.max(scores, axis=-1, keepdims=True))
    expo = jnp.exp(scores - peak)
    return expo / lax.optimization_barrier(jnp.sum(expo, axis=-1, keepdims=True))

def adamw(weight, first, second, grad, factor, rate):
    clipped = grad * factor
    first = BETA_ONE * first + (1.0 - BETA_ONE) * clipped
    second = BETA_TWO * second + (1.0 - BETA_TWO) * clipped * clipped
    first_hat = first / (1.0 - BETA_ONE ** OPT_STEP)
    second_hat = second / (1.0 - BETA_TWO ** OPT_STEP)
    weight = weight - rate * (first_hat / (jnp.sqrt(second_hat) + EPSILON) + DECAY_RATE * weight)
    return (weight, first, second)

def forward(latent, attn_w, mlp_w, up_bias, side_vec, time_w, noise, text, tsteps, live, text_len):
    clips = tsteps.shape[0]
    seq_rows = PATCHES * FRAMES
    head_width = D // HEADS
    scale = head_width ** (-0.5)
    tlen = text.shape[1]
    abar = pick_rows(alpha_bar(), tsteps)
    keep_root = jnp.sqrt(abar)[:, None, None]
    noise_root = jnp.sqrt(1.0 - abar)[:, None, None]
    start = keep_root * latent.reshape(clips, seq_rows, D) + noise_root * noise.reshape(clips, seq_rows, D)
    feats = low(jax.nn.silu(time_features(tsteps)))
    w_attn = low(attn_w)
    w_mlp = low(mlp_w)
    w_time = low(time_w)
    modul = side_vec[3:][None] + jnp.einsum('cf,jfd->cjd', feats, w_time, precision=HIGHEST)
    hidden_one = low(layer_norm(start) * (1.0 + modul[:, 1:2]) + modul[:, 0:1])
    projected = low_back(low(jnp.einsum('cqd,kde->kcqe', hidden_one, w_attn[0:3], precision=HIGHEST)))
    shaped = projected.reshape(3, clips * PATCHES, FRAMES, HEADS, head_width)
    scores = low_back(scale * jnp.einsum('sfhd,sghd->shfg', shaped[0], shaped[1], precision=HIGHEST))
    probs = low(softmax_rows(scores))
    mixed = jnp.einsum('shfg,sghd->sfhd', probs, shaped[2], precision=HIGHEST)
    mixed = low_back(low(mixed.reshape(clips, seq_rows, D)))
    attended = low_back(jnp.einsum('cqe,oe->cqo', mixed, w_attn[3], precision=HIGHEST)) + side_vec[0]
    middle = start + modul[:, 2:3] * attended
    query_in = low(middle)
    cross_query = low_back(low(jnp.einsum('cqd,de->cqe', query_in, w_attn[4], precision=HIGHEST)))
    text_proj = low_back(low(jnp.einsum('cld,kde->kcle', text, w_attn[5:7], precision=HIGHEST)))
    query_heads = cross_query.reshape(clips, seq_rows, HEADS, head_width)
    text_heads = text_proj.reshape(2, clips, tlen, HEADS, head_width)
    cross_scores = low_back(scale * jnp.einsum('cqhd,ckhd->chqk', query_heads, text_heads[0], precision=HIGHEST))
    allowed = (jnp.arange(tlen).astype(jnp.int32)[None, :] < text_len[:, None])[:, None, None, :]
    cross_probs = low(softmax_rows(jnp.where(allowed, cross_scores, -1e+30)))
    cross_mixed = jnp.einsum('chqk,ckhd->cqhd', cross_probs, text_heads[1], precision=HIGHEST)
    cross_mixed = low_back(low(cross_mixed.reshape(clips, seq_rows, D)))
    crossed = low_back(jnp.einsum('cqe,oe->cqo', cross_mixed, w_attn[7], precision=HIGHEST)) + side_vec[1]
    after = middle + crossed
    hidden_two = low(layer_norm(after) * (1.0 + modul[:, 4:5]) + modul[:, 3:4])
    upper = low_back(jnp.einsum('cqd,df->cqf', hidden_two, w_mlp[0], precision=HIGHEST) + up_bias)
    activated = low(gelu_tanh(upper))
    mlp_out = low_back(jnp.einsum('cqf,of->cqo', activated, w_mlp[1], precision=HIGHEST)) + side_vec[2]
    final = after + modul[:, 5:6] * mlp_out
    return (live[:, None, None] * final).reshape(clips * seq_rows, D)

def reference(latent, noise, text, tsteps, clip_count, text_len, cotangent, attn_w, attn_m, attn_v, mlp_w, mlp_m, mlp_v, up_bias, up_m, up_v, side_vec, side_m, side_v, time_w, time_m, time_v):
    live = (jnp.arange(CLIPS_DEV).astype(jnp.int32)[None, :] < clip_count[:, None]).reshape(-1).astype(jnp.float32)
    noise_full = noise.astype(jnp.float32)
    text_full = text.astype(jnp.float32)

    def apply(latent_in, attn_in, mlp_in, bias_in, side_in, time_in):
        return forward(latent_in, attn_in, mlp_in, bias_in, side_in, time_in, noise_full, text_full, tsteps, live, text_len)
    block, pull = jax.vjp(apply, latent.astype(jnp.float32), attn_w, mlp_w, up_bias, side_vec, time_w)
    latent_grad, grad_attn, grad_mlp, grad_up, grad_side, grad_time = pull(cotangent.astype(jnp.float32))
    squared_terms = jnp.sum(grad_attn * grad_attn) + jnp.sum(grad_mlp * grad_mlp) + jnp.sum(grad_up * grad_up)
    squared_terms = squared_terms + jnp.sum(grad_side * grad_side) + jnp.sum(grad_time * grad_time)
    grad_norm = jnp.sqrt(squared_terms)
    factor = jnp.minimum(1.0, CLIP_NORM / (grad_norm + 1e-06))
    attn_new, attn_m_new, attn_v_new = adamw(attn_w, attn_m, attn_v, grad_attn, factor, RATE_MATRIX)
    mlp_new, mlp_m_new, mlp_v_new = adamw(mlp_w, mlp_m, mlp_v, grad_mlp, factor, RATE_MATRIX)
    up_new, up_m_new, up_v_new = adamw(up_bias, up_m, up_v, grad_up, factor, RATE_VECTOR)
    side_new, side_m_new, side_v_new = adamw(side_vec, side_m, side_v, grad_side, factor, RATE_VECTOR)
    time_new, time_m_new, time_v_new = adamw(time_w, time_m, time_v, grad_time, factor, RATE_TIME)
    return (block.astype(jnp.bfloat16), latent_grad, grad_norm, attn_new, attn_m_new, attn_v_new, mlp_new, mlp_m_new, mlp_v_new, up_new, up_m_new, up_v_new, side_new, side_m_new, side_v_new, time_new, time_m_new, time_v_new)
```

```python
import functools
import math

import jax
import jax.numpy as jnp
from jax import lax
from jax.experimental import pallas as pl
from jax.experimental.pallas import tpu as pltpu
from jax.sharding import PartitionSpec as P

D = 1152
HEADS = 16
TFREQ = 256
FRAMES = 16
OPT_STEP = 10


HIGHEST = lax.Precision.HIGHEST
BETA_ONE = 0.9
BETA_TWO = 0.999
EPSILON = 1e-08
DECAY_RATE = 0.01
CLIP_NORM = 1.0
RATE_MATRIX = 0.02
RATE_TIME = 0.05
RATE_VECTOR = 0.3


def alpha_bar():
    steps = jnp.arange(1000).astype(jnp.float32)
    betas = 0.0001 + (0.02 - 0.0001) * steps / 999.0
    return jnp.exp(jnp.cumsum(jnp.log(1.0 - betas)))


def pick_rows(table, indices):
    spots = jnp.arange(table.shape[0])
    return jnp.sum(jnp.where(spots[None, :] == indices[:, None], table[None, :], 0.0), axis=1)


def time_features(indices):
    half = TFREQ // 2
    freqs = jnp.exp(-math.log(10000.0) * jnp.arange(half).astype(jnp.float32) / half)
    angles = indices.astype(jnp.float32)[:, None] * freqs[None, :]
    return jnp.concatenate([jnp.cos(angles), jnp.sin(angles)], axis=1)


def layer_parts(values):
    centered = values - jnp.mean(values, axis=-1, keepdims=True)
    inverse = lax.rsqrt(jnp.mean(centered * centered, axis=-1, keepdims=True) + 1e-06)
    return (centered * inverse, inverse)


def norm_back(grad_out, normed, inverse):
    first_mean = jnp.mean(grad_out, axis=-1, keepdims=True)
    second_mean = jnp.mean(grad_out * normed, axis=-1, keepdims=True)
    return inverse * (grad_out - first_mean - normed * second_mean)


def gelu_tanh(upper):
    return (
        0.5
        * upper
        * (1.0 + jnp.tanh(0.7978845608028654 * (upper + 0.044715 * upper * upper * upper)))
    )


def gelu_slope(upper):
    tangent = jnp.tanh(0.7978845608028654 * (upper + 0.044715 * upper * upper * upper))
    inner = 0.7978845608028654 * (1.0 + 3.0 * 0.044715 * upper * upper)
    return 0.5 * (1.0 + tangent) + 0.5 * upper * (1.0 - tangent * tangent) * inner


def log_total(scores):
    peak = jnp.max(scores, axis=-1, keepdims=True)
    return peak + jnp.log(jnp.sum(jnp.exp(scores - peak), axis=-1, keepdims=True))


def softmax_back(probs, grad_probs):
    return probs * (grad_probs - jnp.sum(probs * grad_probs, axis=-1, keepdims=True))


def adamw(weight, first, second, grad, factor, rate):
    clipped = grad * factor
    first = BETA_ONE * first + (1.0 - BETA_ONE) * clipped
    second = BETA_TWO * second + (1.0 - BETA_TWO) * clipped * clipped
    first_hat = first / (1.0 - BETA_ONE**OPT_STEP)
    second_hat = second / (1.0 - BETA_TWO**OPT_STEP)
    weight = weight - rate * (first_hat / (jnp.sqrt(second_hat) + EPSILON) + DECAY_RATE * weight)
    return (weight, first, second)


def row_layout():
    return (1, jnp.int32(0))


def row_total(term_fn, total_rows):
    return lax.psum(term_fn(0, total_rows), "tensor")


def clip_totals(modul_terms, bias_terms):
    return (modul_terms, bias_terms)


def plain_shards(
    latent,
    noise,
    text,
    tsteps,
    clip_count,
    text_len,
    cotangent,
    attn_w,
    attn_m,
    attn_v,
    mlp_w,
    mlp_m,
    mlp_v,
    up_bias,
    up_m,
    up_v,
    side_vec,
    side_m,
    side_v,
    time_w,
    time_m,
    time_v,
):
    low_type = jnp.bfloat16
    full_type = jnp.float32
    n_tensor = lax.axis_size("tensor")
    n_data = lax.axis_size("dp")
    clips, tlen, width = text.shape
    row_count = latent.shape[0]
    seq_rows = row_count // clips
    seqs = row_count // FRAMES
    head_width = D // HEADS
    scale = head_width ** (-0.5)
    w_attn, w_mlp, w_time = (
        lax.all_gather(attn_w.astype(low_type), "dp", axis=1, tiled=True),
        lax.all_gather(mlp_w.astype(low_type), "dp", axis=1, tiled=True),
        lax.all_gather(time_w.astype(low_type), "dp", axis=1, tiled=True),
    )
    device_local = w_attn.shape[2]
    heads_here = device_local // head_width
    pieces, part = row_layout()
    share = row_count // pieces
    row_ids = jnp.arange(share)
    select = (row_ids[:, None] // seq_rows == jnp.arange(clips)[None, :]).astype(full_type)

    def per_row(values):
        return jnp.tensordot(select, values, axes=1, precision=HIGHEST)

    def per_clip(values):
        return jnp.tensordot(select.T, values, axes=1, precision=HIGHEST)

    abar = pick_rows(alpha_bar(), tsteps)
    keep_root = jnp.sqrt(abar)[:, None, None]
    noise_root = jnp.sqrt(1.0 - abar)[:, None, None]
    start = keep_root * latent.astype(full_type).reshape(
        clips, seq_rows, width
    ) + noise_root * noise.astype(full_type).reshape(clips, seq_rows, width)
    feats = jax.nn.silu(time_features(tsteps)).astype(low_type)
    modul = side_vec[3:][None] + jnp.einsum(
        "cf,jfd->cjd", feats, w_time, preferred_element_type=full_type
    )
    live_clip = (jnp.arange(clips) < clip_count[0]).astype(full_type)
    live = live_clip[:, None, None]
    mod_rows = per_row(modul)
    live_rows = per_row(live_clip)[:, None]
    root_rows = per_row(jnp.sqrt(abar))[:, None]
    normed_one, inverse_one = layer_parts(start)
    hidden_one = (
        (normed_one * (1.0 + modul[:, 1:2]) + modul[:, 0:1])
        .astype(low_type)
        .reshape(row_count, width)
    )
    projected = jnp.einsum(
        "rd,kde->kre", hidden_one, w_attn[0:3], preferred_element_type=full_type
    ).astype(low_type)
    shaped = projected.reshape(3, seqs, FRAMES, heads_here, head_width)
    self_scores = (
        jnp.einsum("sfhd,sghd->shfg", shaped[0], shaped[1], preferred_element_type=full_type)
        * scale
    )
    self_log = log_total(self_scores)
    self_probs = jnp.exp(self_scores - self_log).astype(low_type)
    mixed_one = (
        jnp.einsum("shfg,sghd->sfhd", self_probs, shaped[2], preferred_element_type=full_type)
        .astype(low_type)
        .reshape(row_count, device_local)
    )

    def self_out(begin, count):
        return jnp.einsum("re,oe->ro", mixed_one, w_attn[3], preferred_element_type=full_type)

    attended = row_total(self_out, row_count) + side_vec[0]
    start_rows = start.reshape(row_count, width)
    middle = start_rows + mod_rows[:, 2] * attended
    query_in = middle.astype(low_type)
    cross_query = jnp.dot(query_in, w_attn[4], preferred_element_type=full_type).astype(low_type)
    text_proj = jnp.einsum(
        "cld,kde->kcle", text, w_attn[5:7], preferred_element_type=full_type
    ).astype(low_type)
    query_heads = cross_query.reshape(clips, seq_rows, heads_here, head_width)
    text_heads = text_proj.reshape(2, clips, tlen, heads_here, head_width)
    allowed = (jnp.arange(tlen)[None, :] < text_len[:, None])[:, None, None, :]
    cross_scores = jnp.where(
        allowed,
        jnp.einsum("cqhd,ckhd->chqk", query_heads, text_heads[0], preferred_element_type=full_type)
        * scale,
        -1e30,
    )
    cross_log = log_total(cross_scores)
    cross_probs = jnp.exp(cross_scores - cross_log).astype(low_type)
    mixed_two = (
        jnp.einsum("chqk,ckhd->cqhd", cross_probs, text_heads[1], preferred_element_type=full_type)
        .astype(low_type)
        .reshape(row_count, device_local)
    )

    def cross_out(begin, count):
        return jnp.einsum("re,oe->ro", mixed_two, w_attn[7], preferred_element_type=full_type)

    crossed = row_total(cross_out, row_count) + side_vec[1]
    after = middle + crossed
    normed_two, inverse_two = layer_parts(after)
    hidden_two = (normed_two * (1.0 + mod_rows[:, 4]) + mod_rows[:, 3]).astype(low_type)
    upper = jnp.dot(hidden_two, w_mlp[0], preferred_element_type=full_type) + up_bias
    activated = gelu_tanh(upper).astype(low_type)

    def down_out(begin, count):
        return jnp.einsum("rf,of->ro", activated, w_mlp[1], preferred_element_type=full_type)

    mlp_out = row_total(down_out, row_count) + side_vec[2]
    final = after + mod_rows[:, 5] * mlp_out
    block_out = (live_rows * final).astype(low_type)
    grad_four = live_rows * cotangent.astype(full_type)
    d_gate_two = per_clip(grad_four * mlp_out)
    d_mlp_full = (
        modul[:, 5:6] * live * cotangent.astype(full_type).reshape(clips, seq_rows, width)
    ).reshape(row_count, width)
    d_bias_two = jnp.sum(d_mlp_full, axis=0)
    d_mlp_low = d_mlp_full.astype(low_type)
    grad_down = jnp.einsum("ro,rf->of", d_mlp_low, activated, preferred_element_type=full_type)
    d_act = jnp.einsum("ro,of->rf", d_mlp_low, w_mlp[1], preferred_element_type=full_type)
    d_upper = (d_act * gelu_slope(upper)).astype(low_type)
    grad_upbias = jnp.sum(d_upper.astype(full_type), axis=0)
    grad_up = jnp.einsum("rd,rf->df", hidden_two, d_upper, preferred_element_type=full_type)
    grad_mlp = jnp.stack([grad_up, grad_down])

    def up_back(begin, count):
        return jnp.einsum("rf,df->rd", d_upper, w_mlp[0], preferred_element_type=full_type)

    d_hidden_two = row_total(up_back, row_count)
    d_shift_two = per_clip(d_hidden_two)
    d_scale_two = per_clip(d_hidden_two * normed_two)
    grad_three = grad_four + norm_back(
        d_hidden_two * (1.0 + mod_rows[:, 4]), normed_two, inverse_two
    )
    d_bias_one = jnp.sum(grad_three, axis=0)
    d_cross_low = grad_three.astype(low_type)
    grad_cout = jnp.einsum("ro,re->oe", d_cross_low, mixed_two, preferred_element_type=full_type)
    d_mixed_two = (
        jnp.einsum("ro,oe->re", d_cross_low, w_attn[7], preferred_element_type=full_type)
        .astype(low_type)
        .reshape(clips, seq_rows, heads_here, head_width)
    )
    cross_again = jnp.where(
        allowed,
        jnp.einsum("cqhd,ckhd->chqk", query_heads, text_heads[0], preferred_element_type=full_type)
        * scale,
        -1e30,
    )
    cross_full = jnp.exp(cross_again - cross_log)
    d_cprobs = jnp.einsum(
        "cqhd,ckhd->chqk", d_mixed_two, text_heads[1], preferred_element_type=full_type
    )
    d_cvalues = jnp.einsum(
        "chqk,cqhd->ckhd",
        cross_full.astype(low_type),
        d_mixed_two,
        preferred_element_type=full_type,
    ).astype(low_type)
    d_cscores = softmax_back(cross_full, d_cprobs).astype(low_type)
    d_cquery = (
        (
            jnp.einsum(
                "chqk,ckhd->cqhd", d_cscores, text_heads[0], preferred_element_type=full_type
            )
            * scale
        )
        .astype(low_type)
        .reshape(row_count, device_local)
    )
    d_ckeys = (
        jnp.einsum("chqk,cqhd->ckhd", d_cscores, query_heads, preferred_element_type=full_type)
        * scale
    ).astype(low_type)
    d_text_proj = jnp.stack([d_ckeys, d_cvalues]).reshape(2, clips * tlen, device_local)
    grad_cquery = jnp.einsum("rd,re->de", query_in, d_cquery, preferred_element_type=full_type)
    grad_ctext = jnp.einsum(
        "rd,kre->kde",
        text.reshape(clips * tlen, width),
        d_text_proj,
        preferred_element_type=full_type,
    )

    def cquery_back(begin, count):
        return jnp.einsum("re,de->rd", d_cquery, w_attn[4], preferred_element_type=full_type)

    grad_two = grad_three + row_total(cquery_back, row_count)
    d_gate_one = per_clip(grad_two * attended)
    d_attended = mod_rows[:, 2] * grad_two
    d_bias_zero = jnp.sum(d_attended, axis=0)
    d_att_low = d_attended.astype(low_type)
    grad_sout = jnp.einsum("ro,re->oe", d_att_low, mixed_one, preferred_element_type=full_type)
    d_mixed_one = (
        jnp.einsum("ro,oe->re", d_att_low, w_attn[3], preferred_element_type=full_type)
        .astype(low_type)
        .reshape(seqs, FRAMES, heads_here, head_width)
    )
    self_again = (
        jnp.einsum("sfhd,sghd->shfg", shaped[0], shaped[1], preferred_element_type=full_type)
        * scale
    )
    self_full = jnp.exp(self_again - self_log)
    d_sprobs = jnp.einsum(
        "sfhd,sghd->shfg", d_mixed_one, shaped[2], preferred_element_type=full_type
    )
    self_value_gradient = jnp.einsum(
        "shfg,sfhd->sghd", self_full.astype(low_type), d_mixed_one, preferred_element_type=full_type
    ).astype(low_type)
    d_sscores = softmax_back(self_full, d_sprobs).astype(low_type)
    self_query_gradient = (
        jnp.einsum("shfg,sghd->sfhd", d_sscores, shaped[1], preferred_element_type=full_type)
        * scale
    ).astype(low_type)
    self_key_gradient = (
        jnp.einsum("shfg,sfhd->sghd", d_sscores, shaped[0], preferred_element_type=full_type)
        * scale
    ).astype(low_type)
    projection_gradient = jnp.stack(
        [self_query_gradient, self_key_gradient, self_value_gradient]
    ).reshape(3, row_count, device_local)
    grad_qkv = jnp.einsum(
        "rd,kre->kde", hidden_one, projection_gradient, preferred_element_type=full_type
    )

    def qkv_back(begin, count):
        return jnp.einsum(
            "kre,kde->rd", projection_gradient, w_attn[0:3], preferred_element_type=full_type
        )

    d_hidden_one = row_total(qkv_back, row_count)
    normed_one_rows = normed_one.reshape(row_count, width)
    inverse_one_rows = inverse_one.reshape(row_count, 1)
    d_shift_one = per_clip(d_hidden_one)
    d_scale_one = per_clip(d_hidden_one * normed_one_rows)
    grad_one = grad_two + norm_back(
        d_hidden_one * (1.0 + mod_rows[:, 1]), normed_one_rows, inverse_one_rows
    )
    latent_grad = root_rows * grad_one
    d_modul_part = jnp.stack(
        [d_shift_one, d_scale_one, d_gate_one, d_shift_two, d_scale_two, d_gate_two], axis=1
    )
    bias_part = jnp.stack([d_bias_zero, d_bias_one, d_bias_two])
    d_modul, bias_three = clip_totals(d_modul_part, bias_part)
    grad_time = jnp.einsum("cf,cjd->jfd", feats.astype(full_type), d_modul, precision=HIGHEST)
    grad_side = jnp.concatenate([bias_three, jnp.sum(d_modul, axis=0)], axis=0)
    grad_attn = jnp.concatenate(
        [grad_qkv, grad_sout[None], grad_cquery[None], grad_ctext, grad_cout[None]], axis=0
    )
    attn_shard, mlp_shard, time_shard = (
        lax.psum_scatter(grad_attn, "dp", scatter_dimension=1, tiled=True),
        lax.psum_scatter(grad_mlp, "dp", scatter_dimension=1, tiled=True),
        lax.psum_scatter(grad_time, "dp", scatter_dimension=1, tiled=True),
    )
    side_total, upbias_total = lax.psum((grad_side, grad_upbias), "dp")
    squared_terms = jnp.sum(attn_shard * attn_shard) + jnp.sum(mlp_shard * mlp_shard)
    squared_terms = squared_terms + jnp.sum(time_shard * time_shard) / n_tensor
    squared_terms = squared_terms + jnp.sum(upbias_total * upbias_total) / n_data
    squared_terms = squared_terms + jnp.sum(side_total * side_total) / (n_data * n_tensor)
    grad_norm = jnp.sqrt(lax.psum(squared_terms, ("dp", "tensor")))
    factor = jnp.minimum(1.0, CLIP_NORM / (grad_norm + 1e-06))
    attn_new, attn_m_new, attn_v_new = adamw(
        attn_w, attn_m, attn_v, attn_shard, factor, RATE_MATRIX
    )
    mlp_new, mlp_m_new, mlp_v_new = adamw(mlp_w, mlp_m, mlp_v, mlp_shard, factor, RATE_MATRIX)
    up_new, up_m_new, up_v_new = adamw(up_bias, up_m, up_v, upbias_total, factor, RATE_VECTOR)
    side_new, side_m_new, side_v_new = adamw(
        side_vec, side_m, side_v, side_total, factor, RATE_VECTOR
    )
    time_new, time_m_new, time_v_new = adamw(time_w, time_m, time_v, time_shard, factor, RATE_TIME)
    return (
        block_out,
        latent_grad,
        grad_norm,
        attn_new,
        attn_m_new,
        attn_v_new,
        mlp_new,
        mlp_m_new,
        mlp_v_new,
        up_new,
        up_m_new,
        up_v_new,
        side_new,
        side_m_new,
        side_v_new,
        time_new,
        time_m_new,
        time_v_new,
    )


MESH = pl.DeviceIdType.MESH
LOW = jnp.bfloat16
FULL = jnp.float32
TILE = 384


def dot(left, right, left_dim, right_dim):
    return lax.dot_general(
        left, right, (((left_dim,), (right_dim,)), ((), ())), preferred_element_type=FULL
    )


def ring_place(index, count):
    z, x = lax.div(index, 2), lax.rem(index, 2)
    return z + x * (count - 1 - 2 * z)


def ring_index(place, count):
    high = lax.div(place, count // 2)
    return 2 * (place + high * (count - 1 - 2 * place)) + high


def ring_items(count):
    right, left = [], []
    for hop in range(1, count // 2 + 1):
        for half in (0, 1):
            if hop <= count // 2 - half:
                right.append((half, hop))
                left.append((1 - half, hop))
    return right, left


class Ring:
    def __init__(self, count, rows, dp, tensor):
        self.count, self.rows = count, rows
        self.lead = -(-rows // 32) * 16
        self.items = ring_items(count)
        self.place = ring_place(dp, count)
        self.sides = [
            (ring_index(lax.rem(self.place + step, count), count), tensor)
            for step in (1, count - 1)
        ]
        self.steps = count - 1
        self.queue = []

    def half_rows(self, half):
        return (0, self.lead) if half == 0 else (self.lead, self.rows - self.lead)

    def block_rows(self, offset, half):
        index = ring_index(lax.rem(self.place + offset + 2 * self.count, self.count), self.count)
        begin, size = self.half_rows(half)
        return pl.ds(pl.multiple_of(index * self.rows + begin, 16), size)

    def pump(self, times):
        for _ in range(min(times, len(self.queue))):
            self.queue.pop(0)()


class Gather(Ring):
    def __init__(self, count, rows, dp, tensor, own, full, send, recv):
        super().__init__(count, rows, dp, tensor)
        self.own, self.full, self.send, self.recv = own, full, send, recv
        self.copies = {}
        self.left = {panel: self.steps for panel in range(full.shape[0])}
        for panel in range(full.shape[0]):
            for step in range(self.steps):
                self.queue.append(functools.partial(self.step, panel, step))

    def copy(self, panel, step, side):
        half, hop = self.items[side][step]
        sign = 1 if side == 0 else -1
        begin, size = self.half_rows(half)
        target = self.full.at[panel, self.block_rows(-sign * (hop - 1), half)]
        source = self.own.at[panel, pl.ds(begin, size)] if hop == 1 else target
        return pltpu.make_async_remote_copy(
            src_ref=source,
            dst_ref=target,
            send_sem=self.send.at[side, panel, step],
            recv_sem=self.recv.at[side, panel, step],
            device_id=self.sides[side],
            device_id_type=MESH,
        )

    def arrived(self, panel, step, side):
        half, hop = self.items[side][step]
        sign = 1 if side == 0 else -1
        here = self.full.at[panel, self.block_rows(-sign * hop, half)]
        pltpu.make_async_remote_copy(
            src_ref=here,
            dst_ref=here,
            send_sem=self.send.at[side, panel, step],
            recv_sem=self.recv.at[side, panel, step],
            device_id=self.sides[side],
            device_id_type=MESH,
        ).wait_recv()

    def step(self, panel, step):
        for side in (0, 1):
            if step >= 2:
                self.arrived(panel, step - 2, side)
            copy = self.copy(panel, step, side)
            copy.start()
            self.copies[side, panel, step] = copy
        self.left[panel] -= 1

    def finish(self, panel):
        while self.left[panel]:
            self.pump(1)
        if panel + 1 in self.left and self.left[panel + 1] == self.steps:
            self.pump(min(2, self.steps))
        for step in range(max(0, self.steps - 2), self.steps):
            for side in (0, 1):
                self.arrived(panel, step, side)

    def drain(self):
        for copy in self.copies.values():
            copy.wait_send()


class Reduce(Ring):
    def __init__(self, count, rows, dp, tensor, part, slots, total, send, recv):
        super().__init__(count, rows, dp, tensor)
        self.part, self.slots, self.total = part, slots, total
        self.send, self.recv = send, recv
        self.copies = {}
        self.last = None

    def reach(self, side, half):
        return max(hop for kind, hop in self.items[side] if kind == half)

    def copy(self, panel, step, side):
        half, hop = self.items[side][step]
        size = self.half_rows(half)[1]
        if hop == 1:
            sign = 1 if side == 0 else -1
            offset = sign * self.reach(side, half)
            source = self.part.at[panel, self.block_rows(offset, half)]
        else:
            source = self.slots.at[side, panel, step - 2, pl.ds(0, size)]
        return pltpu.make_async_remote_copy(
            src_ref=source,
            dst_ref=self.slots.at[side, panel, step, pl.ds(0, size)],
            send_sem=self.send.at[side, panel, step],
            recv_sem=self.recv.at[side, panel, step],
            device_id=self.sides[side],
            device_id_type=MESH,
        )

    def step(self, panel, step):
        for side in (0, 1):
            half, hop = self.items[side][step]
            if hop > 1:
                self.copies[side, panel, step - 2].wait_recv()
                sign = 1 if side == 0 else -1
                offset = sign * (self.reach(side, half) + 1 - hop)
                size = self.half_rows(half)[1]
                slot = self.slots.at[side, panel, step - 2, pl.ds(0, size)]
                slot[...] = (
                    slot[...].astype(FULL)
                    + self.part[panel, self.block_rows(offset, half), :].astype(FULL)
                ).astype(LOW)
            copy = self.copy(panel, step, side)
            copy.start()
            self.copies[side, panel, step] = copy

    def add_panel(self, panel):
        for step in range(self.steps):
            self.queue.append(functools.partial(self.step, panel, step))
            if step == min(1, self.steps - 1) and self.last is not None:
                self.queue.append(functools.partial(self.finish, self.last))
        self.last = panel

    def finish(self, panel):
        for step in range(max(0, self.steps - 2), self.steps):
            for side in (0, 1):
                self.copies[side, panel, step].wait_recv()
        for half in (0, 1):
            begin, size = self.half_rows(half)
            value = self.part[panel, self.block_rows(0, half), :].astype(FULL)
            for side in (0, 1):
                spots = [s for s, item in enumerate(self.items[side]) if item[0] == half]
                if spots:
                    value = value + self.slots[side, panel, spots[-1], pl.ds(0, size), :].astype(FULL)
            self.total[panel, pl.ds(begin, size), :] = value

    def complete(self):
        self.pump(len(self.queue))
        self.finish(self.last)

    def drain(self):
        for copy in self.copies.values():
            copy.wait_send()


class Sum:
    def __init__(self, place, part, near, out, far, sems):
        self.place, self.part, self.near, self.out, self.far, self.sems = place, part, near, out, far, sems

    def start(self):
        dp, me, mate, across, beyond, rows = self.place
        self.copies = []
        for spot, block in enumerate((mate, beyond)):
            copy = pltpu.make_async_remote_copy(
                src_ref=self.part.at[pl.ds(pl.multiple_of(block * rows, 16), rows)],
                dst_ref=self.near.at[spot],
                send_sem=self.sems.at[spot],
                recv_sem=self.sems.at[3 + spot],
                device_id=(dp, mate),
                device_id_type=MESH,
            )
            copy.start()
            self.copies.append(copy)

    def middle(self):
        dp, me, mate, across, beyond, rows = self.place
        for copy in self.copies:
            copy.wait()
        block = pl.ds(pl.multiple_of(across * rows, 16), rows)
        self.out[...] = (self.part[block, :] + self.near[1]).astype(LOW)
        self.last = pltpu.make_async_remote_copy(
            src_ref=self.out,
            dst_ref=self.far,
            send_sem=self.sems.at[2],
            recv_sem=self.sems.at[5],
            device_id=(dp, across),
            device_id_type=MESH,
        )
        self.last.start()

    def end(self):
        dp, me, mate, across, beyond, rows = self.place
        self.last.wait()
        block = pl.ds(pl.multiple_of(me * rows, 16), rows)
        return self.part[block, :] + self.near[0] + self.far[...].astype(FULL)


class Share:
    def __init__(self, place, full, sems):
        self.place, self.full, self.sems = place, full, sems

    def rows(self, block):
        rows = self.place[5]
        return self.full.at[pl.ds(pl.multiple_of(block * rows, 16), rows)]

    def copy(self, block, target, spot):
        return pltpu.make_async_remote_copy(
            src_ref=self.rows(block),
            dst_ref=self.rows(block),
            send_sem=self.sems.at[spot],
            recv_sem=self.sems.at[3 + spot],
            device_id=(self.place[0], target),
            device_id_type=MESH,
        )

    def start(self):
        dp, me, mate, across, beyond, rows = self.place
        self.far = self.copy(me, across, 0)
        self.near = self.copy(me, mate, 1)
        self.far.start()
        self.near.start()

    def middle(self):
        dp, me, mate, across, beyond, rows = self.place
        self.far.wait()
        self.onward = self.copy(across, mate, 2)
        self.onward.start()

    def end(self):
        self.near.wait()
        self.onward.wait()


def row_norm(values):
    centered = values - jnp.mean(values, axis=-1, keepdims=True)
    inverse = lax.rsqrt(jnp.mean(centered * centered, axis=-1, keepdims=True) + 1e-06)
    return centered * inverse, inverse


def block_kernel(
    n_data,
    n_tensor,
    clips,
    latent,
    noise,
    cot,
    text,
    panels,
    time_map,
    feats,
    row_factors,
    key_mask,
    up_bias,
    side,
    block_out,
    latent_grad,
    grad_panels,
    grad_time,
    grad_side,
    square_sum,
    weights,
    parts,
    slots,
    feats_all,
    modul_out,
    modul_in,
    modul,
    hidden_one,
    heads_one,
    probs_one,
    mixed_one,
    heads_two,
    text_heads,
    probs_two,
    mixed_two,
    shared,
    activated,
    slope,
    d_mlp,
    d_upper,
    d_heads,
    d_text,
    sums,
    near,
    out,
    far,
    own,
    inverses,
    small,
    small_all,
    totals,
    totals_all,
    norms,
    norms_all,
    splits,
    gather_send,
    gather_recv,
    reduce_send,
    reduce_recv,
    sum_sems,
    share_sems,
    feat_sems,
    modul_sems,
    modul_share_sems,
    small_sems,
    total_sems,
    norm_sems,
    norm_share_sems,
):
    dp, me = lax.axis_index("dp"), lax.axis_index("tensor")
    rows, width = latent.shape
    clip_rows = rows // clips
    own_rows = rows // n_tensor
    per_clip = n_tensor // clips
    head_width = width // HEADS
    local = width // n_tensor
    heads = local // head_width
    scale = head_width ** (-0.5)
    tlen = key_mask.shape[1]
    mate = me + 1 - 2 * lax.rem(me, 2)
    across = lax.rem(me + 2, n_tensor)
    beyond = lax.rem(mate + 2, n_tensor)
    place = (dp, me, mate, across, beyond, own_rows)
    data_peers = [lax.rem(dp + k, n_data) for k in range(1, n_data)]
    tensor_peers = [lax.rem(me + k, n_tensor) for k in range(1, n_tensor)]
    mine = pl.ds(pl.multiple_of(me * own_rows, 16), own_rows)

    barrier = pltpu.get_barrier_semaphore()
    for peer in data_peers:
        pl.semaphore_signal(barrier, inc=1, device_id=(peer, me), device_id_type=MESH)
    for peer in tensor_peers:
        pl.semaphore_signal(barrier, inc=1, device_id=(dp, peer), device_id_type=MESH)
    pl.semaphore_wait(barrier, n_data + n_tensor - 2)

    def send_all(source_of, target, sems, along):
        copies = []
        peers = data_peers if along == "dp" else tensor_peers
        for k, peer in enumerate(peers):
            copy = pltpu.make_async_remote_copy(
                src_ref=source_of(peer),
                dst_ref=target,
                send_sem=sems.at[0, k],
                recv_sem=sems.at[1, k],
                device_id=(peer, me) if along == "dp" else (dp, peer),
                device_id_type=MESH,
            )
            copy.start()
            copies.append(copy)
        return copies

    def wait_all(copies):
        for copy in copies:
            copy.wait()

    panel_rows = panels.shape[1]
    gather = Gather(n_data, panel_rows, dp, me, panels, weights, gather_send, gather_recv)
    reduce = Reduce(n_data, panel_rows, dp, me, parts, slots, grad_panels, reduce_send, reduce_recv)
    feats_all[dp] = feats[...]
    feat_copies = send_all(lambda peer: feats, feats_all.at[dp], feat_sems, "dp")
    gather.pump(2)
    for panel in range(4):
        weights[panel, pl.ds(pl.multiple_of(dp * panel_rows, 16), panel_rows), :] = panels[panel]

    n_feats = time_map.shape[1]
    feat_rows, n_freq = feats.shape
    modul_share = clips * 6 // n_tensor
    wait_all(feat_copies)
    pick = (
        lax.broadcasted_iota(jnp.int32, (n_freq, n_feats), 0)
        == lax.broadcasted_iota(jnp.int32, (n_freq, n_feats), 1) + n_feats * dp
    ).astype(FULL).astype(LOW)
    feats_flat = feats_all[...].reshape(n_data * feat_rows, n_freq)
    feats_mine = dot(feats_flat, pick, 1, 0).astype(LOW)
    my_clip = lax.div(me, per_clip)
    first = modul_share * lax.rem(me, per_clip)
    rows_of_clip = (
        lax.broadcasted_iota(jnp.int32, (n_data, n_data * feat_rows), 1)
        == feat_rows * lax.broadcasted_iota(jnp.int32, (n_data, n_data * feat_rows), 0) + my_clip
    ).astype(FULL).astype(LOW)
    feats_clip = dot(rows_of_clip, feats_mine, 1, 0).astype(LOW)
    for k in range(modul_share):
        partial = dot(feats_clip, time_map[first + k].astype(LOW), 1, 0)
        for peer in range(n_data):
            modul_out[peer, k : k + 1, :] = partial[peer : peer + 1]
    for peer in range(n_data):
        modul_out[peer, modul_share:8, :] = jnp.zeros((8 - modul_share, width), FULL)
    modul_in[dp] = modul_out[dp]
    modul_copies = send_all(lambda peer: modul_out.at[peer], modul_in.at[dp], modul_sems, "dp")
    gather.pump(1)
    lane = lax.broadcasted_iota(jnp.int32, (1, local), 1)
    head_masks = [
        ((lane >= h * head_width) & (lane < (h + 1) * head_width)).astype(FULL) for h in range(heads)
    ]
    wait_all(modul_copies)
    total = modul_in[0]
    for peer in range(1, n_data):
        total = total + modul_in[peer]
    chosen = jnp.where(lax.rem(me, per_clip) == 0, side[3 : 3 + modul_share, :], side[3 + modul_share : 9, :])
    modul[me] = jnp.concatenate(
        [total[0:modul_share] + chosen, jnp.zeros((8 - modul_share, width), FULL)], axis=0
    )
    modul_copies = send_all(lambda peer: modul.at[me], modul.at[me], modul_share_sems, "tensor")
    gather.pump(1)
    wait_all(modul_copies)

    def modul_row(clip, j):
        return modul[clip * per_clip + j // modul_share, pl.ds(j % modul_share, 1), :]

    def start_of(block, size):
        factors = row_factors[block, :]
        return factors[:, 0:1] * latent[block, :].astype(FULL) + factors[:, 1:2] * noise[block, :].astype(FULL)

    step_rows = 32

    def first_norm(clip, step, carry):
        block = pl.ds(pl.multiple_of(clip * clip_rows + step * step_rows, step_rows), step_rows)
        normed, _ = row_norm(start_of(block, step_rows))
        hidden_one[block, :] = (normed * (1.0 + modul_row(clip, 1)) + modul_row(clip, 0)).astype(LOW)
        return carry

    for clip in range(clips):
        lax.fori_loop(0, clip_rows // step_rows, functools.partial(first_norm, clip), 0)
        gather.pump(1)
    start_mine = start_of(mine, own_rows)
    normed, inverse = row_norm(start_mine)
    own[0], own[1] = start_mine, normed
    inverses[0] = jnp.broadcast_to(inverse, (own_rows, 128))
    live_mine = row_factors[mine, 2:3]
    for clip in range(clips):
        block = pl.ds(clip * clip_rows, clip_rows)
        value = (
            modul_row(clip, 5) * row_factors[block, 2:3] * cot[block, :].astype(FULL)
        )
        d_mlp[block, :] = value.astype(LOW)
    gather.finish(0)

    spread = 3 * local - 2 * 128 if False else None
    self_cols = -(-3 * local // 128) * 128
    out_cols = 3 * local // 128 * 128
    out_pad = 3 * local - out_cols
    text_cols = local // 128 * 128
    text_pad = local - text_cols
    query_cols = -(-local // 128) * 128

    def split_heads(values, offsets, target, block):
        for k, offset in enumerate(offsets):
            target[k, block, :] = values[:, offset : offset + local].astype(LOW)

    def stacked(values):
        return jnp.concatenate([(values.astype(FULL) * mask).astype(LOW) for mask in head_masks], axis=0)

    def unstacked(values, size):
        total = values[0:size] * head_masks[0]
        for h in range(1, heads):
            total = total + values[h * size : (h + 1) * size] * head_masks[h]
        return total

    def attend(query, keys, values, allowed):
        scores = jnp.where(allowed, dot(stacked(query), keys, 1, 1) * scale, -1e30)
        expo = jnp.exp(scores - jnp.max(scores, axis=-1, keepdims=True))
        probs = expo / jnp.sum(expo, axis=-1, keepdims=True)
        return probs, unstacked(dot(probs.astype(LOW), values, 1, 0), clip_rows)

    def pad_left(values):
        return jnp.concatenate([jnp.zeros((values.shape[0], out_pad), FULL), values], axis=1).astype(LOW)

    def sum_of(index, buffer):
        return Sum(place, sums.at[buffer], near.at[index], out.at[index], far.at[index], sum_sems.at[index])

    def columns(body, total):
        for begin in range(0, total, TILE):
            body(begin, min(TILE, total - begin))

    def product_nt(left, panel, begin, end, buffer):
        def tile(at, size):
            sums[buffer, :, at : at + size] = dot(left, weights[panel, at : at + size, begin:end], 1, 1)

        columns(tile, width)

    for block_at in range(0, rows, 128):
        block = pl.ds(block_at, 128)
        split_heads(
            dot(hidden_one[block, :], weights[0, :, 0:self_cols], 1, 0), (0, local, 2 * local), heads_one, block
        )
    gather.pump(1)
    size = heads * clip_rows
    frame_row = lax.broadcasted_iota(jnp.int32, (size, clip_rows), 0)
    frame_col = lax.broadcasted_iota(jnp.int32, (size, clip_rows), 1)
    frame_bits = FRAMES.bit_length() - 1
    same_sequence = ((frame_row & (clip_rows - 1)) >> frame_bits) == (frame_col >> frame_bits)
    for clip in range(clips):
        block = pl.ds(clip * clip_rows, clip_rows)
        probs, mixed = attend(heads_one[0, block, :], heads_one[1, block, :], heads_one[2, block, :], same_sequence)
        probs_one[clip] = probs
        mixed_one[block, :] = pad_left(mixed)
        gather.pump(1)
    product_nt(mixed_one[...], 0, out_cols, width, 0)
    self_sum = sum_of(0, 0)
    self_sum.start()
    gather.pump(1)
    self_sum.middle()
    gather.pump(1)
    clip_mine = lax.div(me, per_clip)

    def modul_mine(j):
        return modul[clip_mine * per_clip + j // modul_share, pl.ds(j % modul_share, 1), :]

    attended = self_sum.end() + side[0:1, :]
    own[2] = attended
    middle = own[0] + modul_mine(2) * attended
    own[0] = middle
    shared[0, mine, :] = middle.astype(LOW)
    share = Share(place, shared.at[0], share_sems.at[0])
    share.start()
    gather.pump(1)
    share.middle()
    gather.finish(1)

    for block_at in range(0, clips * tlen, 128):
        block = pl.ds(block_at, 128)
        split_heads(
            dot(text[block, :], weights[1, :, text_cols : text_cols + 5 * 128], 1, 0),
            (text_pad, text_pad + local),
            text_heads,
            block,
        )
    share.end()
    gather.pump(1)
    heads_two[...] = dot(shared[0], weights[1, :, 0:query_cols], 1, 0)[:, 0:local].astype(LOW)
    for clip in range(clips):
        block = pl.ds(clip * clip_rows, clip_rows)
        words = pl.ds(clip * tlen, tlen)
        probs, mixed = attend(
            heads_two[block, :], text_heads[0, words, :], text_heads[1, words, :], key_mask[clip : clip + 1, :] > 0.5
        )
        probs_two[clip] = probs
        mixed_two[block, :] = pad_left(mixed)
        gather.pump(1)
    product_nt(mixed_two[...], 1, out_cols, width, 0)
    cross_sum = sum_of(1, 0)
    cross_sum.start()
    gather.pump(1)
    cross_sum.middle()
    gather.pump(1)
    after = own[0] + cross_sum.end() + side[1:2, :]
    own[0] = after
    normed, inverse = row_norm(after)
    own[3] = normed
    inverses[1] = jnp.broadcast_to(inverse, (own_rows, 128))
    shared[1, mine, :] = (normed * (1.0 + modul_mine(4)) + modul_mine(3)).astype(LOW)
    share = Share(place, shared.at[1], share_sems.at[1])
    share.start()
    gather.pump(1)
    share.middle()
    gather.finish(2)
    share.end()

    def up(at, size):
        cols = slice(at, at + size)
        upper = dot(shared[1], weights[2, :, cols], 1, 0) + up_bias[:, cols]
        tangent = jnp.tanh(0.7978845608028654 * (upper + 0.044715 * upper * upper * upper))
        inner = 0.7978845608028654 * (1.0 + 3.0 * 0.044715 * upper * upper)
        activated[:, cols] = (0.5 * upper * (1.0 + tangent)).astype(LOW)
        slope[:, cols] = 0.5 * (1.0 + tangent) + 0.5 * upper * (1.0 - tangent * tangent) * inner
        gather.pump(1)

    columns(up, width)

    def grad_tile(panel, left, right, at, size):
        cols = slice(at, at + size)
        parts[panel, :, cols] = dot(left, right[:, cols], 0, 0).astype(LOW)

    def grad_panel(panel, left, right):
        columns(functools.partial(grad_tile, panel, left, right), width)

    grad_panel(3, d_mlp[...], activated)
    gather.finish(3)
    reduce.add_panel(3)
    reduce.pump(2)

    small[...] = jnp.zeros_like(small)

    def up_slope(at, size):
        cols = slice(at, at + size)
        value = (dot(d_mlp[...], weights[3, :, cols], 1, 0) * slope[:, cols]).astype(LOW)
        d_upper[:, cols] = value
        small[9:10, cols] = jnp.sum(value.astype(FULL), axis=0, keepdims=True)

    columns(up_slope, width)
    grad_panel(2, shared[1], d_upper)
    reduce.add_panel(2)
    product_nt(d_upper[...], 2, 0, width, 0)
    hidden_sum = sum_of(2, 0)
    hidden_sum.start()
    reduce.pump(1)
    hidden_sum.middle()
    product_nt(activated[...], 3, 0, width, 1)
    mlp_sum = sum_of(3, 1)
    mlp_sum.start()
    reduce.pump(1)

    def norm_back(grad_out, normed, inverse):
        first_mean = jnp.mean(grad_out, axis=-1, keepdims=True)
        second_mean = jnp.mean(grad_out * normed, axis=-1, keepdims=True)
        return inverse * (grad_out - first_mean - normed * second_mean)

    def row_sum(values):
        return jnp.sum(values, axis=0, keepdims=True)

    cot_mine = cot[mine, :].astype(FULL)
    d_hidden = hidden_sum.end()
    normed = own[3]
    small[3:4, :] = row_sum(d_hidden)
    small[4:5, :] = row_sum(d_hidden * normed)
    grad_three = live_mine * cot_mine + norm_back(
        d_hidden * (1.0 + modul_mine(4)), normed, inverses[1, :, 0:1]
    )
    own[3] = grad_three
    small[7:8, :] = row_sum(grad_three)
    shared[2, mine, :] = grad_three.astype(LOW)
    share = Share(place, shared.at[2], share_sems.at[2])
    share.start()
    mlp_sum.middle()
    reduce.pump(1)
    share.middle()
    reduce.pump(1)
    mlp_out = mlp_sum.end() + side[2:3, :]
    grad_four = live_mine * cot_mine
    small[5:6, :] = row_sum(grad_four * mlp_out)
    small[8:9, :] = row_sum(modul_mine(5) * grad_four)
    block_out[mine, :] = (live_mine * (own[0] + modul_mine(5) * mlp_out)).astype(LOW)
    share.end()
    out_share = Share(place, block_out, share_sems.at[3])
    out_share.start()

    def attend_back(query, keys, values, probs, d_mixed):
        stacked_grad = stacked(d_mixed)
        stacked_query = stacked(query)
        d_probs = dot(stacked_grad, values, 1, 1)
        d_values = dot(probs.astype(LOW), stacked_grad, 0, 0).astype(LOW)
        d_scores = (probs * (d_probs - jnp.sum(probs * d_probs, axis=-1, keepdims=True))).astype(LOW)
        d_query = (unstacked(dot(d_scores, keys, 1, 0), clip_rows) * scale).astype(LOW)
        d_keys = (dot(d_scores, stacked_query, 0, 0) * scale).astype(LOW)
        return d_query, d_keys, d_values

    def spread_out(pieces, offset, total):
        have = sum(piece.shape[1] for piece in pieces)
        height = pieces[0].shape[0]
        ends = [(offset, pieces[:0]), (total - offset - have, None)]
        full = list(pieces)
        if ends[0][0]:
            full.insert(0, jnp.zeros((height, offset), LOW))
        if ends[1][0]:
            full.append(jnp.zeros((height, ends[1][0]), LOW))
        return jnp.concatenate(full, axis=1)

    d_mixed = dot(shared[2], weights[1, :, out_cols:width], 1, 0)[:, out_pad:].astype(LOW)
    reduce.pump(1)
    for clip in range(clips):
        block = pl.ds(clip * clip_rows, clip_rows)
        words = pl.ds(clip * tlen, tlen)
        d_query, d_keys, d_values = attend_back(
            heads_two[block, :],
            text_heads[0, words, :],
            text_heads[1, words, :],
            probs_two[clip],
            d_mixed[clip * clip_rows : (clip + 1) * clip_rows],
        )
        d_heads[block, 0:query_cols] = spread_out([d_query], 0, query_cols)
        d_text[words, :] = spread_out([d_keys, d_values], text_pad, 5 * 128)
        reduce.pump(1)
    product_nt(d_heads[:, 0:query_cols], 1, 0, query_cols, 0)
    query_sum = sum_of(4, 0)
    query_sum.start()
    reduce.pump(1)
    out_share.middle()
    query_sum.middle()
    query_part = dot(shared[0], d_heads[:, 0:query_cols], 0, 0)
    text_part = dot(text[...], d_text[...], 0, 0)
    out_part = dot(shared[2], mixed_two[...], 0, 0)
    parts[1, :, 0:text_cols] = query_part[:, 0:text_cols].astype(LOW)
    parts[1, :, text_cols:query_cols] = (
        query_part[:, text_cols:query_cols] + text_part[:, 0 : query_cols - text_cols]
    ).astype(LOW)
    parts[1, :, query_cols:out_cols] = text_part[:, query_cols - text_cols : out_cols - text_cols].astype(LOW)
    parts[1, :, out_cols:self_cols] = (
        text_part[:, out_cols - text_cols : self_cols - text_cols] + out_part[:, 0 : self_cols - out_cols]
    ).astype(LOW)
    parts[1, :, self_cols:width] = out_part[:, self_cols - out_cols :].astype(LOW)
    reduce.add_panel(1)
    reduce.pump(1)
    grad_two = own[3] + query_sum.end()
    own[3] = grad_two
    small[2:3, :] = row_sum(grad_two * own[2])
    d_attended = modul_mine(2) * grad_two
    small[6:7, :] = row_sum(d_attended)
    shared[3, mine, :] = d_attended.astype(LOW)
    share = Share(place, shared.at[3], share_sems.at[4])
    share.start()
    out_share.end()
    reduce.pump(1)
    share.middle()
    reduce.pump(1)
    share.end()

    d_mixed = dot(shared[3], weights[0, :, out_cols:width], 1, 0)[:, out_pad:].astype(LOW)
    for clip in range(clips):
        block = pl.ds(clip * clip_rows, clip_rows)
        grads = attend_back(
            heads_one[0, block, :],
            heads_one[1, block, :],
            heads_one[2, block, :],
            probs_one[clip],
            d_mixed[clip * clip_rows : (clip + 1) * clip_rows],
        )
        d_heads[block, :] = spread_out(list(grads), 0, self_cols)
        reduce.pump(1)
    product_nt(d_heads[...], 0, 0, self_cols, 1)
    first_sum = sum_of(5, 1)
    first_sum.start()
    reduce.pump(1)
    first_sum.middle()
    for at in range(0, width, TILE):
        row_part = dot(hidden_one[:, at : at + TILE], d_heads[...], 0, 0)
        out_part = dot(shared[3, :, at : at + TILE], mixed_one[...], 0, 0)
        block = slice(at, at + TILE)
        parts[0, block, 0:out_cols] = row_part[:, 0:out_cols].astype(LOW)
        parts[0, block, out_cols:self_cols] = (
            row_part[:, out_cols:self_cols] + out_part[:, 0 : self_cols - out_cols]
        ).astype(LOW)
        parts[0, block, self_cols:width] = out_part[:, self_cols - out_cols :].astype(LOW)
    reduce.add_panel(0)
    reduce.pump(1)
    d_hidden = first_sum.end()
    normed = own[1]
    small[0:1, :] = row_sum(d_hidden)
    small[1:2, :] = row_sum(d_hidden * normed)
    grad_one = own[3] + norm_back(d_hidden * (1.0 + modul_mine(1)), normed, inverses[0, :, 0:1])
    latent_grad[mine, :] = row_factors[mine, 0:1] * grad_one
    small_all[me] = small[...]
    small_copies = send_all(lambda peer: small, small_all.at[me], small_sems, "tensor")
    share = Share(place, latent_grad, share_sems.at[5])
    share.start()
    reduce.pump(1)

    wait_all(small_copies)
    for clip in range(clips):
        value = small_all[clip * per_clip, 0:6, :]
        for k in range(1, per_clip):
            value = value + small_all[clip * per_clip + k, 0:6, :]
        totals[6 * clip : 6 * clip + 6, :] = value
    value = small_all[0, 6:9, :]
    for k in range(1, n_tensor):
        value = value + small_all[k, 6:9, :]
    totals[6 * clips : 6 * clips + 3, :] = value
    totals[6 * clips + 3 : 6 * clips + 4, :] = small[9:10, :]
    totals_all[dp] = totals[...]
    total_copies = send_all(lambda peer: totals, totals_all.at[dp], total_sems, "dp")
    reduce.pump(1)
    share.middle()
    reduce.pump(2)
    share.end()
    wait_all(total_copies)
    sides = totals_all[0]
    for peer in range(1, n_data):
        sides = sides + totals_all[peer]
    grad_side[0:3, :] = sides[6 * clips : 6 * clips + 3]
    value = sides[0:6]
    for clip in range(1, clips):
        value = value + sides[6 * clip : 6 * clip + 6]
    grad_side[3:9, :] = value
    grad_side[9:10, :] = sides[6 * clips + 3 : 6 * clips + 4]
    grad_side[10:16, :] = jnp.zeros((6, width), FULL)
    reduce.pump(1)
    total_rows = n_data * totals.shape[0]
    flat = totals_all[...].reshape(total_rows, width)
    for k in range(3):
        piece = flat.astype(LOW)
        splits[pl.ds(k * total_rows, total_rows), :] = piece
        flat = flat - piece.astype(FULL)
    feat_index = lax.broadcasted_iota(jnp.int32, (total_rows, n_data * feat_rows), 1)
    total_index = lax.broadcasted_iota(jnp.int32, (total_rows, n_data * feat_rows), 0)
    feat_clip, total_row = feat_index & (feat_rows - 1), total_index & (totals.shape[0] - 1)
    feat_bits, total_bits = feat_rows.bit_length() - 1, totals.shape[0].bit_length() - 1
    same_data = ((feat_index >> feat_bits) == (total_index >> total_bits)) & (feat_clip < clips)
    squares = jnp.zeros((1, width), FULL)
    for j in range(6):
        spot = (same_data & (total_row == 6 * feat_clip + j)).astype(FULL).astype(LOW)
        lifted = dot(spot, feats_mine, 1, 0).astype(LOW)
        value = dot(jnp.concatenate([lifted] * 3, axis=0), splits[...], 0, 0)
        grad_time[j] = value
        squares = squares + row_sum(value * value)
        if j % 2 == 1:
            reduce.pump(1)
    squares = squares * (1.0 / n_tensor)
    value = grad_side[9:10, :]
    squares = squares + value * value * (1.0 / n_data)
    value = grad_side[0:9, :]
    squares = squares + row_sum(value * value) * (1.0 / (n_data * n_tensor))
    reduce.complete()
    for panel in range(4):
        value = grad_panels[panel]
        squares = squares + row_sum(value * value)
    mine_sum = jnp.broadcast_to(jnp.sum(squares, axis=1, keepdims=True), (8, 128))
    norms[0] = mine_sum
    norms_all[0, dp] = mine_sum
    norm_copies = send_all(lambda peer: norms.at[0], norms_all.at[0, dp], norm_sems, "dp")
    gather.drain()
    reduce.drain()
    wait_all(norm_copies)
    value = norms_all[0, 0]
    for peer in range(1, n_data):
        value = value + norms_all[0, peer]
    norms[1] = value
    norms_all[1, me] = value
    norm_copies = send_all(lambda peer: norms.at[1], norms_all.at[1, me], norm_share_sems, "tensor")
    wait_all(norm_copies)
    value = norms_all[1, 0]
    for peer in range(1, n_tensor):
        value = value + norms_all[1, peer]
    square_sum[...] = value


def fits(n_data, n_tensor, rows, clips, panel_rows, units):
    clip_rows = rows // clips
    return (
        n_tensor == 4
        and clips == 2
        and n_data % 2 == 0
        and n_data <= 8
        and panel_rows % 16 == 0
        and clip_rows == 128
        and units == D
    )


def run_block(latent, noise, cot, text, panels, time_w, feats, row_factors, key_mask, up_bias, side_vec):
    n_data, n_tensor = lax.axis_size("dp"), lax.axis_size("tensor")
    clips, tlen = key_mask.shape
    rows, width = latent.shape
    own_rows = rows // n_tensor
    local = width // n_tensor
    heads = HEADS // n_tensor
    clip_rows = rows // clips
    panel_rows, units = panels.shape[1:]
    wide = -(-local // 128) * 128
    self_cols = -(-3 * local // 128) * 128
    steps = n_data - 1
    lead = -(-panel_rows // 32) * 16
    feat_rows = feats.shape[0]
    dma = pltpu.SemaphoreType.DMA
    scratch = [
        pltpu.VMEM((4, width, units), LOW),
        pltpu.VMEM((4, width, units), LOW),
        pltpu.VMEM((2, 4, steps, lead, units), LOW),
        pltpu.VMEM((n_data, feat_rows, TFREQ), LOW),
        pltpu.VMEM((n_data, 8, width), FULL),
        pltpu.VMEM((n_data, 8, width), FULL),
        pltpu.VMEM((n_tensor, 8, width), FULL),
        pltpu.VMEM((rows, width), LOW),
        pltpu.VMEM((3, rows, local), LOW),
        pltpu.VMEM((clips, heads * clip_rows, clip_rows), FULL),
        pltpu.VMEM((rows, wide), LOW),
        pltpu.VMEM((rows, local), LOW),
        pltpu.VMEM((2, clips * tlen, local), LOW),
        pltpu.VMEM((clips, heads * clip_rows, tlen), FULL),
        pltpu.VMEM((rows, wide), LOW),
        pltpu.VMEM((4, rows, width), LOW),
        pltpu.VMEM((rows, units), LOW),
        pltpu.VMEM((rows, units), FULL),
        pltpu.VMEM((rows, width), LOW),
        pltpu.VMEM((rows, units), LOW),
        pltpu.VMEM((rows, self_cols), LOW),
        pltpu.VMEM((clips * tlen, 5 * 128), LOW),
        pltpu.VMEM((2, rows, width), FULL),
        pltpu.VMEM((6, 2, own_rows, width), FULL),
        pltpu.VMEM((6, own_rows, width), LOW),
        pltpu.VMEM((6, own_rows, width), LOW),
        pltpu.VMEM((4, own_rows, width), FULL),
        pltpu.VMEM((2, own_rows, 128), FULL),
        pltpu.VMEM((16, width), FULL),
        pltpu.VMEM((n_tensor, 16, width), FULL),
        pltpu.VMEM((16, width), FULL),
        pltpu.VMEM((n_data, 16, width), FULL),
        pltpu.VMEM((2, 8, 128), FULL),
        pltpu.VMEM((2, max(n_data, n_tensor), 8, 128), FULL),
        pltpu.VMEM((3 * n_data * 16, width), LOW),
        dma((2, 4, steps)),
        dma((2, 4, steps)),
        dma((2, 4, steps)),
        dma((2, 4, steps)),
        dma((6, 6)),
        dma((6, 6)),
        dma((2, steps)),
        dma((2, steps)),
        dma((2, n_tensor - 1)),
        dma((2, n_tensor - 1)),
        dma((2, steps)),
        dma((2, steps)),
        dma((2, n_tensor - 1)),
    ]
    shape = jax.ShapeDtypeStruct
    vmem = pl.BlockSpec(memory_space=pltpu.VMEM)
    return pl.pallas_call(
        functools.partial(block_kernel, n_data, n_tensor, clips),
        out_shape=(
            shape((rows, width), LOW),
            shape((rows, width), FULL),
            shape((4, panel_rows, units), FULL),
            shape(time_w.shape, FULL),
            shape((16, width), FULL),
            shape((8, 128), FULL),
        ),
        in_specs=[vmem] * 11,
        out_specs=(vmem,) * 6,
        scratch_shapes=scratch,
        compiler_params=pltpu.CompilerParams(
            collective_id=0, has_side_effects=True, vmem_limit_bytes=63 * 2**20
        ),
    )(latent, noise, cot, text, panels, time_w, feats, row_factors, key_mask, up_bias, side_vec)


def shards(
    latent,
    noise,
    text,
    tsteps,
    clip_count,
    text_len,
    cotangent,
    attn_w,
    attn_m,
    attn_v,
    mlp_w,
    mlp_m,
    mlp_v,
    up_bias,
    up_m,
    up_v,
    side_vec,
    side_m,
    side_v,
    time_w,
    time_m,
    time_v,
):
    n_tensor = lax.axis_size("tensor")
    n_data = lax.axis_size("dp")
    clips, tlen, width = text.shape
    rows = latent.shape[0]
    panel_rows, local = attn_w.shape[1:]
    if not fits(n_data, n_tensor, rows, clips, panel_rows, mlp_w.shape[2]):
        return plain_shards(
            latent, noise, text, tsteps, clip_count, text_len, cotangent, attn_w, attn_m, attn_v, mlp_w, mlp_m,
            mlp_v, up_bias, up_m, up_v, side_vec, side_m, side_v, time_w, time_m, time_v,
        )
    four = attn_w.astype(LOW).reshape(2, 4, panel_rows, local).transpose(0, 2, 1, 3)
    panels = jnp.concatenate([four.reshape(2, panel_rows, 4 * local), mlp_w.astype(LOW)], axis=0)
    abar = pick_rows(alpha_bar(), tsteps)
    live = (jnp.arange(clips) < clip_count[0]).astype(FULL)
    feats = jax.nn.silu(time_features(tsteps)).astype(LOW)
    feats = jnp.concatenate([feats, jnp.zeros((16 - clips, TFREQ), LOW)], axis=0)
    factors = jnp.stack([jnp.sqrt(abar), jnp.sqrt(1.0 - abar), live], axis=1)
    row_factors = jnp.pad(jnp.repeat(factors, rows // clips, axis=0), ((0, 0), (0, 125)))
    key_mask = (jnp.arange(tlen)[None, :] < text_len[:, None]).astype(FULL)
    block_out, latent_grad, grad_panels, grad_time, grad_side, squares = run_block(
        latent,
        noise,
        cotangent,
        text.reshape(clips * tlen, width),
        panels,
        time_w,
        feats,
        row_factors,
        key_mask,
        up_bias[None],
        side_vec,
    )
    grad_norm = jnp.sqrt(squares[0, 0])
    factor = jnp.minimum(1.0, CLIP_NORM / (grad_norm + 1e-06))
    attn_grad = grad_panels[0:2].reshape(2, panel_rows, 4, local).transpose(0, 2, 1, 3)
    attn_grad = attn_grad.reshape(attn_w.shape)
    attn_new, attn_m_new, attn_v_new = adamw(attn_w, attn_m, attn_v, attn_grad, factor, RATE_MATRIX)
    mlp_new, mlp_m_new, mlp_v_new = adamw(mlp_w, mlp_m, mlp_v, grad_panels[2:4], factor, RATE_MATRIX)
    up_new, up_m_new, up_v_new = adamw(up_bias, up_m, up_v, grad_side[9], factor, RATE_VECTOR)
    side_new, side_m_new, side_v_new = adamw(
        side_vec, side_m, side_v, grad_side[0:9], factor, RATE_VECTOR
    )
    time_new, time_m_new, time_v_new = adamw(time_w, time_m, time_v, grad_time, factor, RATE_TIME)
    return (
        block_out,
        latent_grad,
        grad_norm,
        attn_new,
        attn_m_new,
        attn_v_new,
        mlp_new,
        mlp_m_new,
        mlp_v_new,
        up_new,
        up_m_new,
        up_v_new,
        side_new,
        side_m_new,
        side_v_new,
        time_new,
        time_m_new,
        time_v_new,
    )


def solution(mesh):
    placed = (
        P("dp", None),
        P("dp", None),
        P("dp", None, None),
        P("dp"),
        P("dp"),
        P("dp"),
        P("dp", None),
        P(None, "dp", "tensor"),
        P(None, "dp", "tensor"),
        P(None, "dp", "tensor"),
        P(None, "dp", "tensor"),
        P(None, "dp", "tensor"),
        P(None, "dp", "tensor"),
        P("tensor"),
        P("tensor"),
        P("tensor"),
        P(),
        P(),
        P(),
        P(None, "dp", None),
        P(None, "dp", None),
        P(None, "dp", None),
    )
    return jax.shard_map(
        shards,
        mesh=mesh,
        in_specs=placed,
        out_specs=(
            P("dp", None),
            P("dp", None),
            P(),
            P(None, "dp", "tensor"),
            P(None, "dp", "tensor"),
            P(None, "dp", "tensor"),
            P(None, "dp", "tensor"),
            P(None, "dp", "tensor"),
            P(None, "dp", "tensor"),
            P("tensor"),
            P("tensor"),
            P("tensor"),
            P(),
            P(),
            P(),
            P(None, "dp", None),
            P(None, "dp", None),
            P(None, "dp", None),
        ),
        check_vma=False,
    )
```

```python
import functools
import math

import jax
import jax.numpy as jnp
from jax import lax
from jax.experimental import pallas as pl
from jax.experimental.pallas import tpu as pltpu
from jax.sharding import PartitionSpec as P

D = 1152
HEADS = 16
TFREQ = 256
FRAMES = 16
OPT_STEP = 10


HIGHEST = lax.Precision.HIGHEST
BETA_ONE = 0.9
BETA_TWO = 0.999
EPSILON = 1e-08
DECAY_RATE = 0.01
CLIP_NORM = 1.0
RATE_MATRIX = 0.02
RATE_TIME = 0.05
RATE_VECTOR = 0.3


def alpha_bar():
    steps = jnp.arange(1000).astype(jnp.float32)
    betas = 0.0001 + (0.02 - 0.0001) * steps / 999.0
    return jnp.exp(jnp.cumsum(jnp.log(1.0 - betas)))


def pick_rows(table, indices):
    spots = jnp.arange(table.shape[0])
    return jnp.sum(jnp.where(spots[None, :] == indices[:, None], table[None, :], 0.0), axis=1)


def time_features(indices):
    half = TFREQ // 2
    freqs = jnp.exp(-math.log(10000.0) * jnp.arange(half).astype(jnp.float32) / half)
    angles = indices.astype(jnp.float32)[:, None] * freqs[None, :]
    return jnp.concatenate([jnp.cos(angles), jnp.sin(angles)], axis=1)


def layer_parts(values):
    centered = values - jnp.mean(values, axis=-1, keepdims=True)
    inverse = lax.rsqrt(jnp.mean(centered * centered, axis=-1, keepdims=True) + 1e-06)
    return (centered * inverse, inverse)


def norm_back(grad_out, normed, inverse):
    first_mean = jnp.mean(grad_out, axis=-1, keepdims=True)
    second_mean = jnp.mean(grad_out * normed, axis=-1, keepdims=True)
    return inverse * (grad_out - first_mean - normed * second_mean)


def gelu_tanh(upper):
    return (
        0.5
        * upper
        * (1.0 + jnp.tanh(0.7978845608028654 * (upper + 0.044715 * upper * upper * upper)))
    )


def gelu_slope(upper):
    tangent = jnp.tanh(0.7978845608028654 * (upper + 0.044715 * upper * upper * upper))
    inner = 0.7978845608028654 * (1.0 + 3.0 * 0.044715 * upper * upper)
    return 0.5 * (1.0 + tangent) + 0.5 * upper * (1.0 - tangent * tangent) * inner


def log_total(scores):
    peak = jnp.max(scores, axis=-1, keepdims=True)
    return peak + jnp.log(jnp.sum(jnp.exp(scores - peak), axis=-1, keepdims=True))


def softmax_back(probs, grad_probs):
    return probs * (grad_probs - jnp.sum(probs * grad_probs, axis=-1, keepdims=True))


def adamw(weight, first, second, grad, factor, rate):
    clipped = grad * factor
    first = BETA_ONE * first + (1.0 - BETA_ONE) * clipped
    second = BETA_TWO * second + (1.0 - BETA_TWO) * clipped * clipped
    first_hat = first / (1.0 - BETA_ONE**OPT_STEP)
    second_hat = second / (1.0 - BETA_TWO**OPT_STEP)
    weight = weight - rate * (first_hat / (jnp.sqrt(second_hat) + EPSILON) + DECAY_RATE * weight)
    return (weight, first, second)


def row_layout():
    return (1, jnp.int32(0))


def row_total(term_fn, total_rows):
    return lax.psum(term_fn(0, total_rows), "tensor")


def clip_totals(modul_terms, bias_terms):
    return (modul_terms, bias_terms)


def plain_shards(
    latent,
    noise,
    text,
    tsteps,
    clip_count,
    text_len,
    cotangent,
    attn_w,
    attn_m,
    attn_v,
    mlp_w,
    mlp_m,
    mlp_v,
    up_bias,
    up_m,
    up_v,
    side_vec,
    side_m,
    side_v,
    time_w,
    time_m,
    time_v,
):
    low_type = jnp.bfloat16
    full_type = jnp.float32
    n_tensor = lax.axis_size("tensor")
    n_data = lax.axis_size("dp")
    clips, tlen, width = text.shape
    row_count = latent.shape[0]
    seq_rows = row_count // clips
    seqs = row_count // FRAMES
    head_width = D // HEADS
    scale = head_width ** (-0.5)
    w_attn, w_mlp, w_time = (
        lax.all_gather(attn_w.astype(low_type), "dp", axis=1, tiled=True),
        lax.all_gather(mlp_w.astype(low_type), "dp", axis=1, tiled=True),
        lax.all_gather(time_w.astype(low_type), "dp", axis=1, tiled=True),
    )
    device_local = w_attn.shape[2]
    heads_here = device_local // head_width
    pieces, part = row_layout()
    share = row_count // pieces
    row_ids = jnp.arange(share)
    select = (row_ids[:, None] // seq_rows == jnp.arange(clips)[None, :]).astype(full_type)

    def per_row(values):
        return jnp.tensordot(select, values, axes=1, precision=HIGHEST)

    def per_clip(values):
        return jnp.tensordot(select.T, values, axes=1, precision=HIGHEST)

    abar = pick_rows(alpha_bar(), tsteps)
    keep_root = jnp.sqrt(abar)[:, None, None]
    noise_root = jnp.sqrt(1.0 - abar)[:, None, None]
    start = keep_root * latent.astype(full_type).reshape(
        clips, seq_rows, width
    ) + noise_root * noise.astype(full_type).reshape(clips, seq_rows, width)
    feats = jax.nn.silu(time_features(tsteps)).astype(low_type)
    modul = side_vec[3:][None] + jnp.einsum(
        "cf,jfd->cjd", feats, w_time, preferred_element_type=full_type
    )
    live_clip = (jnp.arange(clips) < clip_count[0]).astype(full_type)
    live = live_clip[:, None, None]
    mod_rows = per_row(modul)
    live_rows = per_row(live_clip)[:, None]
    root_rows = per_row(jnp.sqrt(abar))[:, None]
    normed_one, inverse_one = layer_parts(start)
    hidden_one = (
        (normed_one * (1.0 + modul[:, 1:2]) + modul[:, 0:1])
        .astype(low_type)
        .reshape(row_count, width)
    )
    projected = jnp.einsum(
        "rd,kde->kre", hidden_one, w_attn[0:3], preferred_element_type=full_type
    ).astype(low_type)
    shaped = projected.reshape(3, seqs, FRAMES, heads_here, head_width)
    self_scores = (
        jnp.einsum("sfhd,sghd->shfg", shaped[0], shaped[1], preferred_element_type=full_type)
        * scale
    )
    self_log = log_total(self_scores)
    self_probs = jnp.exp(self_scores - self_log).astype(low_type)
    mixed_one = (
        jnp.einsum("shfg,sghd->sfhd", self_probs, shaped[2], preferred_element_type=full_type)
        .astype(low_type)
        .reshape(row_count, device_local)
    )

    def self_out(begin, count):
        return jnp.einsum("re,oe->ro", mixed_one, w_attn[3], preferred_element_type=full_type)

    attended = row_total(self_out, row_count) + side_vec[0]
    start_rows = start.reshape(row_count, width)
    middle = start_rows + mod_rows[:, 2] * attended
    query_in = middle.astype(low_type)
    cross_query = jnp.dot(query_in, w_attn[4], preferred_element_type=full_type).astype(low_type)
    text_proj = jnp.einsum(
        "cld,kde->kcle", text, w_attn[5:7], preferred_element_type=full_type
    ).astype(low_type)
    query_heads = cross_query.reshape(clips, seq_rows, heads_here, head_width)
    text_heads = text_proj.reshape(2, clips, tlen, heads_here, head_width)
    allowed = (jnp.arange(tlen)[None, :] < text_len[:, None])[:, None, None, :]
    cross_scores = jnp.where(
        allowed,
        jnp.einsum("cqhd,ckhd->chqk", query_heads, text_heads[0], preferred_element_type=full_type)
        * scale,
        -1e30,
    )
    cross_log = log_total(cross_scores)
    cross_probs = jnp.exp(cross_scores - cross_log).astype(low_type)
    mixed_two = (
        jnp.einsum("chqk,ckhd->cqhd", cross_probs, text_heads[1], preferred_element_type=full_type)
        .astype(low_type)
        .reshape(row_count, device_local)
    )

    def cross_out(begin, count):
        return jnp.einsum("re,oe->ro", mixed_two, w_attn[7], preferred_element_type=full_type)

    crossed = row_total(cross_out, row_count) + side_vec[1]
    after = middle + crossed
    normed_two, inverse_two = layer_parts(after)
    hidden_two = (normed_two * (1.0 + mod_rows[:, 4]) + mod_rows[:, 3]).astype(low_type)
    upper = jnp.dot(hidden_two, w_mlp[0], preferred_element_type=full_type) + up_bias
    activated = gelu_tanh(upper).astype(low_type)

    def down_out(begin, count):
        return jnp.einsum("rf,of->ro", activated, w_mlp[1], preferred_element_type=full_type)

    mlp_out = row_total(down_out, row_count) + side_vec[2]
    final = after + mod_rows[:, 5] * mlp_out
    block_out = (live_rows * final).astype(low_type)
    grad_four = live_rows * cotangent.astype(full_type)
    d_gate_two = per_clip(grad_four * mlp_out)
    d_mlp_full = (
        modul[:, 5:6] * live * cotangent.astype(full_type).reshape(clips, seq_rows, width)
    ).reshape(row_count, width)
    d_bias_two = jnp.sum(d_mlp_full, axis=0)
    d_mlp_low = d_mlp_full.astype(low_type)
    grad_down = jnp.einsum("ro,rf->of", d_mlp_low, activated, preferred_element_type=full_type)
    d_act = jnp.einsum("ro,of->rf", d_mlp_low, w_mlp[1], preferred_element_type=full_type)
    d_upper = (d_act * gelu_slope(upper)).astype(low_type)
    grad_upbias = jnp.sum(d_upper.astype(full_type), axis=0)
    grad_up = jnp.einsum("rd,rf->df", hidden_two, d_upper, preferred_element_type=full_type)
    grad_mlp = jnp.stack([grad_up, grad_down])

    def up_back(begin, count):
        return jnp.einsum("rf,df->rd", d_upper, w_mlp[0], preferred_element_type=full_type)

    d_hidden_two = row_total(up_back, row_count)
    d_shift_two = per_clip(d_hidden_two)
    d_scale_two = per_clip(d_hidden_two * normed_two)
    grad_three = grad_four + norm_back(
        d_hidden_two * (1.0 + mod_rows[:, 4]), normed_two, inverse_two
    )
    d_bias_one = jnp.sum(grad_three, axis=0)
    d_cross_low = grad_three.astype(low_type)
    grad_cout = jnp.einsum("ro,re->oe", d_cross_low, mixed_two, preferred_element_type=full_type)
    d_mixed_two = (
        jnp.einsum("ro,oe->re", d_cross_low, w_attn[7], preferred_element_type=full_type)
        .astype(low_type)
        .reshape(clips, seq_rows, heads_here, head_width)
    )
    cross_again = jnp.where(
        allowed,
        jnp.einsum("cqhd,ckhd->chqk", query_heads, text_heads[0], preferred_element_type=full_type)
        * scale,
        -1e30,
    )
    cross_full = jnp.exp(cross_again - cross_log)
    d_cprobs = jnp.einsum(
        "cqhd,ckhd->chqk", d_mixed_two, text_heads[1], preferred_element_type=full_type
    )
    d_cvalues = jnp.einsum(
        "chqk,cqhd->ckhd",
        cross_full.astype(low_type),
        d_mixed_two,
        preferred_element_type=full_type,
    ).astype(low_type)
    d_cscores = softmax_back(cross_full, d_cprobs).astype(low_type)
    d_cquery = (
        (
            jnp.einsum(
                "chqk,ckhd->cqhd", d_cscores, text_heads[0], preferred_element_type=full_type
            )
            * scale
        )
        .astype(low_type)
        .reshape(row_count, device_local)
    )
    d_ckeys = (
        jnp.einsum("chqk,cqhd->ckhd", d_cscores, query_heads, preferred_element_type=full_type)
        * scale
    ).astype(low_type)
    d_text_proj = jnp.stack([d_ckeys, d_cvalues]).reshape(2, clips * tlen, device_local)
    grad_cquery = jnp.einsum("rd,re->de", query_in, d_cquery, preferred_element_type=full_type)
    grad_ctext = jnp.einsum(
        "rd,kre->kde",
        text.reshape(clips * tlen, width),
        d_text_proj,
        preferred_element_type=full_type,
    )

    def cquery_back(begin, count):
        return jnp.einsum("re,de->rd", d_cquery, w_attn[4], preferred_element_type=full_type)

    grad_two = grad_three + row_total(cquery_back, row_count)
    d_gate_one = per_clip(grad_two * attended)
    d_attended = mod_rows[:, 2] * grad_two
    d_bias_zero = jnp.sum(d_attended, axis=0)
    d_att_low = d_attended.astype(low_type)
    grad_sout = jnp.einsum("ro,re->oe", d_att_low, mixed_one, preferred_element_type=full_type)
    d_mixed_one = (
        jnp.einsum("ro,oe->re", d_att_low, w_attn[3], preferred_element_type=full_type)
        .astype(low_type)
        .reshape(seqs, FRAMES, heads_here, head_width)
    )
    self_again = (
        jnp.einsum("sfhd,sghd->shfg", shaped[0], shaped[1], preferred_element_type=full_type)
        * scale
    )
    self_full = jnp.exp(self_again - self_log)
    d_sprobs = jnp.einsum(
        "sfhd,sghd->shfg", d_mixed_one, shaped[2], preferred_element_type=full_type
    )
    self_value_gradient = jnp.einsum(
        "shfg,sfhd->sghd", self_full.astype(low_type), d_mixed_one, preferred_element_type=full_type
    ).astype(low_type)
    d_sscores = softmax_back(self_full, d_sprobs).astype(low_type)
    self_query_gradient = (
        jnp.einsum("shfg,sghd->sfhd", d_sscores, shaped[1], preferred_element_type=full_type)
        * scale
    ).astype(low_type)
    self_key_gradient = (
        jnp.einsum("shfg,sfhd->sghd", d_sscores, shaped[0], preferred_element_type=full_type)
        * scale
    ).astype(low_type)
    projection_gradient = jnp.stack(
        [self_query_gradient, self_key_gradient, self_value_gradient]
    ).reshape(3, row_count, device_local)
    grad_qkv = jnp.einsum(
        "rd,kre->kde", hidden_one, projection_gradient, preferred_element_type=full_type
    )

    def qkv_back(begin, count):
        return jnp.einsum(
            "kre,kde->rd", projection_gradient, w_attn[0:3], preferred_element_type=full_type
        )

    d_hidden_one = row_total(qkv_back, row_count)
    normed_one_rows = normed_one.reshape(row_count, width)
    inverse_one_rows = inverse_one.reshape(row_count, 1)
    d_shift_one = per_clip(d_hidden_one)
    d_scale_one = per_clip(d_hidden_one * normed_one_rows)
    grad_one = grad_two + norm_back(
        d_hidden_one * (1.0 + mod_rows[:, 1]), normed_one_rows, inverse_one_rows
    )
    latent_grad = root_rows * grad_one
    d_modul_part = jnp.stack(
        [d_shift_one, d_scale_one, d_gate_one, d_shift_two, d_scale_two, d_gate_two], axis=1
    )
    bias_part = jnp.stack([d_bias_zero, d_bias_one, d_bias_two])
    d_modul, bias_three = clip_totals(d_modul_part, bias_part)
    grad_time = jnp.einsum("cf,cjd->jfd", feats.astype(full_type), d_modul, precision=HIGHEST)
    grad_side = jnp.concatenate([bias_three, jnp.sum(d_modul, axis=0)], axis=0)
    grad_attn = jnp.concatenate(
        [grad_qkv, grad_sout[None], grad_cquery[None], grad_ctext, grad_cout[None]], axis=0
    )
    attn_shard, mlp_shard, time_shard = (
        lax.psum_scatter(grad_attn, "dp", scatter_dimension=1, tiled=True),
        lax.psum_scatter(grad_mlp, "dp", scatter_dimension=1, tiled=True),
        lax.psum_scatter(grad_time, "dp", scatter_dimension=1, tiled=True),
    )
    side_total, upbias_total = lax.psum((grad_side, grad_upbias), "dp")
    squared_terms = jnp.sum(attn_shard * attn_shard) + jnp.sum(mlp_shard * mlp_shard)
    squared_terms = squared_terms + jnp.sum(time_shard * time_shard) / n_tensor
    squared_terms = squared_terms + jnp.sum(upbias_total * upbias_total) / n_data
    squared_terms = squared_terms + jnp.sum(side_total * side_total) / (n_data * n_tensor)
    grad_norm = jnp.sqrt(lax.psum(squared_terms, ("dp", "tensor")))
    factor = jnp.minimum(1.0, CLIP_NORM / (grad_norm + 1e-06))
    attn_new, attn_m_new, attn_v_new = adamw(
        attn_w, attn_m, attn_v, attn_shard, factor, RATE_MATRIX
    )
    mlp_new, mlp_m_new, mlp_v_new = adamw(mlp_w, mlp_m, mlp_v, mlp_shard, factor, RATE_MATRIX)
    up_new, up_m_new, up_v_new = adamw(up_bias, up_m, up_v, upbias_total, factor, RATE_VECTOR)
    side_new, side_m_new, side_v_new = adamw(
        side_vec, side_m, side_v, side_total, factor, RATE_VECTOR
    )
    time_new, time_m_new, time_v_new = adamw(time_w, time_m, time_v, time_shard, factor, RATE_TIME)
    return (
        block_out,
        latent_grad,
        grad_norm,
        attn_new,
        attn_m_new,
        attn_v_new,
        mlp_new,
        mlp_m_new,
        mlp_v_new,
        up_new,
        up_m_new,
        up_v_new,
        side_new,
        side_m_new,
        side_v_new,
        time_new,
        time_m_new,
        time_v_new,
    )


MESH = pl.DeviceIdType.MESH
LOW = jnp.bfloat16
FULL = jnp.float32
TILE = 384


def dot(left, right, left_dim, right_dim):
    return lax.dot_general(
        left, right, (((left_dim,), (right_dim,)), ((), ())), preferred_element_type=FULL
    )


def ring_place(index, count):
    z, x = lax.div(index, 2), lax.rem(index, 2)
    return z + x * (count - 1 - 2 * z)


def ring_index(place, count):
    high = lax.div(place, count // 2)
    return 2 * (place + high * (count - 1 - 2 * place)) + high


def ring_items(count):
    right, left = [], []
    for hop in range(1, count // 2 + 1):
        for half in (0, 1):
            if hop <= count // 2 - half:
                right.append((half, hop))
                left.append((1 - half, hop))
    return right, left


def flip(items):
    return [(1 - half, hop) for half, hop in items]


class Ring:
    def __init__(self, count, rows, dp, tensor):
        self.count, self.rows = count, rows
        self.lead = -(-rows // 32) * 16
        right, left = ring_items(count)
        self.both = [(right, left), (flip(right), flip(left))]
        self.place = ring_place(dp, count)
        self.sides = [
            (ring_index(lax.rem(self.place + step, count), count), tensor)
            for step in (1, count - 1)
        ]
        self.steps = count - 1
        self.queue = []

    def half_rows(self, half):
        return (0, self.lead) if half == 0 else (self.lead, self.rows - self.lead)

    def block_rows(self, offset, half):
        index = ring_index(lax.rem(self.place + offset + 2 * self.count, self.count), self.count)
        begin, size = self.half_rows(half)
        return pl.ds(pl.multiple_of(index * self.rows + begin, 16), size)

    def pump(self, times):
        for _ in range(min(times, len(self.queue))):
            self.queue.pop(0)()


class Gather(Ring):
    def __init__(self, count, rows, dp, tensor, full, send, recv):
        super().__init__(count, rows, dp, tensor)
        self.full, self.send, self.recv = full, send, recv
        self.copies = {}
        panels = full.shape[0]
        self.left = {panel: self.steps for panel in range(panels)}
        first = min(2, self.steps)
        order = [(panel, step) for panel in range(min(2, panels)) for step in range(first)]
        for panel in range(panels):
            order += [(panel, step) for step in range(first, self.steps)]
            if panel + 2 < panels:
                order += [(panel + 2, step) for step in range(first)]
        for panel, step in order:
            self.queue.append(functools.partial(self.step, panel, step))

    def copy(self, panel, step, side):
        half, hop = self.both[panel % 2][side][step]
        sign = 1 if side == 0 else -1
        target = self.full.at[panel, self.block_rows(-sign * (hop - 1), half)]
        return pltpu.make_async_remote_copy(
            src_ref=target,
            dst_ref=target,
            send_sem=self.send.at[side, panel, step],
            recv_sem=self.recv.at[side, panel, step],
            device_id=self.sides[side],
            device_id_type=MESH,
        )

    def arrived(self, panel, step, side):
        half, hop = self.both[panel % 2][side][step]
        sign = 1 if side == 0 else -1
        here = self.full.at[panel, self.block_rows(-sign * hop, half)]
        pltpu.make_async_remote_copy(
            src_ref=here,
            dst_ref=here,
            send_sem=self.send.at[side, panel, step],
            recv_sem=self.recv.at[side, panel, step],
            device_id=self.sides[side],
            device_id_type=MESH,
        ).wait_recv()

    def step(self, panel, step):
        for side in (0, 1):
            if step >= 2:
                self.arrived(panel, step - 2, side)
            copy = self.copy(panel, step, side)
            copy.start()
            self.copies[side, panel, step] = copy
        self.left[panel] -= 1

    def finish(self, panel):
        while self.left[panel]:
            self.pump(1)
        self.pump(3)
        for step in range(max(0, self.steps - 2), self.steps):
            for side in (0, 1):
                self.arrived(panel, step, side)

    def drain(self):
        for copy in self.copies.values():
            copy.wait_send()


class Reduce(Ring):
    def __init__(self, count, rows, dp, tensor, part, slots, store, send, recv):
        super().__init__(count, rows, dp, tensor)
        self.part, self.slots, self.store = part, slots, store
        self.send, self.recv = send, recv
        self.copies = {}
        self.last = None

    def reach(self, panel, side, half):
        return max(hop for kind, hop in self.both[panel % 2][side] if kind == half)

    def copy(self, panel, step, side):
        half, hop = self.both[panel % 2][side][step]
        size = self.half_rows(half)[1]
        if hop == 1:
            sign = 1 if side == 0 else -1
            offset = sign * self.reach(panel, side, half)
            source = self.part.at[panel, self.block_rows(offset, half)]
        else:
            source = self.slots.at[side, panel, step - 2, pl.ds(0, size)]
        return pltpu.make_async_remote_copy(
            src_ref=source,
            dst_ref=self.slots.at[side, panel, step, pl.ds(0, size)],
            send_sem=self.send.at[side, panel, step],
            recv_sem=self.recv.at[side, panel, step],
            device_id=self.sides[side],
            device_id_type=MESH,
        )

    def step(self, panel, step):
        for side in (0, 1):
            half, hop = self.both[panel % 2][side][step]
            if hop > 1:
                self.copies[side, panel, step - 2].wait_recv()
                sign = 1 if side == 0 else -1
                offset = sign * (self.reach(panel, side, half) + 1 - hop)
                size = self.half_rows(half)[1]
                slot = self.slots.at[side, panel, step - 2, pl.ds(0, size)]
                slot[...] = (
                    slot[...].astype(FULL)
                    + self.part[panel, self.block_rows(offset, half), :].astype(FULL)
                ).astype(LOW)
            copy = self.copy(panel, step, side)
            copy.start()
            self.copies[side, panel, step] = copy

    def add_panel(self, panel):
        first = min(2, self.steps)
        for step in range(first):
            self.queue.insert(step, functools.partial(self.step, panel, step))
        for step in range(first, self.steps):
            self.queue.append(functools.partial(self.step, panel, step))
            if step == first and self.last is not None:
                self.queue.append(functools.partial(self.finish, self.last))
        if first == self.steps and self.last is not None:
            self.queue.append(functools.partial(self.finish, self.last))
        self.last = panel

    def finish(self, panel):
        for step in range(max(0, self.steps - 2), self.steps):
            for side in (0, 1):
                self.copies[side, panel, step].wait_recv()
        for half in (0, 1):
            begin, size = self.half_rows(half)
            value = self.part[panel, self.block_rows(0, half), :].astype(FULL)
            for side in (0, 1):
                spots = [s for s, item in enumerate(self.both[panel % 2][side]) if item[0] == half]
                if spots:
                    value = value + self.slots[side, panel, spots[-1], pl.ds(0, size), :].astype(FULL)
            self.store(panel, pl.ds(begin, size), value)

    def complete(self):
        self.pump(len(self.queue))
        self.finish(self.last)

    def drain(self):
        for copy in self.copies.values():
            copy.wait_send()


class Sum:
    def __init__(self, place, part, near, out, far, sems):
        self.place, self.part, self.near, self.out, self.far, self.sems = place, part, near, out, far, sems

    def start(self):
        dp, me, mate, across, beyond, rows = self.place
        self.copies = []
        for spot, block in enumerate((mate, beyond)):
            copy = pltpu.make_async_remote_copy(
                src_ref=self.part.at[pl.ds(pl.multiple_of(block * rows, 16), rows)],
                dst_ref=self.near.at[spot],
                send_sem=self.sems.at[spot],
                recv_sem=self.sems.at[3 + spot],
                device_id=(dp, mate),
                device_id_type=MESH,
            )
            copy.start()
            self.copies.append(copy)

    def middle(self):
        dp, me, mate, across, beyond, rows = self.place
        for copy in self.copies:
            copy.wait()
        block = pl.ds(pl.multiple_of(across * rows, 16), rows)
        self.out[...] = (self.part[block, :] + self.near[1]).astype(LOW)
        self.last = pltpu.make_async_remote_copy(
            src_ref=self.out,
            dst_ref=self.far,
            send_sem=self.sems.at[2],
            recv_sem=self.sems.at[5],
            device_id=(dp, across),
            device_id_type=MESH,
        )
        self.last.start()

    def end(self):
        dp, me, mate, across, beyond, rows = self.place
        self.last.wait()
        block = pl.ds(pl.multiple_of(me * rows, 16), rows)
        return self.part[block, :] + self.near[0] + self.far[...].astype(FULL)


class Share:
    def __init__(self, place, full, sems):
        self.place, self.full, self.sems = place, full, sems

    def rows(self, block):
        rows = self.place[5]
        return self.full.at[pl.ds(pl.multiple_of(block * rows, 16), rows)]

    def copy(self, block, target, spot):
        return pltpu.make_async_remote_copy(
            src_ref=self.rows(block),
            dst_ref=self.rows(block),
            send_sem=self.sems.at[spot],
            recv_sem=self.sems.at[3 + spot],
            device_id=(self.place[0], target),
            device_id_type=MESH,
        )

    def start(self):
        dp, me, mate, across, beyond, rows = self.place
        self.far = self.copy(me, across, 0)
        self.near = self.copy(me, mate, 1)
        self.far.start()
        self.near.start()

    def middle(self):
        dp, me, mate, across, beyond, rows = self.place
        self.far.wait()
        self.onward = self.copy(across, mate, 2)
        self.onward.start()

    def end(self):
        self.near.wait()
        self.onward.wait()


def row_norm(values):
    centered = values - jnp.mean(values, axis=-1, keepdims=True)
    inverse = lax.rsqrt(jnp.mean(centered * centered, axis=-1, keepdims=True) + 1e-06)
    return centered * inverse, inverse


def block_kernel(
    n_data,
    n_tensor,
    clips,
    tsteps,
    clip_count,
    text_len,
    latent_in,
    noise_in,
    cot_in,
    text_in,
    attn_in,
    mlp_in,
    time_in,
    up_bias,
    side,
    block_out,
    latent_grad_out,
    grad_attn_out,
    grad_mlp_out,
    grad_time_out,
    grad_up,
    grad_side,
    square_sum,
    latent,
    noise,
    cot,
    text,
    attn_w,
    mlp_w,
    time_map,
    latent_grad,
    weights,
    parts,
    slots,
    feats,
    feats_all,
    modul_out,
    modul_in,
    modul,
    hidden_one,
    heads_one,
    probs_one,
    mixed_one,
    heads_two,
    text_heads,
    probs_two,
    mixed_two,
    shared,
    activated,
    slope,
    d_upper,
    d_heads,
    d_text,
    sums,
    near,
    out,
    far,
    own,
    inverses,
    small,
    small_all,
    totals,
    totals_all,
    up_row,
    up_all,
    norms,
    norms_all,
    splits,
    squares,
    load_sems,
    store_sems,
    gather_send,
    gather_recv,
    reduce_send,
    reduce_recv,
    sum_sems,
    share_sems,
    feat_sems,
    modul_sems,
    modul_share_sems,
    small_sems,
    total_sems,
    up_sems,
    total_share_sems,
    norm_sems,
    norm_share_sems,
):
    dp, me = lax.axis_index("dp"), lax.axis_index("tensor")
    loads = [
        pltpu.make_async_copy(source, target, load_sems.at[k])
        for k, (source, target) in enumerate(
            (
                (attn_in, attn_w),
                (mlp_in, mlp_w),
                (time_in, time_map),
                (latent_in, latent),
                (noise_in, noise),
                (cot_in, cot),
                (text_in, text),
            )
        )
    ]
    for load in loads:
        load.start()
    grad_attn, grad_mlp, grad_time = attn_w, mlp_w, time_map
    final, d_mlp = latent, noise
    stores = []

    def store_out(source, target):
        copy = pltpu.make_async_copy(source, target, store_sems.at[len(stores)])
        copy.start()
        stores.append(copy)

    rows, width = latent.shape
    clip_rows = rows // clips
    own_rows = rows // n_tensor
    per_clip = n_tensor // clips
    head_width = width // HEADS
    local = width // n_tensor
    heads = local // head_width
    scale = head_width ** (-0.5)
    tlen = text.shape[0] // clips
    mate = me + 1 - 2 * lax.rem(me, 2)
    across = lax.rem(me + 2, n_tensor)
    beyond = lax.rem(mate + 2, n_tensor)
    place = (dp, me, mate, across, beyond, own_rows)
    data_peers = [lax.rem(dp + k, n_data) for k in range(1, n_data)]
    tensor_peers = [lax.rem(me + k, n_tensor) for k in range(1, n_tensor)]
    mine = pl.ds(pl.multiple_of(me * own_rows, 16), own_rows)

    barrier = pltpu.get_barrier_semaphore()
    for peer in data_peers:
        pl.semaphore_signal(barrier, inc=1, device_id=(peer, me), device_id_type=MESH)
    for peer in tensor_peers:
        pl.semaphore_signal(barrier, inc=1, device_id=(dp, peer), device_id_type=MESH)

    table_step = 128 * lax.broadcasted_iota(jnp.int32, (8, 128), 0) + lax.broadcasted_iota(jnp.int32, (8, 128), 1)
    betas = 0.0001 + (0.02 - 0.0001) * table_step.astype(FULL) / 999.0
    logs = jnp.log(1.0 - jnp.where(table_step < 1000, betas, 0.0))

    def abar_of(clip):
        chosen = jnp.where(table_step <= tsteps[clip], logs, 0.0)
        return jnp.exp(jnp.sum(jnp.sum(chosen, axis=0, keepdims=True), axis=1, keepdims=True))

    def live_of(clip):
        return jnp.where(clip < clip_count[0], 1.0, 0.0)

    half = TFREQ // 2
    freqs = jnp.exp(
        -math.log(10000.0) * lax.broadcasted_iota(jnp.int32, (1, half), 1).astype(FULL) / half
    )
    lines = []
    for clip in range(clips):
        angles = tsteps[clip].astype(FULL) * freqs
        lines.append(jnp.concatenate([jnp.cos(angles), jnp.sin(angles)], axis=1))
    lines = jnp.concatenate(lines, axis=0)
    lines = lines / (1.0 + jnp.exp(-lines))
    feats[...] = jnp.concatenate([lines, jnp.zeros((feats.shape[0] - clips, TFREQ), FULL)], axis=0).astype(LOW)

    def send_all(source_of, target, sems, along):
        copies = []
        peers = data_peers if along == "dp" else tensor_peers
        for k, peer in enumerate(peers):
            copy = pltpu.make_async_remote_copy(
                src_ref=source_of(peer),
                dst_ref=target,
                send_sem=sems.at[0, k],
                recv_sem=sems.at[1, k],
                device_id=(peer, me) if along == "dp" else (dp, peer),
                device_id_type=MESH,
            )
            copy.start()
            copies.append(copy)
        return copies

    def wait_all(copies):
        for copy in copies:
            copy.wait()

    panel_rows = mlp_w.shape[1]

    def store_grad(panel, block, value):
        squares[...] += jnp.sum(value * value, axis=0, keepdims=True)
        if panel >= 2:
            grad_mlp[panel - 2, block, :] = value
        else:
            for k in range(4):
                grad_attn[4 * panel + k, block, :] = value[:, k * local : (k + 1) * local]

    gather = Gather(n_data, panel_rows, dp, me, weights, gather_send, gather_recv)
    reduce = Reduce(n_data, panel_rows, dp, me, parts, slots, store_grad, reduce_send, reduce_recv)
    own_panel = pl.ds(pl.multiple_of(dp * panel_rows, 16), panel_rows)

    def pack(panel):
        if panel >= 2:
            weights[panel, own_panel, :] = mlp_w[panel - 2].astype(LOW)
        else:
            weights[panel, own_panel, :] = jnp.concatenate(
                [attn_w[4 * panel + k] for k in range(4)], axis=1
            ).astype(LOW)

    loads[0].wait()
    pack(0)
    pl.semaphore_wait(barrier, n_data + n_tensor - 2)
    feats_all[dp] = feats[...]
    feat_copies = send_all(lambda peer: feats, feats_all.at[dp], feat_sems, "dp")
    gather.pump(min(2, n_data - 1))
    pack(1)
    gather.pump(min(2, n_data - 1))
    loads[1].wait()
    pack(2)
    pack(3)

    n_feats = time_map.shape[1]
    feat_rows, n_freq = feats.shape
    modul_share = clips * 6 // n_tensor
    loads[2].wait()
    wait_all(feat_copies)
    pick = (
        lax.broadcasted_iota(jnp.int32, (n_freq, n_feats), 0)
        == lax.broadcasted_iota(jnp.int32, (n_freq, n_feats), 1) + n_feats * dp
    ).astype(FULL).astype(LOW)
    feats_flat = feats_all[...].reshape(n_data * feat_rows, n_freq)
    feats_mine = dot(feats_flat, pick, 1, 0).astype(LOW)
    my_clip = lax.div(me, per_clip)
    first = modul_share * lax.rem(me, per_clip)
    rows_of_clip = (
        lax.broadcasted_iota(jnp.int32, (n_data, n_data * feat_rows), 1)
        == feat_rows * lax.broadcasted_iota(jnp.int32, (n_data, n_data * feat_rows), 0) + my_clip
    ).astype(FULL).astype(LOW)
    feats_clip = dot(rows_of_clip, feats_mine, 1, 0).astype(LOW)
    for k in range(modul_share):
        partial = dot(feats_clip, time_map[first + k].astype(LOW), 1, 0)
        for peer in range(n_data):
            modul_out[peer, k : k + 1, :] = partial[peer : peer + 1]
    for peer in range(n_data):
        modul_out[peer, modul_share:, :] = jnp.zeros((modul_out.shape[1] - modul_share, width), FULL)
    modul_in[dp] = modul_out[dp]
    modul_copies = send_all(lambda peer: modul_out.at[peer], modul_in.at[dp], modul_sems, "dp")
    gather.pump(1)
    lane = lax.broadcasted_iota(jnp.int32, (1, local), 1)
    head_masks = [
        ((lane >= h * head_width) & (lane < (h + 1) * head_width)).astype(FULL) for h in range(heads)
    ]
    wait_all(modul_copies)
    total = modul_in[0]
    for peer in range(1, n_data):
        total = total + modul_in[peer]
    chosen = jnp.where(lax.rem(me, per_clip) == 0, side[3 : 3 + modul_share, :], side[3 + modul_share : 9, :])
    modul[me] = jnp.concatenate(
        [total[0:modul_share] + chosen, total[modul_share:]], axis=0
    )
    modul_copies = send_all(lambda peer: modul.at[me], modul.at[me], modul_share_sems, "tensor")
    gather.pump(1)
    wait_all(modul_copies)

    def modul_row(clip, j):
        return modul[clip * per_clip + j // modul_share, pl.ds(j % modul_share, 1), :]

    def start_of(abar, block):
        return jnp.sqrt(abar) * latent[block, :].astype(FULL) + jnp.sqrt(1.0 - abar) * noise[
            block, :
        ].astype(FULL)

    for load in loads[3:6]:
        load.wait()

    step_rows = 32

    def first_norm(clip, abar, step, carry):
        block = pl.ds(pl.multiple_of(clip * clip_rows + step * step_rows, step_rows), step_rows)
        normed, _ = row_norm(start_of(abar, block))
        hidden_one[block, :] = (normed * (1.0 + modul_row(clip, 1)) + modul_row(clip, 0)).astype(LOW)
        return carry

    for clip in range(clips):
        lax.fori_loop(0, clip_rows // step_rows, functools.partial(first_norm, clip, abar_of(clip)), 0)
        gather.pump(1)
    clip_mine = lax.div(me, per_clip)
    abar_mine = abar_of(clip_mine)
    start_mine = start_of(abar_mine, mine)
    normed, inverse = row_norm(start_mine)
    own[0], own[1] = start_mine, normed
    inverses[0] = jnp.broadcast_to(inverse, (own_rows, 128))
    live_mine = live_of(clip_mine)
    for clip in range(clips):
        block = pl.ds(clip * clip_rows, clip_rows)
        d_mlp[block, :] = (modul_row(clip, 5) * live_of(clip) * cot[block, :].astype(FULL)).astype(LOW)
    gather.finish(0)

    self_cols = -(-3 * local // 128) * 128
    out_cols = 3 * local // 128 * 128
    out_pad = 3 * local - out_cols
    text_cols = local // 128 * 128
    text_pad = local - text_cols
    query_cols = -(-local // 128) * 128

    def split_heads(values, offsets, target, block):
        for k, offset in enumerate(offsets):
            target[k, block, :] = values[:, offset : offset + local].astype(LOW)

    def stacked(values):
        return jnp.concatenate([(values.astype(FULL) * mask).astype(LOW) for mask in head_masks], axis=0)

    def unstacked(values, size):
        total = values[0:size] * head_masks[0]
        for h in range(1, heads):
            total = total + values[h * size : (h + 1) * size] * head_masks[h]
        return total

    def attend(query, keys, values, allowed):
        scores = jnp.where(allowed, dot(stacked(query), keys, 1, 1) * scale, -1e30)
        expo = jnp.exp(scores - jnp.max(scores, axis=-1, keepdims=True))
        probs = expo / jnp.sum(expo, axis=-1, keepdims=True)
        return probs, unstacked(dot(probs.astype(LOW), values, 1, 0), clip_rows)

    def pad_left(values):
        return jnp.concatenate([jnp.zeros((values.shape[0], out_pad), FULL), values], axis=1).astype(LOW)

    def sum_of(index, buffer):
        return Sum(place, sums.at[buffer], near.at[index % 3], out.at[index % 3], far.at[index % 3], sum_sems.at[index])

    def columns(body, total):
        for begin in range(0, total, TILE):
            body(begin, min(TILE, total - begin))

    def product_nt(left, panel, begin, end, buffer):
        def tile(at, size):
            sums[buffer, :, at : at + size] = dot(left, weights[panel, at : at + size, begin:end], 1, 1)

        columns(tile, width)

    for block_at in range(0, rows, 128):
        block = pl.ds(block_at, 128)
        split_heads(
            dot(hidden_one[block, :], weights[0, :, 0:self_cols], 1, 0), (0, local, 2 * local), heads_one, block
        )
    gather.pump(1)
    size = heads * clip_rows
    frame_row = lax.broadcasted_iota(jnp.int32, (size, clip_rows), 0)
    frame_col = lax.broadcasted_iota(jnp.int32, (size, clip_rows), 1)
    frame_bits = FRAMES.bit_length() - 1
    same_sequence = ((frame_row & (clip_rows - 1)) >> frame_bits) == (frame_col >> frame_bits)
    for clip in range(clips):
        block = pl.ds(clip * clip_rows, clip_rows)
        probs, mixed = attend(heads_one[0, block, :], heads_one[1, block, :], heads_one[2, block, :], same_sequence)
        probs_one[clip] = probs
        mixed_one[block, :] = pad_left(mixed)
        gather.pump(1)
    product_nt(mixed_one[...], 0, out_cols, width, 0)
    self_sum = sum_of(0, 0)
    self_sum.start()
    gather.pump(1)
    self_sum.middle()
    gather.pump(1)

    def modul_mine(j):
        return modul[clip_mine * per_clip + j // modul_share, pl.ds(j % modul_share, 1), :]

    attended = self_sum.end() + side[0:1, :]
    own[2] = attended
    middle = own[0] + modul_mine(2) * attended
    own[0] = middle
    shared[0, mine, :] = middle.astype(LOW)
    share = Share(place, shared.at[0], share_sems.at[0])
    share.start()
    gather.pump(1)
    share.middle()
    gather.finish(1)

    loads[6].wait()
    for block_at in range(0, clips * tlen, 128):
        block = pl.ds(block_at, 128)
        split_heads(
            dot(text[block, :], weights[1, :, text_cols : text_cols + 5 * 128], 1, 0),
            (text_pad, text_pad + local),
            text_heads,
            block,
        )
    share.end()
    gather.pump(1)
    key_index = lax.broadcasted_iota(jnp.int32, (size, tlen), 1)
    heads_two[...] = dot(shared[0], weights[1, :, 0:query_cols], 1, 0)[:, 0:local].astype(LOW)
    for clip in range(clips):
        block = pl.ds(clip * clip_rows, clip_rows)
        words = pl.ds(clip * tlen, tlen)
        probs, mixed = attend(
            heads_two[block, :], text_heads[0, words, :], text_heads[1, words, :], key_index < text_len[clip]
        )
        probs_two[clip] = probs
        mixed_two[block, :] = pad_left(mixed)
        gather.pump(1)
    product_nt(mixed_two[...], 1, out_cols, width, 0)
    cross_sum = sum_of(1, 0)
    cross_sum.start()
    gather.pump(1)
    cross_sum.middle()
    gather.pump(1)
    after = own[0] + cross_sum.end() + side[1:2, :]
    own[0] = after
    normed, inverse = row_norm(after)
    own[3] = normed
    inverses[1] = jnp.broadcast_to(inverse, (own_rows, 128))
    shared[1, mine, :] = (normed * (1.0 + modul_mine(4)) + modul_mine(3)).astype(LOW)
    share = Share(place, shared.at[1], share_sems.at[1])
    share.start()
    gather.pump(1)
    share.middle()
    gather.finish(2)
    share.end()

    def up(at, size):
        cols = slice(at, at + size)
        upper = dot(shared[1], weights[2, :, cols], 1, 0) + up_bias[cols].reshape(1, size)
        tangent = jnp.tanh(0.7978845608028654 * (upper + 0.044715 * upper * upper * upper))
        inner = 0.7978845608028654 * (1.0 + 3.0 * 0.044715 * upper * upper)
        activated[:, cols] = (0.5 * upper * (1.0 + tangent)).astype(LOW)
        slope[:, cols] = 0.5 * (1.0 + tangent) + 0.5 * upper * (1.0 - tangent * tangent) * inner
        gather.pump(1)

    columns(up, width)

    def grad_tile(panel, left, right, at, size):
        cols = slice(at, at + size)
        parts[panel, :, cols] = dot(left, right[:, cols], 0, 0).astype(LOW)

    def grad_panel(panel, left, right):
        columns(functools.partial(grad_tile, panel, left, right), width)

    grad_panel(3, d_mlp[...], activated)
    gather.finish(3)
    reduce.add_panel(3)
    reduce.pump(2)

    small[...] = jnp.zeros_like(small)
    squares[...] = jnp.zeros_like(squares)

    def up_slope(at, size):
        cols = slice(at, at + size)
        value = (dot(d_mlp[...], weights[3, :, cols], 1, 0) * slope[:, cols]).astype(LOW)
        d_upper[:, cols] = value
        small[9:10, cols] = jnp.sum(value.astype(FULL), axis=0, keepdims=True)

    columns(up_slope, width)
    grad_panel(2, shared[1], d_upper)
    reduce.add_panel(2)
    reduce.pump(2)
    product_nt(d_upper[...], 2, 0, width, 0)
    hidden_sum = sum_of(2, 0)
    hidden_sum.start()
    reduce.pump(1)
    hidden_sum.middle()
    product_nt(activated[...], 3, 0, width, 1)
    mlp_sum = sum_of(3, 1)
    mlp_sum.start()
    reduce.pump(1)

    def norm_back(grad_out, normed, inverse):
        first_mean = jnp.mean(grad_out, axis=-1, keepdims=True)
        second_mean = jnp.mean(grad_out * normed, axis=-1, keepdims=True)
        return inverse * (grad_out - first_mean - normed * second_mean)

    def row_sum(values):
        return jnp.sum(values, axis=0, keepdims=True)

    cot_mine = cot[mine, :].astype(FULL)
    d_hidden = hidden_sum.end()
    normed = own[3]
    small[3:4, :] = row_sum(d_hidden)
    small[4:5, :] = row_sum(d_hidden * normed)
    grad_three = live_mine * cot_mine + norm_back(
        d_hidden * (1.0 + modul_mine(4)), normed, inverses[1, :, 0:1]
    )
    own[3] = grad_three
    small[7:8, :] = row_sum(grad_three)
    shared[2, mine, :] = grad_three.astype(LOW)
    share = Share(place, shared.at[2], share_sems.at[2])
    share.start()
    mlp_sum.middle()
    reduce.pump(1)
    share.middle()
    reduce.pump(1)
    mlp_out = mlp_sum.end() + side[2:3, :]
    grad_four = live_mine * cot_mine
    small[5:6, :] = row_sum(grad_four * mlp_out)
    small[8:9, :] = row_sum(modul_mine(5) * grad_four)
    final[mine, :] = (live_mine * (own[0] + modul_mine(5) * mlp_out)).astype(LOW)
    share.end()
    out_share = Share(place, final, share_sems.at[3])
    out_share.start()

    def attend_back(query, keys, values, probs, d_mixed):
        stacked_grad = stacked(d_mixed)
        stacked_query = stacked(query)
        d_probs = dot(stacked_grad, values, 1, 1)
        d_values = dot(probs.astype(LOW), stacked_grad, 0, 0).astype(LOW)
        d_scores = (probs * (d_probs - jnp.sum(probs * d_probs, axis=-1, keepdims=True))).astype(LOW)
        d_query = (unstacked(dot(d_scores, keys, 1, 0), clip_rows) * scale).astype(LOW)
        d_keys = (dot(d_scores, stacked_query, 0, 0) * scale).astype(LOW)
        return d_query, d_keys, d_values

    def spread_out(pieces, offset, total):
        have = sum(piece.shape[1] for piece in pieces)
        height = pieces[0].shape[0]
        ends = [(offset, pieces[:0]), (total - offset - have, None)]
        full = list(pieces)
        if ends[0][0]:
            full.insert(0, jnp.zeros((height, offset), LOW))
        if ends[1][0]:
            full.append(jnp.zeros((height, ends[1][0]), LOW))
        return jnp.concatenate(full, axis=1)

    d_mixed = dot(shared[2], weights[1, :, out_cols:width], 1, 0)[:, out_pad:].astype(LOW)
    reduce.pump(1)
    for clip in range(clips):
        block = pl.ds(clip * clip_rows, clip_rows)
        words = pl.ds(clip * tlen, tlen)
        d_query, d_keys, d_values = attend_back(
            heads_two[block, :],
            text_heads[0, words, :],
            text_heads[1, words, :],
            probs_two[clip],
            d_mixed[clip * clip_rows : (clip + 1) * clip_rows],
        )
        d_heads[block, 0:query_cols] = spread_out([d_query], 0, query_cols)
        d_text[words, :] = spread_out([d_keys, d_values], text_pad, 5 * 128)
        reduce.pump(1)
    product_nt(d_heads[:, 0:query_cols], 1, 0, query_cols, 0)
    query_sum = sum_of(4, 0)
    query_sum.start()
    reduce.pump(1)
    out_share.middle()
    query_sum.middle()
    reduce.pump(1)
    query_part = dot(shared[0], d_heads[:, 0:query_cols], 0, 0)
    text_part = dot(text[...], d_text[...], 0, 0)
    out_part = dot(shared[2], mixed_two[...], 0, 0)
    parts[1, :, 0:text_cols] = query_part[:, 0:text_cols].astype(LOW)
    parts[1, :, text_cols:query_cols] = (
        query_part[:, text_cols:query_cols] + text_part[:, 0 : query_cols - text_cols]
    ).astype(LOW)
    parts[1, :, query_cols:out_cols] = text_part[:, query_cols - text_cols : out_cols - text_cols].astype(LOW)
    parts[1, :, out_cols:self_cols] = (
        text_part[:, out_cols - text_cols : self_cols - text_cols] + out_part[:, 0 : self_cols - out_cols]
    ).astype(LOW)
    parts[1, :, self_cols:width] = out_part[:, self_cols - out_cols :].astype(LOW)
    reduce.add_panel(1)
    reduce.pump(2)
    grad_two = own[3] + query_sum.end()
    own[3] = grad_two
    small[2:3, :] = row_sum(grad_two * own[2])
    d_attended = modul_mine(2) * grad_two
    small[6:7, :] = row_sum(d_attended)
    shared[3, mine, :] = d_attended.astype(LOW)
    share = Share(place, shared.at[3], share_sems.at[4])
    share.start()
    out_share.end()
    store_out(final, block_out)
    reduce.pump(1)
    share.middle()
    reduce.pump(1)
    share.end()

    d_mixed = dot(shared[3], weights[0, :, out_cols:width], 1, 0)[:, out_pad:].astype(LOW)
    for clip in range(clips):
        block = pl.ds(clip * clip_rows, clip_rows)
        grads = attend_back(
            heads_one[0, block, :],
            heads_one[1, block, :],
            heads_one[2, block, :],
            probs_one[clip],
            d_mixed[clip * clip_rows : (clip + 1) * clip_rows],
        )
        d_heads[block, :] = spread_out(list(grads), 0, self_cols)
        reduce.pump(1)
    product_nt(d_heads[...], 0, 0, self_cols, 1)
    first_sum = sum_of(5, 1)
    first_sum.start()
    reduce.pump(1)
    first_sum.middle()
    for at in range(0, width, TILE):
        row_part = dot(hidden_one[:, at : at + TILE], d_heads[...], 0, 0)
        out_part = dot(shared[3, :, at : at + TILE], mixed_one[...], 0, 0)
        block = slice(at, at + TILE)
        parts[0, block, 0:out_cols] = row_part[:, 0:out_cols].astype(LOW)
        parts[0, block, out_cols:self_cols] = (
            row_part[:, out_cols:self_cols] + out_part[:, 0 : self_cols - out_cols]
        ).astype(LOW)
        parts[0, block, self_cols:width] = out_part[:, self_cols - out_cols :].astype(LOW)
    reduce.add_panel(0)
    reduce.pump(2)
    d_hidden = first_sum.end()
    normed = own[1]
    small[0:1, :] = row_sum(d_hidden)
    small[1:2, :] = row_sum(d_hidden * normed)
    grad_one = own[3] + norm_back(d_hidden * (1.0 + modul_mine(1)), normed, inverses[0, :, 0:1])
    latent_grad[mine, :] = jnp.sqrt(abar_mine) * grad_one
    small_all[me] = small[...]
    small_copies = send_all(lambda peer: small, small_all.at[me], small_sems, "tensor")
    share = Share(place, latent_grad, share_sems.at[5])
    share.start()
    up_row[...] = small[9:10, :]
    up_all[dp] = up_row[...]
    up_copies = send_all(lambda peer: up_row, up_all.at[dp], up_sems, "dp")
    reduce.pump(1)

    wait_all(small_copies)
    totals[...] = jnp.zeros_like(totals)
    for clip in range(clips):
        value = small_all[clip * per_clip, 0:6, :]
        for k in range(1, per_clip):
            value = value + small_all[clip * per_clip + k, 0:6, :]
        totals[6 * clip : 6 * clip + 6, 0:width] = value
    value = small_all[0, 6:9, :]
    for k in range(1, n_tensor):
        value = value + small_all[k, 6:9, :]
    totals[6 * clips : 6 * clips + 3, 0:width] = value
    piece = totals.shape[1] // n_tensor
    my_columns = pl.ds(pl.multiple_of(me * piece, 128), piece)
    totals_all[dp, :, my_columns] = totals[:, my_columns]
    total_copies = send_all(
        lambda peer: totals.at[:, my_columns], totals_all.at[dp, :, my_columns], total_sems, "dp"
    )
    reduce.pump(1)
    share.middle()
    reduce.pump(1)
    wait_all(total_copies)
    my_totals = totals_all.at[:, :, my_columns]
    total_copies = send_all(lambda peer: my_totals, my_totals, total_share_sems, "tensor")
    reduce.pump(1)
    share.end()
    store_out(latent_grad, latent_grad_out)
    wait_all(up_copies)
    reduce.pump(1)
    wait_all(total_copies)
    sides = totals_all[0, :, 0:width]
    ups = up_all[0]
    for peer in range(1, n_data):
        sides = sides + totals_all[peer, :, 0:width]
        ups = ups + up_all[peer]
    grad_side[0:3, :] = sides[6 * clips : 6 * clips + 3]
    value = sides[0:6]
    for clip in range(1, clips):
        value = value + sides[6 * clip : 6 * clip + 6]
    grad_side[3:9, :] = value
    grad_up[...] = ups.reshape(width)
    reduce.pump(1)
    total_rows = n_data * totals.shape[0]
    flat = totals_all[:, :, 0:width].reshape(total_rows, width)
    for k in range(3):
        piece = flat.astype(LOW)
        splits[pl.ds(k * total_rows, total_rows), :] = piece
        flat = flat - piece.astype(FULL)
    feat_index = lax.broadcasted_iota(jnp.int32, (total_rows, n_data * feat_rows), 1)
    total_index = lax.broadcasted_iota(jnp.int32, (total_rows, n_data * feat_rows), 0)
    feat_clip, total_row = feat_index & (feat_rows - 1), total_index & (totals.shape[0] - 1)
    feat_bits, total_bits = feat_rows.bit_length() - 1, totals.shape[0].bit_length() - 1
    same_data = ((feat_index >> feat_bits) == (total_index >> total_bits)) & (feat_clip < clips)
    lesser = jnp.zeros((1, width), FULL)
    for j in range(6):
        spot = (same_data & (total_row == 6 * feat_clip + j)).astype(FULL).astype(LOW)
        lifted = dot(spot, feats_mine, 1, 0).astype(LOW)
        value = dot(jnp.concatenate([lifted] * 3, axis=0), splits[...], 0, 0)
        grad_time[j] = value
        lesser = lesser + row_sum(value * value)
        if j % 2 == 1:
            reduce.pump(1)
    store_out(grad_time, grad_time_out)
    lesser = lesser * (1.0 / n_tensor)
    lesser = lesser + ups * ups * (1.0 / n_data)
    value = grad_side[...]
    lesser = lesser + row_sum(value * value) * (1.0 / (n_data * n_tensor))
    reduce.complete()
    store_out(grad_attn, grad_attn_out)
    store_out(grad_mlp, grad_mlp_out)
    mine_sum = jnp.broadcast_to(jnp.sum(lesser + squares[...], axis=1, keepdims=True), (8, 128))
    norms[0] = mine_sum
    norms_all[0, dp] = mine_sum
    norm_copies = send_all(lambda peer: norms.at[0], norms_all.at[0, dp], norm_sems, "dp")
    gather.drain()
    reduce.drain()
    wait_all(norm_copies)
    value = norms_all[0, 0]
    for peer in range(1, n_data):
        value = value + norms_all[0, peer]
    norms[1] = value
    norms_all[1, me] = value
    norm_copies = send_all(lambda peer: norms.at[1], norms_all.at[1, me], norm_share_sems, "tensor")
    wait_all(norm_copies)
    value = norms_all[1, 0]
    for peer in range(1, n_tensor):
        value = value + norms_all[1, peer]
    square_sum[...] = value
    for copy in stores:
        copy.wait()


def fits(n_data, n_tensor, rows, clips, panel_rows, units):
    clip_rows = rows // clips
    return (
        n_tensor == 4
        and clips == 2
        and n_data % 2 == 0
        and n_data <= 8
        and panel_rows % 16 == 0
        and clip_rows == 128
        and units == D
    )


def run_block(
    tsteps, clip_count, text_len, latent, noise, cot, text, attn_w, mlp_w, time_w, up_bias, side_vec
):
    n_data, n_tensor = lax.axis_size("dp"), lax.axis_size("tensor")
    clips = text_len.shape[0]
    tlen = text.shape[0] // clips
    rows, width = latent.shape
    own_rows = rows // n_tensor
    local = width // n_tensor
    heads = HEADS // n_tensor
    clip_rows = rows // clips
    panel_rows, units = mlp_w.shape[1:]
    wide = -(-local // 128) * 128
    self_cols = -(-3 * local // 128) * 128
    steps = n_data - 1
    lead = -(-panel_rows // 32) * 16
    feat_rows = 16
    split = -(-width // (128 * n_tensor)) * 128 * n_tensor
    dma = pltpu.SemaphoreType.DMA
    scratch = [
        pltpu.VMEM((rows, width), LOW),
        pltpu.VMEM((rows, width), LOW),
        pltpu.VMEM((rows, width), LOW),
        pltpu.VMEM(text.shape, LOW),
        pltpu.VMEM(attn_w.shape, FULL),
        pltpu.VMEM(mlp_w.shape, FULL),
        pltpu.VMEM(time_w.shape, FULL),
        pltpu.VMEM((rows, width), FULL),
        pltpu.VMEM((4, width, units), LOW),
        pltpu.VMEM((4, width, units), LOW),
        pltpu.VMEM((2, 4, steps, lead, units), LOW),
        pltpu.VMEM((feat_rows, TFREQ), LOW),
        pltpu.VMEM((n_data, feat_rows, TFREQ), LOW),
        pltpu.VMEM((n_data, 4, width), FULL),
        pltpu.VMEM((n_data, 4, width), FULL),
        pltpu.VMEM((n_tensor, 4, width), FULL),
        pltpu.VMEM((rows, width), LOW),
        pltpu.VMEM((3, rows, local), LOW),
        pltpu.VMEM((clips, heads * clip_rows, clip_rows), FULL),
        pltpu.VMEM((rows, wide), LOW),
        pltpu.VMEM((rows, local), LOW),
        pltpu.VMEM((2, clips * tlen, local), LOW),
        pltpu.VMEM((clips, heads * clip_rows, tlen), FULL),
        pltpu.VMEM((rows, wide), LOW),
        pltpu.VMEM((4, rows, width), LOW),
        pltpu.VMEM((rows, units), LOW),
        pltpu.VMEM((rows, units), FULL),
        pltpu.VMEM((rows, units), LOW),
        pltpu.VMEM((rows, self_cols), LOW),
        pltpu.VMEM((clips * tlen, 5 * 128), LOW),
        pltpu.VMEM((2, rows, width), FULL),
        pltpu.VMEM((3, 2, own_rows, width), FULL),
        pltpu.VMEM((3, own_rows, width), LOW),
        pltpu.VMEM((3, own_rows, width), LOW),
        pltpu.VMEM((4, own_rows, width), FULL),
        pltpu.VMEM((2, own_rows, 128), FULL),
        pltpu.VMEM((16, width), FULL),
        pltpu.VMEM((n_tensor, 16, width), FULL),
        pltpu.VMEM((16, split), FULL),
        pltpu.VMEM((n_data, 16, split), FULL),
        pltpu.VMEM((1, width), FULL),
        pltpu.VMEM((n_data, 1, width), FULL),
        pltpu.VMEM((2, 8, 128), FULL),
        pltpu.VMEM((2, max(n_data, n_tensor), 8, 128), FULL),
        pltpu.VMEM((3 * n_data * 16, width), LOW),
        pltpu.VMEM((1, width), FULL),
        dma((7,)),
        dma((5,)),
        dma((2, 4, steps)),
        dma((2, 4, steps)),
        dma((2, 4, steps)),
        dma((2, 4, steps)),
        dma((6, 6)),
        dma((6, 6)),
        dma((2, steps)),
        dma((2, steps)),
        dma((2, n_tensor - 1)),
        dma((2, n_tensor - 1)),
        dma((2, steps)),
        dma((2, steps)),
        dma((2, n_tensor - 1)),
        dma((2, steps)),
        dma((2, n_tensor - 1)),
    ]
    shape = jax.ShapeDtypeStruct
    vmem = pl.BlockSpec(memory_space=pltpu.VMEM)
    smem = pl.BlockSpec(memory_space=pltpu.SMEM)
    far = pl.BlockSpec(memory_space=pl.ANY)
    return pl.pallas_call(
        functools.partial(block_kernel, n_data, n_tensor, clips),
        out_shape=(
            shape((rows, width), LOW),
            shape((rows, width), FULL),
            shape(attn_w.shape, FULL),
            shape(mlp_w.shape, FULL),
            shape(time_w.shape, FULL),
            shape(up_bias.shape, FULL),
            shape(side_vec.shape, FULL),
            shape((8, 128), FULL),
        ),
        in_specs=[smem] * 3 + [far] * 7 + [vmem] * 2,
        out_specs=(far,) * 5 + (vmem,) * 3,
        scratch_shapes=scratch,
        compiler_params=pltpu.CompilerParams(
            collective_id=0, has_side_effects=True, vmem_limit_bytes=62 * 2**20
        ),
    )(tsteps, clip_count, text_len, latent, noise, cot, text, attn_w, mlp_w, time_w, up_bias, side_vec)


def update_kernel(block_rows, parts, *refs):
    squares, refs = refs[0], refs[1:]
    count = len(parts)
    ins, passed, outs = refs[: 4 * count], refs[4 * count : 4 * count + 2], refs[4 * count + 2 :]
    step = pl.program_id(0)
    norm = jnp.sqrt(squares[0:1, 0:1])
    outs[-1][...] = norm
    factor = jnp.minimum(1.0, CLIP_NORM / (norm + 1e-06))
    for at, (rate, blocks) in enumerate(parts):
        weight, first, second, grad = ins[4 * at : 4 * at + 4]
        targets = outs[3 * at : 3 * at + 3]

        def update():
            if len(weight.shape) < 3:
                spots = [(Ellipsis,)]
            else:
                spots = [(k,) for k in range(weight.shape[0])]
            clip = factor if len(weight.shape) > 1 else factor[0, 0]
            for spot in spots:
                values = adamw(weight[spot], first[spot], second[spot], grad[spot], clip, rate)
                for target, value in zip(targets, values):
                    target[spot] = value

        if blocks is None:
            update()
        else:
            pl.when(step < blocks)(update)
    for at, source in enumerate(passed):
        target = outs[3 * count + at]
        target[...] = source[...]


def run_update(squares, weights, passed):
    steps = weights[0][0].shape[1] // 16
    parts, in_specs, out_specs, operands, shapes = [], [], [], [squares], []
    in_specs.append(pl.BlockSpec(squares.shape, lambda i: (0, 0)))

    def along(size, rows):
        return lambda i: jnp.minimum(i, size // rows - 1)

    for array, *others, rate in weights:
        if array.ndim == 3:
            rows = 16 if array.shape[1] // 16 == steps else 8
            blocks = array.shape[1] // rows
            at = along(array.shape[1], rows)
            spec = pl.BlockSpec((array.shape[0], rows, array.shape[2]), lambda i, at=at: (0, at(i), 0))
        else:
            blocks = 1
            spec = pl.BlockSpec(array.shape, lambda i, n=array.ndim: (0,) * n)
        parts.append((rate, None if blocks == steps else blocks))
        in_specs += [spec] * 4
        out_specs += [spec] * 3
        operands += [array, *others]
        shapes += [jax.ShapeDtypeStruct(array.shape, FULL)] * 3
    for array in passed:
        at = along(array.shape[0], 32)
        spec = pl.BlockSpec((32, array.shape[1]), lambda i, at=at: (at(i), 0))
        in_specs.append(spec)
        out_specs.append(spec)
        operands.append(array)
        shapes.append(jax.ShapeDtypeStruct(array.shape, array.dtype))
    out_specs.append(pl.BlockSpec((1, 1), lambda i: (0, 0)))
    shapes.append(jax.ShapeDtypeStruct((1, 1), FULL))
    return pl.pallas_call(
        functools.partial(update_kernel, 16, parts),
        grid=(steps,),
        out_shape=shapes,
        in_specs=in_specs,
        out_specs=out_specs,
        compiler_params=pltpu.CompilerParams(vmem_limit_bytes=60 * 2**20),
    )(*operands)


def shards(
    latent,
    noise,
    text,
    tsteps,
    clip_count,
    text_len,
    cotangent,
    attn_w,
    attn_m,
    attn_v,
    mlp_w,
    mlp_m,
    mlp_v,
    up_bias,
    up_m,
    up_v,
    side_vec,
    side_m,
    side_v,
    time_w,
    time_m,
    time_v,
):
    n_tensor = lax.axis_size("tensor")
    n_data = lax.axis_size("dp")
    clips, tlen, width = text.shape
    rows = latent.shape[0]
    panel_rows, local = attn_w.shape[1:]
    if not fits(n_data, n_tensor, rows, clips, panel_rows, mlp_w.shape[2]):
        return plain_shards(
            latent, noise, text, tsteps, clip_count, text_len, cotangent, attn_w, attn_m, attn_v, mlp_w, mlp_m,
            mlp_v, up_bias, up_m, up_v, side_vec, side_m, side_v, time_w, time_m, time_v,
        )
    block_out, latent_grad, grad_attn, grad_mlp, grad_time, grad_up, grad_side, squares = run_block(
        tsteps,
        clip_count,
        text_len,
        latent,
        noise,
        cotangent,
        text.reshape(clips * tlen, width),
        attn_w,
        mlp_w,
        time_w,
        up_bias,
        side_vec,
    )
    (
        attn_new,
        attn_m_new,
        attn_v_new,
        mlp_new,
        mlp_m_new,
        mlp_v_new,
        time_new,
        time_m_new,
        time_v_new,
        up_new,
        up_m_new,
        up_v_new,
        side_new,
        side_m_new,
        side_v_new,
        block_out,
        latent_grad,
        grad_norm,
    ) = run_update(
        squares,
        [
            (attn_w, attn_m, attn_v, grad_attn, RATE_MATRIX),
            (mlp_w, mlp_m, mlp_v, grad_mlp, RATE_MATRIX),
            (time_w, time_m, time_v, grad_time, RATE_TIME),
            (up_bias, up_m, up_v, grad_up, RATE_VECTOR),
            (side_vec, side_m, side_v, grad_side, RATE_VECTOR),
        ],
        [block_out, latent_grad],
    )
    return (
        block_out,
        latent_grad,
        grad_norm[0, 0],
        attn_new,
        attn_m_new,
        attn_v_new,
        mlp_new,
        mlp_m_new,
        mlp_v_new,
        up_new,
        up_m_new,
        up_v_new,
        side_new,
        side_m_new,
        side_v_new,
        time_new,
        time_m_new,
        time_v_new,
    )


def solution(mesh):
    placed = (
        P("dp", None),
        P("dp", None),
        P("dp", None, None),
        P("dp"),
        P("dp"),
        P("dp"),
        P("dp", None),
        P(None, "dp", "tensor"),
        P(None, "dp", "tensor"),
        P(None, "dp", "tensor"),
        P(None, "dp", "tensor"),
        P(None, "dp", "tensor"),
        P(None, "dp", "tensor"),
        P("tensor"),
        P("tensor"),
        P("tensor"),
        P(),
        P(),
        P(),
        P(None, "dp", None),
        P(None, "dp", None),
        P(None, "dp", None),
    )
    return jax.shard_map(
        shards,
        mesh=mesh,
        in_specs=placed,
        out_specs=(
            P("dp", None),
            P("dp", None),
            P(),
            P(None, "dp", "tensor"),
            P(None, "dp", "tensor"),
            P(None, "dp", "tensor"),
            P(None, "dp", "tensor"),
            P(None, "dp", "tensor"),
            P(None, "dp", "tensor"),
            P("tensor"),
            P("tensor"),
            P("tensor"),
            P(),
            P(),
            P(),
            P(None, "dp", None),
            P(None, "dp", None),
            P(None, "dp", None),
        ),
        check_vma=False,
    )
```

```python
import functools
import math

import jax
import jax.numpy as jnp
from jax import lax
from jax.experimental import pallas as pl
from jax.experimental.pallas import tpu as pltpu
from jax.sharding import PartitionSpec as P

D = 1152
HEADS = 16
TFREQ = 256
FRAMES = 16
OPT_STEP = 10


HIGHEST = lax.Precision.HIGHEST
BETA_ONE = 0.9
BETA_TWO = 0.999
EPSILON = 1e-08
DECAY_RATE = 0.01
CLIP_NORM = 1.0
RATE_MATRIX = 0.02
RATE_TIME = 0.05
RATE_VECTOR = 0.3


def alpha_bar():
    steps = jnp.arange(1000).astype(jnp.float32)
    betas = 0.0001 + (0.02 - 0.0001) * steps / 999.0
    return jnp.exp(jnp.cumsum(jnp.log(1.0 - betas)))


def pick_rows(table, indices):
    spots = jnp.arange(table.shape[0])
    return jnp.sum(jnp.where(spots[None, :] == indices[:, None], table[None, :], 0.0), axis=1)


def time_features(indices):
    half = TFREQ // 2
    freqs = jnp.exp(-math.log(10000.0) * jnp.arange(half).astype(jnp.float32) / half)
    angles = indices.astype(jnp.float32)[:, None] * freqs[None, :]
    return jnp.concatenate([jnp.cos(angles), jnp.sin(angles)], axis=1)


def layer_parts(values):
    centered = values - jnp.mean(values, axis=-1, keepdims=True)
    inverse = lax.rsqrt(jnp.mean(centered * centered, axis=-1, keepdims=True) + 1e-06)
    return (centered * inverse, inverse)


def norm_back(grad_out, normed, inverse):
    first_mean = jnp.mean(grad_out, axis=-1, keepdims=True)
    second_mean = jnp.mean(grad_out * normed, axis=-1, keepdims=True)
    return inverse * (grad_out - first_mean - normed * second_mean)


def gelu_tanh(upper):
    return (
        0.5
        * upper
        * (1.0 + jnp.tanh(0.7978845608028654 * (upper + 0.044715 * upper * upper * upper)))
    )


def gelu_slope(upper):
    tangent = jnp.tanh(0.7978845608028654 * (upper + 0.044715 * upper * upper * upper))
    inner = 0.7978845608028654 * (1.0 + 3.0 * 0.044715 * upper * upper)
    return 0.5 * (1.0 + tangent) + 0.5 * upper * (1.0 - tangent * tangent) * inner


def log_total(scores):
    peak = jnp.max(scores, axis=-1, keepdims=True)
    return peak + jnp.log(jnp.sum(jnp.exp(scores - peak), axis=-1, keepdims=True))


def softmax_back(probs, grad_probs):
    return probs * (grad_probs - jnp.sum(probs * grad_probs, axis=-1, keepdims=True))


def adamw(weight, first, second, grad, factor, rate):
    clipped = grad * factor
    first = BETA_ONE * first + (1.0 - BETA_ONE) * clipped
    second = BETA_TWO * second + (1.0 - BETA_TWO) * clipped * clipped
    first_hat = first / (1.0 - BETA_ONE**OPT_STEP)
    second_hat = second / (1.0 - BETA_TWO**OPT_STEP)
    weight = weight - rate * (first_hat / (jnp.sqrt(second_hat) + EPSILON) + DECAY_RATE * weight)
    return (weight, first, second)


def row_layout():
    return (1, jnp.int32(0))


def row_total(term_fn, total_rows):
    return lax.psum(term_fn(0, total_rows), "tensor")


def clip_totals(modul_terms, bias_terms):
    return (modul_terms, bias_terms)


def plain_shards(
    latent,
    noise,
    text,
    tsteps,
    clip_count,
    text_len,
    cotangent,
    attn_w,
    attn_m,
    attn_v,
    mlp_w,
    mlp_m,
    mlp_v,
    up_bias,
    up_m,
    up_v,
    side_vec,
    side_m,
    side_v,
    time_w,
    time_m,
    time_v,
):
    low_type = jnp.bfloat16
    full_type = jnp.float32
    n_tensor = lax.axis_size("tensor")
    n_data = lax.axis_size("dp")
    clips, tlen, width = text.shape
    row_count = latent.shape[0]
    seq_rows = row_count // clips
    seqs = row_count // FRAMES
    head_width = D // HEADS
    scale = head_width ** (-0.5)
    w_attn, w_mlp, w_time = (
        lax.all_gather(attn_w.astype(low_type), "dp", axis=1, tiled=True),
        lax.all_gather(mlp_w.astype(low_type), "dp", axis=1, tiled=True),
        lax.all_gather(time_w.astype(low_type), "dp", axis=1, tiled=True),
    )
    device_local = w_attn.shape[2]
    heads_here = device_local // head_width
    pieces, part = row_layout()
    share = row_count // pieces
    row_ids = jnp.arange(share)
    select = (row_ids[:, None] // seq_rows == jnp.arange(clips)[None, :]).astype(full_type)

    def per_row(values):
        return jnp.tensordot(select, values, axes=1, precision=HIGHEST)

    def per_clip(values):
        return jnp.tensordot(select.T, values, axes=1, precision=HIGHEST)

    abar = pick_rows(alpha_bar(), tsteps)
    keep_root = jnp.sqrt(abar)[:, None, None]
    noise_root = jnp.sqrt(1.0 - abar)[:, None, None]
    start = keep_root * latent.astype(full_type).reshape(
        clips, seq_rows, width
    ) + noise_root * noise.astype(full_type).reshape(clips, seq_rows, width)
    feats = jax.nn.silu(time_features(tsteps)).astype(low_type)
    modul = side_vec[3:][None] + jnp.einsum(
        "cf,jfd->cjd", feats, w_time, preferred_element_type=full_type
    )
    live_clip = (jnp.arange(clips) < clip_count[0]).astype(full_type)
    live = live_clip[:, None, None]
    mod_rows = per_row(modul)
    live_rows = per_row(live_clip)[:, None]
    root_rows = per_row(jnp.sqrt(abar))[:, None]
    normed_one, inverse_one = layer_parts(start)
    hidden_one = (
        (normed_one * (1.0 + modul[:, 1:2]) + modul[:, 0:1])
        .astype(low_type)
        .reshape(row_count, width)
    )
    projected = jnp.einsum(
        "rd,kde->kre", hidden_one, w_attn[0:3], preferred_element_type=full_type
    ).astype(low_type)
    shaped = projected.reshape(3, seqs, FRAMES, heads_here, head_width)
    self_scores = (
        jnp.einsum("sfhd,sghd->shfg", shaped[0], shaped[1], preferred_element_type=full_type)
        * scale
    )
    self_log = log_total(self_scores)
    self_probs = jnp.exp(self_scores - self_log).astype(low_type)
    mixed_one = (
        jnp.einsum("shfg,sghd->sfhd", self_probs, shaped[2], preferred_element_type=full_type)
        .astype(low_type)
        .reshape(row_count, device_local)
    )

    def self_out(begin, count):
        return jnp.einsum("re,oe->ro", mixed_one, w_attn[3], preferred_element_type=full_type)

    attended = row_total(self_out, row_count) + side_vec[0]
    start_rows = start.reshape(row_count, width)
    middle = start_rows + mod_rows[:, 2] * attended
    query_in = middle.astype(low_type)
    cross_query = jnp.dot(query_in, w_attn[4], preferred_element_type=full_type).astype(low_type)
    text_proj = jnp.einsum(
        "cld,kde->kcle", text, w_attn[5:7], preferred_element_type=full_type
    ).astype(low_type)
    query_heads = cross_query.reshape(clips, seq_rows, heads_here, head_width)
    text_heads = text_proj.reshape(2, clips, tlen, heads_here, head_width)
    allowed = (jnp.arange(tlen)[None, :] < text_len[:, None])[:, None, None, :]
    cross_scores = jnp.where(
        allowed,
        jnp.einsum("cqhd,ckhd->chqk", query_heads, text_heads[0], preferred_element_type=full_type)
        * scale,
        -1e30,
    )
    cross_log = log_total(cross_scores)
    cross_probs = jnp.exp(cross_scores - cross_log).astype(low_type)
    mixed_two = (
        jnp.einsum("chqk,ckhd->cqhd", cross_probs, text_heads[1], preferred_element_type=full_type)
        .astype(low_type)
        .reshape(row_count, device_local)
    )

    def cross_out(begin, count):
        return jnp.einsum("re,oe->ro", mixed_two, w_attn[7], preferred_element_type=full_type)

    crossed = row_total(cross_out, row_count) + side_vec[1]
    after = middle + crossed
    normed_two, inverse_two = layer_parts(after)
    hidden_two = (normed_two * (1.0 + mod_rows[:, 4]) + mod_rows[:, 3]).astype(low_type)
    upper = jnp.dot(hidden_two, w_mlp[0], preferred_element_type=full_type) + up_bias
    activated = gelu_tanh(upper).astype(low_type)

    def down_out(begin, count):
        return jnp.einsum("rf,of->ro", activated, w_mlp[1], preferred_element_type=full_type)

    mlp_out = row_total(down_out, row_count) + side_vec[2]
    final = after + mod_rows[:, 5] * mlp_out
    block_out = (live_rows * final).astype(low_type)
    grad_four = live_rows * cotangent.astype(full_type)
    d_gate_two = per_clip(grad_four * mlp_out)
    d_mlp_full = (
        modul[:, 5:6] * live * cotangent.astype(full_type).reshape(clips, seq_rows, width)
    ).reshape(row_count, width)
    d_bias_two = jnp.sum(d_mlp_full, axis=0)
    d_mlp_low = d_mlp_full.astype(low_type)
    grad_down = jnp.einsum("ro,rf->of", d_mlp_low, activated, preferred_element_type=full_type)
    d_act = jnp.einsum("ro,of->rf", d_mlp_low, w_mlp[1], preferred_element_type=full_type)
    d_upper = (d_act * gelu_slope(upper)).astype(low_type)
    grad_upbias = jnp.sum(d_upper.astype(full_type), axis=0)
    grad_up = jnp.einsum("rd,rf->df", hidden_two, d_upper, preferred_element_type=full_type)
    grad_mlp = jnp.stack([grad_up, grad_down])

    def up_back(begin, count):
        return jnp.einsum("rf,df->rd", d_upper, w_mlp[0], preferred_element_type=full_type)

    d_hidden_two = row_total(up_back, row_count)
    d_shift_two = per_clip(d_hidden_two)
    d_scale_two = per_clip(d_hidden_two * normed_two)
    grad_three = grad_four + norm_back(
        d_hidden_two * (1.0 + mod_rows[:, 4]), normed_two, inverse_two
    )
    d_bias_one = jnp.sum(grad_three, axis=0)
    d_cross_low = grad_three.astype(low_type)
    grad_cout = jnp.einsum("ro,re->oe", d_cross_low, mixed_two, preferred_element_type=full_type)
    d_mixed_two = (
        jnp.einsum("ro,oe->re", d_cross_low, w_attn[7], preferred_element_type=full_type)
        .astype(low_type)
        .reshape(clips, seq_rows, heads_here, head_width)
    )
    cross_again = jnp.where(
        allowed,
        jnp.einsum("cqhd,ckhd->chqk", query_heads, text_heads[0], preferred_element_type=full_type)
        * scale,
        -1e30,
    )
    cross_full = jnp.exp(cross_again - cross_log)
    d_cprobs = jnp.einsum(
        "cqhd,ckhd->chqk", d_mixed_two, text_heads[1], preferred_element_type=full_type
    )
    d_cvalues = jnp.einsum(
        "chqk,cqhd->ckhd",
        cross_full.astype(low_type),
        d_mixed_two,
        preferred_element_type=full_type,
    ).astype(low_type)
    d_cscores = softmax_back(cross_full, d_cprobs).astype(low_type)
    d_cquery = (
        (
            jnp.einsum(
                "chqk,ckhd->cqhd", d_cscores, text_heads[0], preferred_element_type=full_type
            )
            * scale
        )
        .astype(low_type)
        .reshape(row_count, device_local)
    )
    d_ckeys = (
        jnp.einsum("chqk,cqhd->ckhd", d_cscores, query_heads, preferred_element_type=full_type)
        * scale
    ).astype(low_type)
    d_text_proj = jnp.stack([d_ckeys, d_cvalues]).reshape(2, clips * tlen, device_local)
    grad_cquery = jnp.einsum("rd,re->de", query_in, d_cquery, preferred_element_type=full_type)
    grad_ctext = jnp.einsum(
        "rd,kre->kde",
        text.reshape(clips * tlen, width),
        d_text_proj,
        preferred_element_type=full_type,
    )

    def cquery_back(begin, count):
        return jnp.einsum("re,de->rd", d_cquery, w_attn[4], preferred_element_type=full_type)

    grad_two = grad_three + row_total(cquery_back, row_count)
    d_gate_one = per_clip(grad_two * attended)
    d_attended = mod_rows[:, 2] * grad_two
    d_bias_zero = jnp.sum(d_attended, axis=0)
    d_att_low = d_attended.astype(low_type)
    grad_sout = jnp.einsum("ro,re->oe", d_att_low, mixed_one, preferred_element_type=full_type)
    d_mixed_one = (
        jnp.einsum("ro,oe->re", d_att_low, w_attn[3], preferred_element_type=full_type)
        .astype(low_type)
        .reshape(seqs, FRAMES, heads_here, head_width)
    )
    self_again = (
        jnp.einsum("sfhd,sghd->shfg", shaped[0], shaped[1], preferred_element_type=full_type)
        * scale
    )
    self_full = jnp.exp(self_again - self_log)
    d_sprobs = jnp.einsum(
        "sfhd,sghd->shfg", d_mixed_one, shaped[2], preferred_element_type=full_type
    )
    self_value_gradient = jnp.einsum(
        "shfg,sfhd->sghd", self_full.astype(low_type), d_mixed_one, preferred_element_type=full_type
    ).astype(low_type)
    d_sscores = softmax_back(self_full, d_sprobs).astype(low_type)
    self_query_gradient = (
        jnp.einsum("shfg,sghd->sfhd", d_sscores, shaped[1], preferred_element_type=full_type)
        * scale
    ).astype(low_type)
    self_key_gradient = (
        jnp.einsum("shfg,sfhd->sghd", d_sscores, shaped[0], preferred_element_type=full_type)
        * scale
    ).astype(low_type)
    projection_gradient = jnp.stack(
        [self_query_gradient, self_key_gradient, self_value_gradient]
    ).reshape(3, row_count, device_local)
    grad_qkv = jnp.einsum(
        "rd,kre->kde", hidden_one, projection_gradient, preferred_element_type=full_type
    )

    def qkv_back(begin, count):
        return jnp.einsum(
            "kre,kde->rd", projection_gradient, w_attn[0:3], preferred_element_type=full_type
        )

    d_hidden_one = row_total(qkv_back, row_count)
    normed_one_rows = normed_one.reshape(row_count, width)
    inverse_one_rows = inverse_one.reshape(row_count, 1)
    d_shift_one = per_clip(d_hidden_one)
    d_scale_one = per_clip(d_hidden_one * normed_one_rows)
    grad_one = grad_two + norm_back(
        d_hidden_one * (1.0 + mod_rows[:, 1]), normed_one_rows, inverse_one_rows
    )
    latent_grad = root_rows * grad_one
    d_modul_part = jnp.stack(
        [d_shift_one, d_scale_one, d_gate_one, d_shift_two, d_scale_two, d_gate_two], axis=1
    )
    bias_part = jnp.stack([d_bias_zero, d_bias_one, d_bias_two])
    d_modul, bias_three = clip_totals(d_modul_part, bias_part)
    grad_time = jnp.einsum("cf,cjd->jfd", feats.astype(full_type), d_modul, precision=HIGHEST)
    grad_side = jnp.concatenate([bias_three, jnp.sum(d_modul, axis=0)], axis=0)
    grad_attn = jnp.concatenate(
        [grad_qkv, grad_sout[None], grad_cquery[None], grad_ctext, grad_cout[None]], axis=0
    )
    attn_shard, mlp_shard, time_shard = (
        lax.psum_scatter(grad_attn, "dp", scatter_dimension=1, tiled=True),
        lax.psum_scatter(grad_mlp, "dp", scatter_dimension=1, tiled=True),
        lax.psum_scatter(grad_time, "dp", scatter_dimension=1, tiled=True),
    )
    side_total, upbias_total = lax.psum((grad_side, grad_upbias), "dp")
    squared_terms = jnp.sum(attn_shard * attn_shard) + jnp.sum(mlp_shard * mlp_shard)
    squared_terms = squared_terms + jnp.sum(time_shard * time_shard) / n_tensor
    squared_terms = squared_terms + jnp.sum(upbias_total * upbias_total) / n_data
    squared_terms = squared_terms + jnp.sum(side_total * side_total) / (n_data * n_tensor)
    grad_norm = jnp.sqrt(lax.psum(squared_terms, ("dp", "tensor")))
    factor = jnp.minimum(1.0, CLIP_NORM / (grad_norm + 1e-06))
    attn_new, attn_m_new, attn_v_new = adamw(
        attn_w, attn_m, attn_v, attn_shard, factor, RATE_MATRIX
    )
    mlp_new, mlp_m_new, mlp_v_new = adamw(mlp_w, mlp_m, mlp_v, mlp_shard, factor, RATE_MATRIX)
    up_new, up_m_new, up_v_new = adamw(up_bias, up_m, up_v, upbias_total, factor, RATE_VECTOR)
    side_new, side_m_new, side_v_new = adamw(
        side_vec, side_m, side_v, side_total, factor, RATE_VECTOR
    )
    time_new, time_m_new, time_v_new = adamw(time_w, time_m, time_v, time_shard, factor, RATE_TIME)
    return (
        block_out,
        latent_grad,
        grad_norm,
        attn_new,
        attn_m_new,
        attn_v_new,
        mlp_new,
        mlp_m_new,
        mlp_v_new,
        up_new,
        up_m_new,
        up_v_new,
        side_new,
        side_m_new,
        side_v_new,
        time_new,
        time_m_new,
        time_v_new,
    )


MESH = pl.DeviceIdType.MESH
LOW = jnp.bfloat16
FULL = jnp.float32
TILE = 384


def dot(left, right, left_dim, right_dim):
    return lax.dot_general(
        left, right, (((left_dim,), (right_dim,)), ((), ())), preferred_element_type=FULL
    )


def ring_place(index, count):
    z, x = lax.div(index, 2), lax.rem(index, 2)
    return z + x * (count - 1 - 2 * z)


def ring_index(place, count):
    high = lax.div(place, count // 2)
    return 2 * (place + high * (count - 1 - 2 * place)) + high


def ring_items(count):
    right, left = [], []
    for hop in range(1, count // 2 + 1):
        for half in (0, 1):
            if hop <= count // 2 - half:
                right.append((half, hop))
                left.append((1 - half, hop))
    return right, left


def flip(items):
    return [(1 - half, hop) for half, hop in items]


class Ring:
    def __init__(self, count, rows, dp, tensor):
        self.count, self.rows = count, rows
        self.lead = -(-rows // 32) * 16
        right, left = ring_items(count)
        self.both = [(right, left), (flip(right), flip(left))]
        self.place = ring_place(dp, count)
        self.sides = [
            (ring_index(lax.rem(self.place + step, count), count), tensor)
            for step in (1, count - 1)
        ]
        self.steps = count - 1
        self.queue = []

    def half_rows(self, half):
        return (0, self.lead) if half == 0 else (self.lead, self.rows - self.lead)

    def block_rows(self, offset, half):
        index = ring_index(lax.rem(self.place + offset + 2 * self.count, self.count), self.count)
        begin, size = self.half_rows(half)
        return pl.ds(pl.multiple_of(index * self.rows + begin, 16), size)

    def pump(self, times):
        for _ in range(min(times, len(self.queue))):
            self.queue.pop(0)[0]()


class Gather(Ring):
    def __init__(self, count, rows, dp, tensor, full, send, recv):
        super().__init__(count, rows, dp, tensor)
        self.full, self.send, self.recv = full, send, recv
        self.copies = {}
        panels = full.shape[0]
        self.left = {panel: self.steps for panel in range(panels)}
        first = min(2, self.steps)
        order = [(panel, step) for panel in range(min(2, panels)) for step in range(first)]
        for panel in range(panels):
            order += [(panel, step) for step in range(first, self.steps)]
            if panel + 2 < panels:
                order += [(panel + 2, step) for step in range(first)]
        for panel, step in order:
            self.queue.append((functools.partial(self.step, panel, step), None))

    def copy(self, panel, step, side):
        half, hop = self.both[panel % 2][side][step]
        sign = 1 if side == 0 else -1
        target = self.full.at[panel, self.block_rows(-sign * (hop - 1), half)]
        return pltpu.make_async_remote_copy(
            src_ref=target,
            dst_ref=target,
            send_sem=self.send.at[side, panel, step],
            recv_sem=self.recv.at[side, panel, step],
            device_id=self.sides[side],
            device_id_type=MESH,
        )

    def arrived(self, panel, step, side):
        half, hop = self.both[panel % 2][side][step]
        sign = 1 if side == 0 else -1
        here = self.full.at[panel, self.block_rows(-sign * hop, half)]
        pltpu.make_async_remote_copy(
            src_ref=here,
            dst_ref=here,
            send_sem=self.send.at[side, panel, step],
            recv_sem=self.recv.at[side, panel, step],
            device_id=self.sides[side],
            device_id_type=MESH,
        ).wait_recv()

    def step(self, panel, step):
        for side in (0, 1):
            if step >= 2:
                self.arrived(panel, step - 2, side)
            copy = self.copy(panel, step, side)
            copy.start()
            self.copies[side, panel, step] = copy
        self.left[panel] -= 1

    def finish(self, panel):
        while self.left[panel]:
            self.pump(1)
        self.pump(3)
        for step in range(max(0, self.steps - 2), self.steps):
            for side in (0, 1):
                self.arrived(panel, step, side)

    def drain(self, panel):
        for key, copy in self.copies.items():
            if key[1] == panel:
                copy.wait_send()


class Reduce(Ring):
    def __init__(self, count, rows, dp, tensor, part, slots, store, free, send, recv):
        super().__init__(count, rows, dp, tensor)
        self.part, self.slots, self.store, self.free = part, slots, store, free
        self.send, self.recv = send, recv
        self.copies = {}
        self.last = None

    def reach(self, panel, side, half):
        return max(hop for kind, hop in self.both[panel % 2][side] if kind == half)

    def copy(self, panel, step, side):
        half, hop = self.both[panel % 2][side][step]
        size = self.half_rows(half)[1]
        if hop == 1:
            sign = 1 if side == 0 else -1
            offset = sign * self.reach(panel, side, half)
            source = self.part[panel].at[self.block_rows(offset, half)]
        else:
            source = self.slots.at[side, panel % 2, step - 2, pl.ds(0, size)]
        return pltpu.make_async_remote_copy(
            src_ref=source,
            dst_ref=self.slots.at[side, panel % 2, step, pl.ds(0, size)],
            send_sem=self.send.at[side, panel, step],
            recv_sem=self.recv.at[side, panel, step],
            device_id=self.sides[side],
            device_id_type=MESH,
        )

    def step(self, panel, step):
        if step == 0 and panel < 2:
            pl.semaphore_wait(self.free.at[panel], 2)
        for side in (0, 1):
            half, hop = self.both[panel % 2][side][step]
            if hop > 1:
                self.copies[side, panel, step - 2].wait_recv()
                sign = 1 if side == 0 else -1
                offset = sign * (self.reach(panel, side, half) + 1 - hop)
                size = self.half_rows(half)[1]
                slot = self.slots.at[side, panel % 2, step - 2, pl.ds(0, size)]
                slot[...] = (
                    slot[...].astype(FULL)
                    + self.part[panel][self.block_rows(offset, half), :].astype(FULL)
                ).astype(LOW)
            copy = self.copy(panel, step, side)
            copy.start()
            self.copies[side, panel, step] = copy

    def add_panel(self, panel):
        first = min(2, self.steps)
        names = [name for _, name in self.queue]
        at = names.index(panel + 2) + 1 if panel + 2 in names else 0
        for step in range(first):
            self.queue.insert(at + step, (functools.partial(self.step, panel, step), None))
        finish = [] if self.last is None else [(functools.partial(self.finish, self.last), self.last)]
        rest = [(functools.partial(self.step, panel, step), None) for step in range(first, self.steps)]
        self.queue += rest[:1] + finish + rest[1:]
        self.last = panel

    def finish(self, panel):
        for step in range(max(0, self.steps - 2), self.steps):
            for side in (0, 1):
                self.copies[side, panel, step].wait_recv()
        for half in (0, 1):
            begin, size = self.half_rows(half)
            value = self.part[panel][self.block_rows(0, half), :].astype(FULL)
            for side in (0, 1):
                spots = [s for s, item in enumerate(self.both[panel % 2][side]) if item[0] == half]
                if spots:
                    value = value + self.slots[side, panel % 2, spots[-1], pl.ds(0, size), :].astype(FULL)
            self.store(panel, pl.ds(begin, size), value)
        for key, copy in self.copies.items():
            if key[1] == panel:
                copy.wait_send()
        if panel >= 2:
            for neighbour in self.sides:
                pl.semaphore_signal(
                    self.free.at[panel - 2], inc=1, device_id=neighbour, device_id_type=MESH
                )

    def complete(self):
        self.pump(len(self.queue))
        self.finish(self.last)


class Sum:
    def __init__(self, place, part, near, out, far, sems):
        self.place, self.part, self.near, self.out, self.far, self.sems = place, part, near, out, far, sems

    def start(self):
        dp, me, mate, across, beyond, rows = self.place
        self.copies = []
        for spot, block in enumerate((mate, beyond)):
            copy = pltpu.make_async_remote_copy(
                src_ref=self.part.at[pl.ds(pl.multiple_of(block * rows, 16), rows)],
                dst_ref=self.near.at[spot],
                send_sem=self.sems.at[spot],
                recv_sem=self.sems.at[3 + spot],
                device_id=(dp, mate),
                device_id_type=MESH,
            )
            copy.start()
            self.copies.append(copy)

    def middle(self):
        dp, me, mate, across, beyond, rows = self.place
        for copy in self.copies:
            copy.wait()
        block = pl.ds(pl.multiple_of(across * rows, 16), rows)
        self.out[...] = (self.part[block, :] + self.near[1]).astype(LOW)
        self.last = pltpu.make_async_remote_copy(
            src_ref=self.out,
            dst_ref=self.far,
            send_sem=self.sems.at[2],
            recv_sem=self.sems.at[5],
            device_id=(dp, across),
            device_id_type=MESH,
        )
        self.last.start()

    def end(self):
        dp, me, mate, across, beyond, rows = self.place
        self.last.wait()
        block = pl.ds(pl.multiple_of(me * rows, 16), rows)
        return self.part[block, :] + self.near[0] + self.far[...].astype(FULL)


class Share:
    def __init__(self, place, full, sems):
        self.place, self.full, self.sems = place, full, sems

    def rows(self, block):
        rows = self.place[5]
        return self.full.at[pl.ds(pl.multiple_of(block * rows, 16), rows)]

    def copy(self, block, target, spot):
        return pltpu.make_async_remote_copy(
            src_ref=self.rows(block),
            dst_ref=self.rows(block),
            send_sem=self.sems.at[spot],
            recv_sem=self.sems.at[3 + spot],
            device_id=(self.place[0], target),
            device_id_type=MESH,
        )

    def start(self):
        dp, me, mate, across, beyond, rows = self.place
        self.far = self.copy(me, across, 0)
        self.near = self.copy(me, mate, 1)
        self.far.start()
        self.near.start()

    def middle(self):
        dp, me, mate, across, beyond, rows = self.place
        self.far.wait()
        self.onward = self.copy(across, mate, 2)
        self.onward.start()

    def end(self):
        self.near.wait()
        self.onward.wait()


def row_norm(values):
    centered = values - jnp.mean(values, axis=-1, keepdims=True)
    inverse = lax.rsqrt(jnp.mean(centered * centered, axis=-1, keepdims=True) + 1e-06)
    return centered * inverse, inverse


def block_kernel(
    n_data,
    n_tensor,
    clips,
    tsteps,
    clip_count,
    text_len,
    latent_in,
    noise_in,
    cot_in,
    text_in,
    attn_in,
    attn_m_in,
    attn_v_in,
    mlp_in,
    mlp_m_in,
    mlp_v_in,
    time_in,
    time_m_in,
    time_v_in,
    up_bias,
    side,
    attn_w,
    attn_m,
    attn_v,
    grad_attn,
    mlp_w,
    mlp_m,
    mlp_v,
    grad_mlp,
    time_map,
    time_m,
    time_v,
    grad_time,
    final,
    latent_grad,
    grad_up,
    grad_side,
    square_sum,
    latent,
    noise,
    cot,
    text,
    weights,
    part_down,
    slots,
    feats,
    feats_all,
    modul_out,
    modul_in,
    modul,
    hidden_one,
    heads_one,
    probs_one,
    mixed_one,
    heads_two,
    text_heads,
    probs_two,
    mixed_two,
    shared,
    activated,
    slope,
    d_upper,
    d_heads,
    d_text,
    sums,
    near,
    out,
    far,
    own,
    inverses,
    small,
    small_all,
    totals,
    totals_all,
    up_row,
    up_all,
    norms,
    norms_all,
    splits,
    squares,
    load_sems,
    moment_sems,
    free,
    gather_send,
    gather_recv,
    reduce_send,
    reduce_recv,
    sum_sems,
    share_sems,
    feat_sems,
    modul_sems,
    modul_share_sems,
    small_sems,
    total_sems,
    up_sems,
    total_share_sems,
    norm_sems,
    norm_share_sems,
):
    dp, me = lax.axis_index("dp"), lax.axis_index("tensor")
    loads = [
        pltpu.make_async_copy(source, target, load_sems.at[k])
        for k, (source, target) in enumerate(
            (
                (attn_in, attn_w),
                (mlp_in, mlp_w),
                (time_in, time_map),
                (latent_in, latent),
                (noise_in, noise),
                (cot_in, cot),
                (text_in, text),
            )
        )
    ]
    for load in loads:
        load.start()
    moments = [
        pltpu.make_async_copy(source, target, moment_sems.at[k])
        for k, (source, target) in enumerate(
            (
                (attn_m_in, attn_m),
                (attn_v_in, attn_v),
                (mlp_m_in, mlp_m),
                (mlp_v_in, mlp_v),
                (time_m_in, time_m),
                (time_v_in, time_v),
            )
        )
    ]
    d_mlp = noise

    rows, width = latent.shape
    clip_rows = rows // clips
    own_rows = rows // n_tensor
    per_clip = n_tensor // clips
    head_width = width // HEADS
    local = width // n_tensor
    heads = local // head_width
    scale = head_width ** (-0.5)
    tlen = text.shape[0] // clips
    mate = me + 1 - 2 * lax.rem(me, 2)
    across = lax.rem(me + 2, n_tensor)
    beyond = lax.rem(mate + 2, n_tensor)
    place = (dp, me, mate, across, beyond, own_rows)
    data_peers = [lax.rem(dp + k, n_data) for k in range(1, n_data)]
    tensor_peers = [lax.rem(me + k, n_tensor) for k in range(1, n_tensor)]
    mine = pl.ds(pl.multiple_of(me * own_rows, 16), own_rows)

    barrier = pltpu.get_barrier_semaphore()
    for peer in data_peers:
        pl.semaphore_signal(barrier, inc=1, device_id=(peer, me), device_id_type=MESH)
    for peer in tensor_peers:
        pl.semaphore_signal(barrier, inc=1, device_id=(dp, peer), device_id_type=MESH)

    table_step = 128 * lax.broadcasted_iota(jnp.int32, (8, 128), 0) + lax.broadcasted_iota(jnp.int32, (8, 128), 1)
    betas = 0.0001 + (0.02 - 0.0001) * table_step.astype(FULL) / 999.0
    logs = jnp.log(1.0 - jnp.where(table_step < 1000, betas, 0.0))

    def abar_of(clip):
        chosen = jnp.where(table_step <= tsteps[clip], logs, 0.0)
        return jnp.exp(jnp.sum(jnp.sum(chosen, axis=0, keepdims=True), axis=1, keepdims=True))

    def live_of(clip):
        return jnp.where(clip < clip_count[0], 1.0, 0.0)

    half = TFREQ // 2
    freqs = jnp.exp(
        -math.log(10000.0) * lax.broadcasted_iota(jnp.int32, (1, half), 1).astype(FULL) / half
    )
    lines = []
    for clip in range(clips):
        angles = tsteps[clip].astype(FULL) * freqs
        lines.append(jnp.concatenate([jnp.cos(angles), jnp.sin(angles)], axis=1))
    lines = jnp.concatenate(lines, axis=0)
    lines = lines / (1.0 + jnp.exp(-lines))
    feats[...] = jnp.concatenate([lines, jnp.zeros((feats.shape[0] - clips, TFREQ), FULL)], axis=0).astype(LOW)

    def send_all(source_of, target, sems, along):
        copies = []
        peers = data_peers if along == "dp" else tensor_peers
        for k, peer in enumerate(peers):
            copy = pltpu.make_async_remote_copy(
                src_ref=source_of(peer),
                dst_ref=target,
                send_sem=sems.at[0, k],
                recv_sem=sems.at[1, k],
                device_id=(peer, me) if along == "dp" else (dp, peer),
                device_id_type=MESH,
            )
            copy.start()
            copies.append(copy)
        return copies

    def wait_all(copies):
        for copy in copies:
            copy.wait()

    panel_rows = mlp_w.shape[1]

    def store_grad(panel, block, value):
        squares[...] += jnp.sum(value * value, axis=0, keepdims=True)
        if panel >= 2:
            grad_mlp[panel - 2, block, :] = value
        else:
            for k in range(4):
                grad_attn[4 * panel + k, block, :] = value[:, k * local : (k + 1) * local]

    gather = Gather(n_data, panel_rows, dp, me, weights, gather_send, gather_recv)
    parts = [weights.at[0], weights.at[1], weights.at[2], part_down]
    reduce = Reduce(n_data, panel_rows, dp, me, parts, slots, store_grad, free, reduce_send, reduce_recv)
    own_panel = pl.ds(pl.multiple_of(dp * panel_rows, 16), panel_rows)

    def pack(panel):
        if panel >= 2:
            weights[panel, own_panel, :] = mlp_w[panel - 2].astype(LOW)
        else:
            weights[panel, own_panel, :] = jnp.concatenate(
                [attn_w[4 * panel + k] for k in range(4)], axis=1
            ).astype(LOW)

    loads[0].wait()
    pack(0)
    pl.semaphore_wait(barrier, n_data + n_tensor - 2)
    feats_all[dp] = feats[...]
    feat_copies = send_all(lambda peer: feats, feats_all.at[dp], feat_sems, "dp")
    gather.pump(min(2, n_data - 1))
    pack(1)
    gather.pump(min(2, n_data - 1))
    loads[1].wait()
    pack(2)
    pack(3)

    n_feats = time_map.shape[1]
    feat_rows, n_freq = feats.shape
    modul_share = clips * 6 // n_tensor
    loads[2].wait()
    wait_all(feat_copies)
    pick = (
        lax.broadcasted_iota(jnp.int32, (n_freq, n_feats), 0)
        == lax.broadcasted_iota(jnp.int32, (n_freq, n_feats), 1) + n_feats * dp
    ).astype(FULL).astype(LOW)
    feats_flat = feats_all[...].reshape(n_data * feat_rows, n_freq)
    feats_mine = dot(feats_flat, pick, 1, 0).astype(LOW)
    my_clip = lax.div(me, per_clip)
    first = modul_share * lax.rem(me, per_clip)
    rows_of_clip = (
        lax.broadcasted_iota(jnp.int32, (n_data, n_data * feat_rows), 1)
        == feat_rows * lax.broadcasted_iota(jnp.int32, (n_data, n_data * feat_rows), 0) + my_clip
    ).astype(FULL).astype(LOW)
    feats_clip = dot(rows_of_clip, feats_mine, 1, 0).astype(LOW)
    for k in range(modul_share):
        partial = dot(feats_clip, time_map[first + k].astype(LOW), 1, 0)
        for peer in range(n_data):
            modul_out[peer, k : k + 1, :] = partial[peer : peer + 1]
    for peer in range(n_data):
        modul_out[peer, modul_share:, :] = jnp.zeros((modul_out.shape[1] - modul_share, width), FULL)
    modul_in[dp] = modul_out[dp]
    modul_copies = send_all(lambda peer: modul_out.at[peer], modul_in.at[dp], modul_sems, "dp")
    gather.pump(1)
    lane = lax.broadcasted_iota(jnp.int32, (1, local), 1)
    head_masks = [
        ((lane >= h * head_width) & (lane < (h + 1) * head_width)).astype(FULL) for h in range(heads)
    ]
    wait_all(modul_copies)
    total = modul_in[0]
    for peer in range(1, n_data):
        total = total + modul_in[peer]
    chosen = jnp.where(lax.rem(me, per_clip) == 0, side[3 : 3 + modul_share, :], side[3 + modul_share : 9, :])
    modul[me] = jnp.concatenate(
        [total[0:modul_share] + chosen, total[modul_share:]], axis=0
    )
    modul_copies = send_all(lambda peer: modul.at[me], modul.at[me], modul_share_sems, "tensor")
    gather.pump(1)
    wait_all(modul_copies)

    def modul_row(clip, j):
        return modul[clip * per_clip + j // modul_share, pl.ds(j % modul_share, 1), :]

    def start_of(abar, block):
        return jnp.sqrt(abar) * latent[block, :].astype(FULL) + jnp.sqrt(1.0 - abar) * noise[
            block, :
        ].astype(FULL)

    for load in loads[3:6]:
        load.wait()

    step_rows = 32

    def first_norm(clip, abar, step, carry):
        block = pl.ds(pl.multiple_of(clip * clip_rows + step * step_rows, step_rows), step_rows)
        normed, _ = row_norm(start_of(abar, block))
        hidden_one[block, :] = (normed * (1.0 + modul_row(clip, 1)) + modul_row(clip, 0)).astype(LOW)
        return carry

    for clip in range(clips):
        lax.fori_loop(0, clip_rows // step_rows, functools.partial(first_norm, clip, abar_of(clip)), 0)
        gather.pump(1)
    clip_mine = lax.div(me, per_clip)
    abar_mine = abar_of(clip_mine)
    start_mine = start_of(abar_mine, mine)
    normed, inverse = row_norm(start_mine)
    own[0], own[1] = start_mine, normed
    inverses[0] = jnp.broadcast_to(inverse, (own_rows, 128))
    live_mine = live_of(clip_mine)
    for clip in range(clips):
        block = pl.ds(clip * clip_rows, clip_rows)
        d_mlp[block, :] = (modul_row(clip, 5) * live_of(clip) * cot[block, :].astype(FULL)).astype(LOW)
    gather.finish(0)
    for moment in moments:
        moment.start()

    self_cols = -(-3 * local // 128) * 128
    out_cols = 3 * local // 128 * 128
    out_pad = 3 * local - out_cols
    text_cols = local // 128 * 128
    text_pad = local - text_cols
    query_cols = -(-local // 128) * 128

    def split_heads(values, offsets, target, block):
        for k, offset in enumerate(offsets):
            target[k, block, :] = values[:, offset : offset + local].astype(LOW)

    def stacked(values):
        return jnp.concatenate([(values.astype(FULL) * mask).astype(LOW) for mask in head_masks], axis=0)

    def unstacked(values, size):
        total = values[0:size] * head_masks[0]
        for h in range(1, heads):
            total = total + values[h * size : (h + 1) * size] * head_masks[h]
        return total

    def attend(query, keys, values, allowed):
        scores = jnp.where(allowed, dot(stacked(query), keys, 1, 1) * scale, -1e30)
        expo = jnp.exp(scores - jnp.max(scores, axis=-1, keepdims=True))
        probs = expo / jnp.sum(expo, axis=-1, keepdims=True)
        return probs, unstacked(dot(probs.astype(LOW), values, 1, 0), clip_rows)

    def pad_left(values):
        return jnp.concatenate([jnp.zeros((values.shape[0], out_pad), FULL), values], axis=1).astype(LOW)

    def sum_of(index, buffer):
        return Sum(place, sums.at[buffer], near.at[index % 3], out.at[index % 3], far.at[index % 3], sum_sems.at[index])

    def columns(body, total):
        for begin in range(0, total, TILE):
            body(begin, min(TILE, total - begin))

    def product_nt(left, panel, begin, end, buffer):
        def tile(at, size):
            sums[buffer, :, at : at + size] = dot(left, weights[panel, at : at + size, begin:end], 1, 1)

        columns(tile, width)

    for block_at in range(0, rows, 128):
        block = pl.ds(block_at, 128)
        split_heads(
            dot(hidden_one[block, :], weights[0, :, 0:self_cols], 1, 0), (0, local, 2 * local), heads_one, block
        )
    gather.pump(1)
    size = heads * clip_rows
    frame_row = lax.broadcasted_iota(jnp.int32, (size, clip_rows), 0)
    frame_col = lax.broadcasted_iota(jnp.int32, (size, clip_rows), 1)
    frame_bits = FRAMES.bit_length() - 1
    same_sequence = ((frame_row & (clip_rows - 1)) >> frame_bits) == (frame_col >> frame_bits)
    for clip in range(clips):
        block = pl.ds(clip * clip_rows, clip_rows)
        probs, mixed = attend(heads_one[0, block, :], heads_one[1, block, :], heads_one[2, block, :], same_sequence)
        probs_one[clip] = probs
        mixed_one[block, :] = pad_left(mixed)
        gather.pump(1)
    product_nt(mixed_one[...], 0, out_cols, width, 0)
    self_sum = sum_of(0, 0)
    self_sum.start()
    gather.pump(1)
    self_sum.middle()
    gather.pump(1)

    def modul_mine(j):
        return modul[clip_mine * per_clip + j // modul_share, pl.ds(j % modul_share, 1), :]

    attended = self_sum.end() + side[0:1, :]
    own[2] = attended
    middle = own[0] + modul_mine(2) * attended
    own[0] = middle
    shared[0, mine, :] = middle.astype(LOW)
    share = Share(place, shared.at[0], share_sems.at[0])
    share.start()
    gather.pump(1)
    share.middle()
    gather.finish(1)

    loads[6].wait()
    for block_at in range(0, clips * tlen, 128):
        block = pl.ds(block_at, 128)
        split_heads(
            dot(text[block, :], weights[1, :, text_cols : text_cols + 5 * 128], 1, 0),
            (text_pad, text_pad + local),
            text_heads,
            block,
        )
    share.end()
    gather.pump(1)
    key_index = lax.broadcasted_iota(jnp.int32, (size, tlen), 1)
    heads_two[...] = dot(shared[0], weights[1, :, 0:query_cols], 1, 0)[:, 0:local].astype(LOW)
    for clip in range(clips):
        block = pl.ds(clip * clip_rows, clip_rows)
        words = pl.ds(clip * tlen, tlen)
        probs, mixed = attend(
            heads_two[block, :], text_heads[0, words, :], text_heads[1, words, :], key_index < text_len[clip]
        )
        probs_two[clip] = probs
        mixed_two[block, :] = pad_left(mixed)
        gather.pump(1)
    product_nt(mixed_two[...], 1, out_cols, width, 0)
    cross_sum = sum_of(1, 0)
    cross_sum.start()
    gather.pump(1)
    cross_sum.middle()
    gather.pump(1)
    after = own[0] + cross_sum.end() + side[1:2, :]
    own[0] = after
    normed, inverse = row_norm(after)
    own[3] = normed
    inverses[1] = jnp.broadcast_to(inverse, (own_rows, 128))
    shared[1, mine, :] = (normed * (1.0 + modul_mine(4)) + modul_mine(3)).astype(LOW)
    share = Share(place, shared.at[1], share_sems.at[1])
    share.start()
    gather.pump(1)
    share.middle()
    gather.finish(2)
    share.end()

    def up(at, size):
        cols = slice(at, at + size)
        upper = dot(shared[1], weights[2, :, cols], 1, 0) + up_bias[cols].reshape(1, size)
        tangent = jnp.tanh(0.7978845608028654 * (upper + 0.044715 * upper * upper * upper))
        inner = 0.7978845608028654 * (1.0 + 3.0 * 0.044715 * upper * upper)
        activated[:, cols] = (0.5 * upper * (1.0 + tangent)).astype(LOW)
        slope[:, cols] = 0.5 * (1.0 + tangent) + 0.5 * upper * (1.0 - tangent * tangent) * inner
        gather.pump(1)

    columns(up, width)

    def grad_tile(panel, left, right, at, size):
        cols = slice(at, at + size)
        parts[panel][:, cols] = dot(left, right[:, cols], 0, 0).astype(LOW)

    def grad_panel(panel, left, right):
        columns(functools.partial(grad_tile, panel, left, right), width)

    grad_panel(3, d_mlp[...], activated)
    gather.finish(3)
    reduce.add_panel(3)
    reduce.pump(2)

    small[...] = jnp.zeros_like(small)
    squares[...] = jnp.zeros_like(squares)

    def up_slope(at, size):
        cols = slice(at, at + size)
        value = (dot(d_mlp[...], weights[3, :, cols], 1, 0) * slope[:, cols]).astype(LOW)
        d_upper[:, cols] = value
        small[9:10, cols] = jnp.sum(value.astype(FULL), axis=0, keepdims=True)

    columns(up_slope, width)
    product_nt(d_upper[...], 2, 0, width, 0)
    hidden_sum = sum_of(2, 0)
    hidden_sum.start()
    gather.drain(2)
    grad_panel(2, shared[1], d_upper)
    reduce.add_panel(2)
    reduce.pump(2)
    hidden_sum.middle()
    reduce.pump(1)
    product_nt(activated[...], 3, 0, width, 1)
    mlp_sum = sum_of(3, 1)
    mlp_sum.start()
    reduce.pump(1)

    def norm_back(grad_out, normed, inverse):
        first_mean = jnp.mean(grad_out, axis=-1, keepdims=True)
        second_mean = jnp.mean(grad_out * normed, axis=-1, keepdims=True)
        return inverse * (grad_out - first_mean - normed * second_mean)

    def row_sum(values):
        return jnp.sum(values, axis=0, keepdims=True)

    cot_mine = cot[mine, :].astype(FULL)
    d_hidden = hidden_sum.end()
    normed = own[3]
    small[3:4, :] = row_sum(d_hidden)
    small[4:5, :] = row_sum(d_hidden * normed)
    grad_three = live_mine * cot_mine + norm_back(
        d_hidden * (1.0 + modul_mine(4)), normed, inverses[1, :, 0:1]
    )
    own[3] = grad_three
    small[7:8, :] = row_sum(grad_three)
    shared[2, mine, :] = grad_three.astype(LOW)
    share = Share(place, shared.at[2], share_sems.at[2])
    share.start()
    mlp_sum.middle()
    reduce.pump(1)
    share.middle()
    reduce.pump(1)
    mlp_out = mlp_sum.end() + side[2:3, :]
    grad_four = live_mine * cot_mine
    small[5:6, :] = row_sum(grad_four * mlp_out)
    small[8:9, :] = row_sum(modul_mine(5) * grad_four)
    final[mine, :] = (live_mine * (own[0] + modul_mine(5) * mlp_out)).astype(LOW)
    share.end()
    out_share = Share(place, final, share_sems.at[3])
    out_share.start()

    def attend_back(query, keys, values, probs, d_mixed):
        stacked_grad = stacked(d_mixed)
        stacked_query = stacked(query)
        d_probs = dot(stacked_grad, values, 1, 1)
        d_values = dot(probs.astype(LOW), stacked_grad, 0, 0).astype(LOW)
        d_scores = (probs * (d_probs - jnp.sum(probs * d_probs, axis=-1, keepdims=True))).astype(LOW)
        d_query = (unstacked(dot(d_scores, keys, 1, 0), clip_rows) * scale).astype(LOW)
        d_keys = (dot(d_scores, stacked_query, 0, 0) * scale).astype(LOW)
        return d_query, d_keys, d_values

    def spread_out(pieces, offset, total):
        have = sum(piece.shape[1] for piece in pieces)
        height = pieces[0].shape[0]
        ends = [(offset, pieces[:0]), (total - offset - have, None)]
        full = list(pieces)
        if ends[0][0]:
            full.insert(0, jnp.zeros((height, offset), LOW))
        if ends[1][0]:
            full.append(jnp.zeros((height, ends[1][0]), LOW))
        return jnp.concatenate(full, axis=1)

    d_mixed = dot(shared[2], weights[1, :, out_cols:width], 1, 0)[:, out_pad:].astype(LOW)
    reduce.pump(1)
    for clip in range(clips):
        block = pl.ds(clip * clip_rows, clip_rows)
        words = pl.ds(clip * tlen, tlen)
        d_query, d_keys, d_values = attend_back(
            heads_two[block, :],
            text_heads[0, words, :],
            text_heads[1, words, :],
            probs_two[clip],
            d_mixed[clip * clip_rows : (clip + 1) * clip_rows],
        )
        d_heads[block, 0:query_cols] = spread_out([d_query], 0, query_cols)
        d_text[words, :] = spread_out([d_keys, d_values], text_pad, 5 * 128)
        reduce.pump(1)
    product_nt(d_heads[:, 0:query_cols], 1, 0, query_cols, 0)
    query_sum = sum_of(4, 0)
    query_sum.start()
    reduce.pump(1)
    out_share.middle()
    query_sum.middle()
    reduce.pump(1)
    gather.drain(1)
    query_part = dot(shared[0], d_heads[:, 0:query_cols], 0, 0)
    text_part = dot(text[...], d_text[...], 0, 0)
    out_part = dot(shared[2], mixed_two[...], 0, 0)
    parts[1][:, 0:text_cols] = query_part[:, 0:text_cols].astype(LOW)
    parts[1][:, text_cols:query_cols] = (
        query_part[:, text_cols:query_cols] + text_part[:, 0 : query_cols - text_cols]
    ).astype(LOW)
    parts[1][:, query_cols:out_cols] = text_part[:, query_cols - text_cols : out_cols - text_cols].astype(LOW)
    parts[1][:, out_cols:self_cols] = (
        text_part[:, out_cols - text_cols : self_cols - text_cols] + out_part[:, 0 : self_cols - out_cols]
    ).astype(LOW)
    parts[1][:, self_cols:width] = out_part[:, self_cols - out_cols :].astype(LOW)
    reduce.add_panel(1)
    reduce.pump(2)
    grad_two = own[3] + query_sum.end()
    own[3] = grad_two
    small[2:3, :] = row_sum(grad_two * own[2])
    d_attended = modul_mine(2) * grad_two
    small[6:7, :] = row_sum(d_attended)
    shared[3, mine, :] = d_attended.astype(LOW)
    share = Share(place, shared.at[3], share_sems.at[4])
    share.start()
    out_share.end()
    reduce.pump(1)
    share.middle()
    reduce.pump(1)
    share.end()

    d_mixed = dot(shared[3], weights[0, :, out_cols:width], 1, 0)[:, out_pad:].astype(LOW)
    for clip in range(clips):
        block = pl.ds(clip * clip_rows, clip_rows)
        grads = attend_back(
            heads_one[0, block, :],
            heads_one[1, block, :],
            heads_one[2, block, :],
            probs_one[clip],
            d_mixed[clip * clip_rows : (clip + 1) * clip_rows],
        )
        d_heads[block, :] = spread_out(list(grads), 0, self_cols)
        reduce.pump(1)
    product_nt(d_heads[...], 0, 0, self_cols, 1)
    first_sum = sum_of(5, 1)
    first_sum.start()
    reduce.pump(1)
    first_sum.middle()
    gather.drain(0)
    for at in range(0, width, TILE):
        row_part = dot(hidden_one[:, at : at + TILE], d_heads[...], 0, 0)
        out_part = dot(shared[3, :, at : at + TILE], mixed_one[...], 0, 0)
        block = slice(at, at + TILE)
        parts[0][block, 0:out_cols] = row_part[:, 0:out_cols].astype(LOW)
        parts[0][block, out_cols:self_cols] = (
            row_part[:, out_cols:self_cols] + out_part[:, 0 : self_cols - out_cols]
        ).astype(LOW)
        parts[0][block, self_cols:width] = out_part[:, self_cols - out_cols :].astype(LOW)
    reduce.add_panel(0)
    reduce.pump(2)
    d_hidden = first_sum.end()
    normed = own[1]
    small[0:1, :] = row_sum(d_hidden)
    small[1:2, :] = row_sum(d_hidden * normed)
    grad_one = own[3] + norm_back(d_hidden * (1.0 + modul_mine(1)), normed, inverses[0, :, 0:1])
    latent_grad[mine, :] = jnp.sqrt(abar_mine) * grad_one
    small_all[me] = small[...]
    small_copies = send_all(lambda peer: small, small_all.at[me], small_sems, "tensor")
    share = Share(place, latent_grad, share_sems.at[5])
    share.start()
    up_row[...] = small[9:10, :]
    up_all[dp] = up_row[...]
    up_copies = send_all(lambda peer: up_row, up_all.at[dp], up_sems, "dp")
    reduce.pump(1)

    wait_all(small_copies)
    totals[...] = jnp.zeros_like(totals)
    for clip in range(clips):
        value = small_all[clip * per_clip, 0:6, :]
        for k in range(1, per_clip):
            value = value + small_all[clip * per_clip + k, 0:6, :]
        totals[6 * clip : 6 * clip + 6, 0:width] = value
    value = small_all[0, 6:9, :]
    for k in range(1, n_tensor):
        value = value + small_all[k, 6:9, :]
    totals[6 * clips : 6 * clips + 3, 0:width] = value
    piece = totals.shape[1] // n_tensor
    my_columns = pl.ds(pl.multiple_of(me * piece, 128), piece)
    totals_all[dp, :, my_columns] = totals[:, my_columns]
    total_copies = send_all(
        lambda peer: totals.at[:, my_columns], totals_all.at[dp, :, my_columns], total_sems, "dp"
    )
    reduce.pump(1)
    share.middle()
    reduce.pump(1)
    wait_all(total_copies)
    my_totals = totals_all.at[:, :, my_columns]
    total_copies = send_all(lambda peer: my_totals, my_totals, total_share_sems, "tensor")
    reduce.pump(1)
    share.end()
    wait_all(up_copies)
    reduce.pump(1)
    wait_all(total_copies)
    sides = totals_all[0, :, 0:width]
    ups = up_all[0]
    for peer in range(1, n_data):
        sides = sides + totals_all[peer, :, 0:width]
        ups = ups + up_all[peer]
    grad_side[0:3, :] = sides[6 * clips : 6 * clips + 3]
    value = sides[0:6]
    for clip in range(1, clips):
        value = value + sides[6 * clip : 6 * clip + 6]
    grad_side[3:9, :] = value
    grad_up[...] = ups.reshape(width)
    reduce.pump(1)
    total_rows = n_data * totals.shape[0]
    flat = totals_all[:, :, 0:width].reshape(total_rows, width)
    for k in range(3):
        piece = flat.astype(LOW)
        splits[pl.ds(k * total_rows, total_rows), :] = piece
        flat = flat - piece.astype(FULL)
    feat_index = lax.broadcasted_iota(jnp.int32, (total_rows, n_data * feat_rows), 1)
    total_index = lax.broadcasted_iota(jnp.int32, (total_rows, n_data * feat_rows), 0)
    feat_clip, total_row = feat_index & (feat_rows - 1), total_index & (totals.shape[0] - 1)
    feat_bits, total_bits = feat_rows.bit_length() - 1, totals.shape[0].bit_length() - 1
    same_data = ((feat_index >> feat_bits) == (total_index >> total_bits)) & (feat_clip < clips)
    lesser = jnp.zeros((1, width), FULL)
    for j in range(6):
        spot = (same_data & (total_row == 6 * feat_clip + j)).astype(FULL).astype(LOW)
        lifted = dot(spot, feats_mine, 1, 0).astype(LOW)
        value = dot(jnp.concatenate([lifted] * 3, axis=0), splits[...], 0, 0)
        grad_time[j] = value
        lesser = lesser + row_sum(value * value)
        if j % 2 == 1:
            reduce.pump(1)
    lesser = lesser * (1.0 / n_tensor)
    lesser = lesser + ups * ups * (1.0 / n_data)
    value = grad_side[...]
    lesser = lesser + row_sum(value * value) * (1.0 / (n_data * n_tensor))
    reduce.complete()
    mine_sum = jnp.broadcast_to(jnp.sum(lesser + squares[...], axis=1, keepdims=True), (8, 128))
    norms[0] = mine_sum
    norms_all[0, dp] = mine_sum
    norm_copies = send_all(lambda peer: norms.at[0], norms_all.at[0, dp], norm_sems, "dp")
    gather.drain(3)
    for moment in moments:
        moment.wait()
    wait_all(norm_copies)
    value = norms_all[0, 0]
    for peer in range(1, n_data):
        value = value + norms_all[0, peer]
    norms[1] = value
    norms_all[1, me] = value
    norm_copies = send_all(lambda peer: norms.at[1], norms_all.at[1, me], norm_share_sems, "tensor")
    wait_all(norm_copies)
    value = norms_all[1, 0]
    for peer in range(1, n_tensor):
        value = value + norms_all[1, peer]
    square_sum[...] = value


def fits(n_data, n_tensor, rows, clips, panel_rows, units):
    clip_rows = rows // clips
    return (
        n_tensor == 4
        and clips == 2
        and n_data % 2 == 0
        and n_data <= 8
        and panel_rows % 16 == 0
        and clip_rows == 128
        and units == D
    )


def run_block(tsteps, clip_count, text_len, latent, noise, cot, text, attn, mlp, time, up_bias, side_vec):
    attn_w, mlp_w, time_w = attn[0], mlp[0], time[0]
    n_data, n_tensor = lax.axis_size("dp"), lax.axis_size("tensor")
    clips = text_len.shape[0]
    tlen = text.shape[0] // clips
    rows, width = latent.shape
    own_rows = rows // n_tensor
    local = width // n_tensor
    heads = HEADS // n_tensor
    clip_rows = rows // clips
    panel_rows, units = mlp_w.shape[1:]
    wide = -(-local // 128) * 128
    self_cols = -(-3 * local // 128) * 128
    steps = n_data - 1
    lead = -(-panel_rows // 32) * 16
    feat_rows = 16
    split = -(-width // (128 * n_tensor)) * 128 * n_tensor
    dma = pltpu.SemaphoreType.DMA
    scratch = [
        pltpu.VMEM((rows, width), LOW),
        pltpu.VMEM((rows, width), LOW),
        pltpu.VMEM((rows, width), LOW),
        pltpu.VMEM(text.shape, LOW),
        pltpu.VMEM((4, width, units), LOW),
        pltpu.VMEM((width, units), LOW),
        pltpu.VMEM((2, 2, steps, lead, units), LOW),
        pltpu.VMEM((feat_rows, TFREQ), LOW),
        pltpu.VMEM((n_data, feat_rows, TFREQ), LOW),
        pltpu.VMEM((n_data, 4, width), FULL),
        pltpu.VMEM((n_data, 4, width), FULL),
        pltpu.VMEM((n_tensor, 4, width), FULL),
        pltpu.VMEM((rows, width), LOW),
        pltpu.VMEM((3, rows, local), LOW),
        pltpu.VMEM((clips, heads * clip_rows, clip_rows), FULL),
        pltpu.VMEM((rows, wide), LOW),
        pltpu.VMEM((rows, local), LOW),
        pltpu.VMEM((2, clips * tlen, local), LOW),
        pltpu.VMEM((clips, heads * clip_rows, tlen), FULL),
        pltpu.VMEM((rows, wide), LOW),
        pltpu.VMEM((4, rows, width), LOW),
        pltpu.VMEM((rows, units), LOW),
        pltpu.VMEM((rows, units), FULL),
        pltpu.VMEM((rows, units), LOW),
        pltpu.VMEM((rows, self_cols), LOW),
        pltpu.VMEM((clips * tlen, 5 * 128), LOW),
        pltpu.VMEM((2, rows, width), FULL),
        pltpu.VMEM((3, 2, own_rows, width), FULL),
        pltpu.VMEM((3, own_rows, width), LOW),
        pltpu.VMEM((3, own_rows, width), LOW),
        pltpu.VMEM((4, own_rows, width), FULL),
        pltpu.VMEM((2, own_rows, 128), FULL),
        pltpu.VMEM((16, width), FULL),
        pltpu.VMEM((n_tensor, 16, width), FULL),
        pltpu.VMEM((16, split), FULL),
        pltpu.VMEM((n_data, 16, split), FULL),
        pltpu.VMEM((1, width), FULL),
        pltpu.VMEM((n_data, 1, width), FULL),
        pltpu.VMEM((2, 8, 128), FULL),
        pltpu.VMEM((2, max(n_data, n_tensor), 8, 128), FULL),
        pltpu.VMEM((3 * n_data * 16, width), LOW),
        pltpu.VMEM((1, width), FULL),
        dma((7,)),
        dma((6,)),
        pltpu.SemaphoreType.REGULAR((2,)),
        dma((2, 4, steps)),
        dma((2, 4, steps)),
        dma((2, 4, steps)),
        dma((2, 4, steps)),
        dma((6, 6)),
        dma((6, 6)),
        dma((2, steps)),
        dma((2, steps)),
        dma((2, n_tensor - 1)),
        dma((2, n_tensor - 1)),
        dma((2, steps)),
        dma((2, steps)),
        dma((2, n_tensor - 1)),
        dma((2, steps)),
        dma((2, n_tensor - 1)),
    ]
    vmem = pl.BlockSpec(memory_space=pltpu.VMEM)
    smem = pl.BlockSpec(memory_space=pltpu.SMEM)
    far = pl.BlockSpec(memory_space=pl.ANY)
    results = [pltpu.VMEM(array.shape, FULL) for array in (attn_w, mlp_w, time_w) for _ in range(4)]
    results += [
        pltpu.VMEM((rows, width), LOW),
        pltpu.VMEM((rows, width), FULL),
        pltpu.VMEM(up_bias.shape, FULL),
        pltpu.VMEM(side_vec.shape, FULL),
        pltpu.VMEM((8, 128), FULL),
    ]
    return pl.pallas_call(
        functools.partial(block_kernel, n_data, n_tensor, clips),
        out_shape=results,
        in_specs=[smem] * 3 + [far] * 13 + [vmem] * 2,
        out_specs=[vmem] * len(results),
        scratch_shapes=scratch,
        compiler_params=pltpu.CompilerParams(
            collective_id=0, has_side_effects=True, vmem_limit_bytes=42 * 2**20
        ),
    )(tsteps, clip_count, text_len, latent, noise, cot, text, *attn, *mlp, *time, up_bias, side_vec)


def update_kernel(rates, *refs):
    count = len(rates)
    squares, refs = refs[0], refs[1:]
    ins, passed, refs = refs[: 4 * count], refs[4 * count : 4 * count + 2], refs[4 * count + 2 :]
    outs, passed_out, norm_out, refs = refs[: 3 * count], refs[3 * count : 3 * count + 2], refs[3 * count + 2], refs[3 * count + 3 :]
    held, sems, passed_sems = refs[: 3 * count], refs[3 * count], refs[3 * count + 1]
    copies = []
    for at in range(2):
        copies.append(pltpu.make_async_copy(passed[at], passed_out[at], passed_sems.at[at]))
        copies[-1].start()
    norm = jnp.sqrt(squares[0:1, 0:1])
    norm_out[...] = norm
    factor = jnp.minimum(1.0, CLIP_NORM / (norm + 1e-06))
    sent = 0
    for at, rate in enumerate(rates):
        weight, first, second, grad = ins[4 * at : 4 * at + 4]
        spots = [(k,) for k in range(weight.shape[0])] if len(weight.shape) == 3 else [(Ellipsis,)]
        clip = factor if len(weight.shape) > 1 else factor[0, 0]
        for spot in spots:
            values = adamw_short(weight[spot], first[spot], second[spot], grad[spot], clip, rate)
            for buffer, target, value in zip(held[3 * at : 3 * at + 3], outs[3 * at : 3 * at + 3], values):
                buffer[spot] = value
                source, target = (buffer, target) if spot[0] is Ellipsis else (buffer.at[spot], target.at[spot])
                copies.append(pltpu.make_async_copy(source, target, sems.at[sent]))
                copies[-1].start()
                sent += 1
    for copy in copies:
        copy.wait()


def adamw_short(weight, first, second, grad, factor, rate):
    clipped = grad * factor
    first = BETA_ONE * first + (1.0 - BETA_ONE) * clipped
    second = BETA_TWO * second + (1.0 - BETA_TWO) * clipped * clipped
    root = jnp.sqrt(second * (1.0 / (1.0 - BETA_TWO**OPT_STEP)))
    step = (rate / (1.0 - BETA_ONE**OPT_STEP)) * first / (root + EPSILON)
    return ((1.0 - rate * DECAY_RATE) * weight - step, first, second)


def run_update(squares, weights, passed):
    operands, held, shapes, sends = [squares], [], [], 0
    for array, *others, _ in weights:
        operands += [array, *others]
        held += [pltpu.VMEM(array.shape, FULL)] * 3
        shapes += [jax.ShapeDtypeStruct(array.shape, FULL)] * 3
        sends += 3 * (array.shape[0] if array.ndim == 3 else 1)
    operands += passed
    shapes += [jax.ShapeDtypeStruct(array.shape, array.dtype) for array in passed]
    shapes.append(jax.ShapeDtypeStruct((1, 1), FULL))
    vmem = pl.BlockSpec(memory_space=pltpu.VMEM)
    far = pl.BlockSpec(memory_space=pl.ANY)
    return pl.pallas_call(
        functools.partial(update_kernel, [rate for *_, rate in weights]),
        out_shape=shapes,
        in_specs=[vmem] * len(operands),
        out_specs=[far] * (len(shapes) - 1) + [vmem],
        scratch_shapes=held + [pltpu.SemaphoreType.DMA((sends,)), pltpu.SemaphoreType.DMA((2,))],
        compiler_params=pltpu.CompilerParams(vmem_limit_bytes=18 * 2**20),
    )(*operands)


def shards(
    latent,
    noise,
    text,
    tsteps,
    clip_count,
    text_len,
    cotangent,
    attn_w,
    attn_m,
    attn_v,
    mlp_w,
    mlp_m,
    mlp_v,
    up_bias,
    up_m,
    up_v,
    side_vec,
    side_m,
    side_v,
    time_w,
    time_m,
    time_v,
):
    n_tensor = lax.axis_size("tensor")
    n_data = lax.axis_size("dp")
    clips, tlen, width = text.shape
    rows = latent.shape[0]
    panel_rows, local = attn_w.shape[1:]
    if not fits(n_data, n_tensor, rows, clips, panel_rows, mlp_w.shape[2]):
        return plain_shards(
            latent, noise, text, tsteps, clip_count, text_len, cotangent, attn_w, attn_m, attn_v, mlp_w, mlp_m,
            mlp_v, up_bias, up_m, up_v, side_vec, side_m, side_v, time_w, time_m, time_v,
        )
    *held, block_out, latent_grad, grad_up, grad_side, squares = run_block(
        tsteps,
        clip_count,
        text_len,
        latent,
        noise,
        cotangent,
        text.reshape(clips * tlen, width),
        (attn_w, attn_m, attn_v),
        (mlp_w, mlp_m, mlp_v),
        (time_w, time_m, time_v),
        up_bias,
        side_vec,
    )
    (
        attn_new,
        attn_m_new,
        attn_v_new,
        mlp_new,
        mlp_m_new,
        mlp_v_new,
        time_new,
        time_m_new,
        time_v_new,
        up_new,
        up_m_new,
        up_v_new,
        side_new,
        side_m_new,
        side_v_new,
        block_out,
        latent_grad,
        grad_norm,
    ) = run_update(
        squares,
        [
            (*held[0:4], RATE_MATRIX),
            (*held[4:8], RATE_MATRIX),
            (*held[8:12], RATE_TIME),
            (up_bias, up_m, up_v, grad_up, RATE_VECTOR),
            (side_vec, side_m, side_v, grad_side, RATE_VECTOR),
        ],
        [block_out, latent_grad],
    )
    return (
        block_out,
        latent_grad,
        grad_norm[0, 0],
        attn_new,
        attn_m_new,
        attn_v_new,
        mlp_new,
        mlp_m_new,
        mlp_v_new,
        up_new,
        up_m_new,
        up_v_new,
        side_new,
        side_m_new,
        side_v_new,
        time_new,
        time_m_new,
        time_v_new,
    )


def solution(mesh):
    placed = (
        P("dp", None),
        P("dp", None),
        P("dp", None, None),
        P("dp"),
        P("dp"),
        P("dp"),
        P("dp", None),
        P(None, "dp", "tensor"),
        P(None, "dp", "tensor"),
        P(None, "dp", "tensor"),
        P(None, "dp", "tensor"),
        P(None, "dp", "tensor"),
        P(None, "dp", "tensor"),
        P("tensor"),
        P("tensor"),
        P("tensor"),
        P(),
        P(),
        P(),
        P(None, "dp", None),
        P(None, "dp", None),
        P(None, "dp", None),
    )
    return jax.shard_map(
        shards,
        mesh=mesh,
        in_specs=placed,
        out_specs=(
            P("dp", None),
            P("dp", None),
            P(),
            P(None, "dp", "tensor"),
            P(None, "dp", "tensor"),
            P(None, "dp", "tensor"),
            P(None, "dp", "tensor"),
            P(None, "dp", "tensor"),
            P(None, "dp", "tensor"),
            P("tensor"),
            P("tensor"),
            P("tensor"),
            P(),
            P(),
            P(),
            P(None, "dp", None),
            P(None, "dp", None),
            P(None, "dp", None),
        ),
        check_vma=False,
    )
```
